32 devices in a mesh: rep: 4 (over y, core), shard: 4 (over z), tp: 2 (over x).
Axes of the slice: x: 2, y: 2, z: 4, core: 2. Of those that a mesh axis runs over, the one named last changes fastest.
Arguments:
- hidden_in: bfloat16 [8192, 8192], P(('rep', 'shard', 'tp')), may hold values from -6 to 6
- lengths: int32 [16], P(('rep', 'shard')), may hold values from 128 to 512, as said below
- kv_grad_out: bfloat16 [8192, 2, 1024], P(('rep', 'shard'), None, 'tp'), may hold values from -384 to 384
- master: float32 [8192, 2, 1024], P('shard', None, 'tp'), may hold values from -0.0625 to 0.0625
- moment_one: float32 [8192, 2, 1024], P('shard', None, 'tp'), may hold values from -3 to 3
- moment_two: float32 [8192, 2, 1024], P('shard', None, 'tp'), may hold values from 0.05 to 2
Outputs:
- new_master: float32 [8192, 2, 1024], P('shard', None, 'tp')
- new_moment_one: float32 [8192, 2, 1024], P('shard', None, 'tp')
- new_moment_two: float32 [8192, 2, 1024], P('shard', None, 'tp')
- fresh_kv: bfloat16 [8192, 2, 1024], P(('rep', 'shard'), None, 'tp')
The draws below stay inside these ranges and needn't reach their ends.
Inputs may be any that keep to these rules, and one draw needn't show every extreme that they name: In block b only its first lengths[b] tokens are valid.
All inputs are finite; a program needn't handle non-finite values.
Results may differ from the reference program's by a relative error of at most 0.014.
Values may be sent and summed in bfloat16 or wider, within the bound.
No kernel may reach another device: no remote copies, remote signals or barrier semaphores. Data moves between devices by JAX's collectives and lax.ppermute only.
A program may use at most 192 MiB of HBM per device.

```python
import math
import jax
import jax.numpy as jnp
from jax import lax

D = 8192
KV = 1024
TOK_DEV = 512
BLOCKS = 16
TOKENS = 8192


def draw_lengths(key, part):
    key = jax.random.fold_in(key, 7)
    index = jnp.arange(BLOCKS, dtype=jnp.int32)
    base = TOK_DEV // 4 + 3 * TOK_DEV // 4 * index // max(BLOCKS - 1, 1)
    jitter = jax.random.randint(key, (BLOCKS,), 0, TOK_DEV // 8 + 1, dtype=jnp.int32)
    jitter = jnp.where(index == 0, 0, jitter)
    return jnp.minimum(base + jitter, TOK_DEV).astype(jnp.int32)


def steps_of(key, extent, shards, smallest, high):
    def one(dim, parts):
        draws = jax.random.uniform(jax.random.fold_in(jax.random.fold_in(key, 6), dim), (parts,), jnp.float32, smallest / len(shards), high / len(shards))
        return jnp.repeat(jnp.exp(draws), extent[dim] // parts).reshape((-1,) + (1,) * (len(extent) - dim - 1))

    loudness = one(*shards[0])
    for cut in shards[1:]:
        loudness = loudness * one(*cut)
    return loudness


def noise(rng, dims, width, limit, split=(), held_as=jnp.bfloat16):
    array = width * jax.random.normal(rng, dims, jnp.float32)
    if split:
        array = array * steps_of(rng, dims, split, -0.22, 0.18)
    return jnp.clip(array, -limit, limit).astype(held_as)


def setup_inputs(seed: int = 0) -> dict:
    splits = jax.random.split(jax.random.key(seed), 7)
    hidden_in = noise(splits[0], (TOKENS, D), 1.0, 6.0, ((0, 32),))
    lengths = draw_lengths(jax.random.fold_in(splits[6], 71), 0)
    kv_grad_out = noise(splits[2], (TOKENS, 2, KV), 64.0, 384.0, ((0, 16), (2, 2)))
    master = noise(splits[3], (D, 2, KV), D ** -0.5, 0.0625, ((0, 4), (2, 2)), jnp.float32)
    moment_one = noise(splits[4], (D, 2, KV), 0.5, 3.0, ((0, 4), (2, 2)), jnp.float32)
    moment_two = jnp.clip(jnp.exp(math.log(2.0) - 3.6888794 * jax.random.uniform(splits[5], (D, 2, KV), jnp.float32) ** steps_of(splits[5], (D, 2, KV), ((0, 4), (2, 2)), -0.2, 0.2)), 0.05, 2.0)
    return dict(hidden_in=hidden_in, lengths=lengths, kv_grad_out=kv_grad_out, master=master, moment_one=moment_one, moment_two=moment_two)


beta_one = 0.9
beta_two = 0.95
step_count = 20
rate = 0.002
decay = 0.1
epsilon = 1e-08

def adamw(master, moment_one, moment_two, grad):
    first = beta_one * moment_one + (1.0 - beta_one) * grad
    second = beta_two * moment_two + (1.0 - beta_two) * grad * grad
    first_hat = first / (1.0 - beta_one ** step_count)
    second_hat = second / (1.0 - beta_two ** step_count)
    updated = master - rate * (first_hat / (jnp.sqrt(second_hat) + epsilon) + decay * master)
    return (updated, first, second)

def reference(hidden_in, lengths, kv_grad_out, master, moment_one, moment_two):
    count = jnp.sum(lengths.astype(jnp.float32))
    flat_cot = kv_grad_out.reshape(TOKENS, 2 * KV)

    def accumulate(total, block):
        start = block * TOK_DEV
        inputs = lax.dynamic_slice_in_dim(hidden_in, start, TOK_DEV, 0)
        cotan = lax.dynamic_slice_in_dim(flat_cot, start, TOK_DEV, 0)
        validity = (jnp.arange(TOK_DEV, dtype=jnp.int32) < lengths[block]).astype(cotan.dtype)
        cotan = cotan * validity[:, None]
        term = lax.dot_general(inputs, cotan, (((0,), (0,)), ((), ())), preferred_element_type=jnp.float32)
        rounded = lax.optimization_barrier(term.astype(jnp.bfloat16))
        return (total + rounded.astype(jnp.float32), None)
    summed, _ = lax.scan(accumulate, jnp.zeros((D, 2 * KV), jnp.float32), jnp.arange(BLOCKS, dtype=jnp.int32))
    grad = summed.reshape(D, 2, KV) / count
    new_master, new_first, new_second = adamw(master, moment_one, moment_two, grad)
    weights = new_master.astype(jnp.bfloat16).reshape(D, 2 * KV)

    def project(block):
        inputs = lax.dynamic_slice_in_dim(hidden_in, block * TOK_DEV, TOK_DEV, 0)
        return jnp.dot(inputs, weights, preferred_element_type=jnp.float32).astype(jnp.bfloat16)
    fresh = lax.map(project, jnp.arange(BLOCKS, dtype=jnp.int32))
    return (new_master, new_first, new_second, fresh.reshape(TOKENS, 2, KV))
```

```python
import functools

import jax
import jax.numpy as jnp
from jax import lax
from jax.experimental import pallas as pl
from jax.experimental.pallas import tpu as pltpu
from jax.sharding import PartitionSpec as P

beta_one = 0.9
beta_two = 0.95
step_count = 20
rate = 0.002
decay = 0.1
epsilon = 1e-08

LANES = 128
GROUPS = 4
VMEM_BYTES = 56 * 1024 * 1024

SMEM = pl.BlockSpec(memory_space=pltpu.SMEM)


def adamw(master, moment_one, moment_two, grad):
    first = beta_one * moment_one + (1.0 - beta_one) * grad
    second = beta_two * moment_two + (1.0 - beta_two) * grad * grad
    first_hat = first / (1.0 - beta_one**step_count)
    second_hat = second / (1.0 - beta_two**step_count)
    updated = master - rate * (first_hat / (jnp.sqrt(second_hat) + epsilon) + decay * master)
    return (updated, first, second)


def lane_rows(array):
    rows, two, features = array.shape
    split = array.reshape(rows, two, features // LANES, LANES)
    return split.transpose(0, 2, 1, 3).reshape(rows * two * features // LANES, LANES)


def from_lane_rows(array, rows, features):
    split = array.reshape(rows, features // LANES, 2, LANES)
    return split.transpose(0, 2, 1, 3).reshape(rows, 2, features)


def slots(features):
    return [half * features + tile * LANES for tile in range(features // LANES) for half in range(2)]


def call(kernel, out_shape, flops, moved, **kwargs):
    return pl.pallas_call(
        kernel,
        out_shape=out_shape,
        cost_estimate=pl.CostEstimate(flops=flops, bytes_accessed=moved, transcendentals=0),
        compiler_params=pltpu.CompilerParams(vmem_limit_bytes=VMEM_BYTES),
        **kwargs,
    )


def full(shape):
    return pl.BlockSpec(shape, lambda *_: (0,) * len(shape))


def f32(ref):
    return ref[...].astype(jnp.float32)


def pack(hidden, rep, groups, replicas, rows):
    tokens = hidden.shape[0]
    specs, shapes, orders = [], [], []
    for start, part, order in groups:
        for k in range(replicas):
            for s in range(len(order)):

                def index(i, place, at=1 + len(orders) + s, k=k, start=start, part=part):
                    return (0, (place[at] * replicas + (place[0] ^ k)) * (rows // part) + start // part)

                specs.append(pl.BlockSpec((tokens, part), index))
            shapes.append((tokens, len(order) * part))
        orders += order

    def kernel(place, *refs):
        sources, outs = iter(refs[: len(specs)]), iter(refs[len(specs) :])
        for start, part, order in groups:
            for k in range(replicas):
                out = next(outs)
                for s in range(len(order)):
                    out[:, s * part : (s + 1) * part] = next(sources)[...]

    outs = call(
        kernel,
        [jax.ShapeDtypeStruct(shape, hidden.dtype) for shape in shapes],
        0,
        4 * sum(shape[0] * shape[1] for shape in shapes),
        grid_spec=pltpu.PrefetchScalarGridSpec(
            num_scalar_prefetch=1,
            grid=(1,),
            in_specs=specs,
            out_specs=[full(shape) for shape in shapes],
        ),
    )(jnp.stack([rep, *orders]), *[hidden] * len(specs))
    return [outs[i : i + replicas] for i in range(0, len(outs), replicas)]


def mask(cotan, place, pairs):
    block, _, features = cotan.shape
    width, tokens = 2 * features, block // pairs
    per = width // LANES

    def kernel(place, source, out, count, scratch):
        scratch[...] = source[...].astype(jnp.float32)
        count[...] = jnp.full(count.shape, place[0]).astype(jnp.float32)
        for o in range(pairs):
            start = (place[1] ^ o) * tokens
            row = lax.broadcasted_iota(jnp.int32, (tokens, LANES), 0) + start
            for slot, column in enumerate(slots(features)):
                rows = scratch[pl.ds(start * per + slot, tokens, stride=per), :]
                out[o * tokens : (o + 1) * tokens, column : column + LANES] = jnp.where(
                    row < place[0], rows, 0.0
                ).astype(out.dtype)

    return call(
        kernel,
        [jax.ShapeDtypeStruct((block, width), cotan.dtype), jax.ShapeDtypeStruct((8, LANES), jnp.float32)],
        0,
        4 * block * width,
        grid=(1,),
        in_specs=[SMEM, full((block * per, LANES))],
        out_specs=[full((block, width)), full((8, LANES))],
        scratch_shapes=[pltpu.VMEM((block * per, LANES), jnp.float32)],
    )(place, lane_rows(cotan))


def fresh_weights(place, count, shares, params):
    part, width = shares[0][1].block_shape
    per = width // LANES

    def kernel(place, count, *refs):
        sources = refs[: len(shares)]
        master, first, second, weights, grad, scratch = refs[len(shares) :]
        grad[...] = sum(f32(source) for source in sources).astype(grad.dtype)
        scale = 1.0 / count[0:1, 0:1]
        starts = slots(width // 2)
        for slot, start in enumerate(starts):
            scratch[pl.ds(slot, part, stride=per), :] = grad[:, start : start + LANES].astype(jnp.float32)
        updated, _, _ = adamw(master[...], first[...], second[...], scratch[...] * scale)
        scratch[...] = updated
        for slot, start in enumerate(starts):
            weights[:, start : start + LANES] = scratch[pl.ds(slot, part, stride=per), :].astype(weights.dtype)

    param_spec = pl.BlockSpec((part * per, LANES), lambda i, place: (place[0], 0))
    return call(
        kernel,
        [jax.ShapeDtypeStruct((part, width), jnp.bfloat16)] * 2,
        20 * part * width,
        20 * part * width,
        grid_spec=pltpu.PrefetchScalarGridSpec(
            num_scalar_prefetch=1,
            grid=(1,),
            in_specs=[full((8, LANES)), *[spec for _, spec in shares], param_spec, param_spec, param_spec],
            out_specs=[pl.BlockSpec((part, width), lambda i, place: (0, 0))] * 2,
            scratch_shapes=[pltpu.VMEM((part * per, LANES), jnp.float32)],
        ),
    )(place, count, *[a for a, _ in shares], *params)


def update_kernel(place, count, grad, master, first, second, new_master, new_first, new_second, scratch):
    rows, width = grad.shape
    per = width // LANES
    scale = 1.0 / count[0:1, 0:1]
    for slot, start in enumerate(slots(width // 2)):
        scratch[pl.ds(slot, rows, stride=per), :] = grad[:, start : start + LANES].astype(jnp.float32)
    updated, one, two = adamw(master[...], first[...], second[...], scratch[...] * scale)
    new_master[...] = updated
    new_first[...] = one
    new_second[...] = two


def update(me, count, grads, params, block):
    replicas, rows, width = grads.shape
    per = width // LANES
    steps = rows // block
    param_spec = pl.BlockSpec((block * per, LANES), lambda k, i, me: ((me[0] ^ k) * steps + i, 0))
    return call(
        update_kernel,
        [jax.ShapeDtypeStruct(params[0].shape, jnp.float32)] * 3,
        20 * replicas * rows * width,
        26 * replicas * rows * width,
        grid_spec=pltpu.PrefetchScalarGridSpec(
            num_scalar_prefetch=1,
            grid=(replicas, steps),
            in_specs=[
                full((8, LANES)),
                pl.BlockSpec((None, block, width), lambda k, i, me: (k, i, 0)),
                param_spec,
                param_spec,
                param_spec,
            ],
            out_specs=[param_spec] * 3,
            scratch_shapes=[pltpu.VMEM((block * per, LANES), jnp.float32)],
        ),
    )(me, count, grads, *params)


def combine(shares, pair, pairs):
    rows, width = shares[0][1].block_shape
    features, tokens = width // 2, rows // pairs
    per = width // LANES

    def kernel(pair, *refs):
        sources, out, scratch = refs[: len(shares)], refs[-2], refs[-1]
        for o in range(pairs):
            start = (pair[0] ^ o) * tokens
            for slot, column in enumerate(slots(features)):
                total = None
                for source in sources:
                    piece = source[o * tokens : (o + 1) * tokens, column : column + LANES].astype(jnp.float32)
                    total = piece if total is None else total + piece
                scratch[pl.ds(start * per + slot, tokens, stride=per), :] = total
        out[...] = scratch[...].astype(out.dtype)

    out = call(
        kernel,
        jax.ShapeDtypeStruct((rows * per, LANES), jnp.bfloat16),
        0,
        8 * rows * width,
        grid=(1,),
        in_specs=[SMEM] + [s for _, s in shares],
        out_specs=full((rows * per, LANES)),
        scratch_shapes=[pltpu.VMEM((rows * per, LANES), jnp.float32)],
    )(pair, *[a for a, _ in shares])
    return from_lane_rows(out, rows, features)


def after(value, *deps):
    return lax.optimization_barrier((value, *deps))[0] if deps else value


def swap(value, axis, k):
    if k == 0:
        return value
    return lax.ppermute(value, axis, [(i, i ^ k) for i in range(lax.axis_size(axis))])


def local(hidden_in, lengths, kv_grad_out, master, moment_one, moment_two):
    replicas, shards, pairs = (lax.axis_size(name) for name in ("rep", "shard", "tp"))
    rep, shard, pair = (lax.axis_index(name).astype(jnp.int32) for name in ("rep", "shard", "tp"))
    tokens, depth = hidden_in.shape
    block, _, features = kv_grad_out.shape
    width = 2 * features
    rows = depth // (shards * replicas)
    near = replicas // 2
    parities = [k for k in range(replicas) if k % 2] + [k for k in range(replicas) if not k % 2]
    odd = replicas // 2 * block

    order, k = [0], shards // 2
    while k:
        order, k = [i + k for i in order] + order, k // 2
    count_of_groups = max(1, min(GROUPS, rows // LANES))
    part = rows // count_of_groups
    groups = [(g * part, part, [shard ^ q for q in order]) for g in range(count_of_groups)]
    last_group = len(groups) - 1
    contract = (((0,), (0,)), ((), ()))

    def terms(here):
        return lax.dot_general(here, cotans, contract, preferred_element_type=jnp.float32).astype(jnp.bfloat16)

    def project(here, weights):
        return jnp.dot(here, weights, preferred_element_type=jnp.float32)

    pieces = pack(hidden_in, rep, groups[:1], replicas, rows)
    cotan, count = mask(kv_grad_out, jnp.stack([lengths[0], pair]), pairs)
    if last_group:
        pieces += pack(hidden_in, rep, groups[1:], replicas, rows)
    arrived, sides, line = [], [], []

    def travel(g, *waits):
        arrived.append(
            [pieces[g][0]]
            + [swap(after(h, *waits) if k >= near else h, "rep", k) for k, h in enumerate(pieces[g]) if k]
        )
        sides.append([])

    def pair_up(g, ks, *waits):
        for k in ks:
            sent = after(arrived[g][k], *line[-2:-1], *waits)
            sides[g].append([arrived[g][k]] + [swap(sent, "tp", o) for o in range(1, pairs)])
            line.append(sides[g][-1][-1])

    def lay(g):
        return jnp.concatenate([p for k in parities for p in sides[g][k]], axis=0)

    low, high = range(near), range(near, replicas)
    travel(0)
    pair_up(0, low)
    pair_up(0, high, cotan, *(pieces[1] if last_group else []))
    cotans = {0: cotan, near: swap(after(cotan, *arrived[0][near:], *line[:near]), "rep", near)}
    count, k = after(count, *arrived[0][near:]), 1
    while k < replicas:
        count, k = count + swap(count, "rep", k), 2 * k
    for g in range(1, len(groups)):
        travel(g, *([cotans[near]] if g == 1 else arrived[g - 1][near:]))
    if last_group:
        pair_up(1, low)
    k = near // 2
    while k:
        for have in list(cotans):
            cotans[have ^ k] = swap(cotans[have], "rep", k)
        k //= 2
    if last_group > 1:
        pair_up(2, low, cotans[near], count)
    cotans = jnp.concatenate([cotans[k] for k in parities], axis=0)
    k = 1
    while k < shards:
        count, k = count + swap(count, "shard", k), 2 * k

    params = [lane_rows(a) for a in (master, moment_one, moment_two)]
    spec = pl.BlockSpec((part, width), lambda i, place: (0, 0))
    inputs, sums, grads, fresh, products, total = [], [], [], [], [], None
    for g in range(len(groups)):
        here = after(lay(g), count)
        if g > 0:
            here = after(here, sums[g - 1][-1])
        if g > 1:
            here = after(here, fresh[g - 2])
        inputs.append(here)
        half = shards // 2 * part
        away = terms(here[:, :half])
        last = terms(after(here, away)[:, half:])
        if 0 < g + 1 <= last_group:
            pair_up(g + 1, high, last)
        if g + 3 <= last_group:
            pair_up(g + 3, low, last)
        shares, k = [last, swap(away, "shard", 1)], 2
        while k < shards:
            half //= 2
            sent = sum(v[:half].astype(jnp.float32) for v in shares).astype(jnp.bfloat16)
            shares, k = [v[half:] for v in shares] + [swap(sent, "shard", k)], 2 * k
        sums.append((shares, sent))
        place = (rep * len(groups) + g)[None]
        weights, grad = fresh_weights(place, count, [(v, spec) for v in shares], params)
        fresh.append(weights)
        grads.append(grad)
        k = shards // 2
        while k > 1:
            weights, k = jnp.concatenate([swap(weights, "shard", k), weights], axis=0), k // 2
        half = weights.shape[0]
        products.append((inputs[g][:, half:], weights))
        products.append((inputs[g][:, :half], swap(weights, "shard", 1)))

    every = {0: jnp.concatenate(grads, axis=0)}
    k = near
    while k:
        for have in list(every):
            every[have ^ k] = swap(every[have], "rep", k)
        k //= 2

    for here, weights in products[:-1]:
        product = project(here, weights)
        total = product if total is None else total + product
    here, weights = products[-1]
    here = after(here, every[near])
    away = project(here[:odd], weights)
    away = (away if total is None else total[:odd] + away).astype(jnp.bfloat16)
    stay = project(after(here, away)[odd:], weights)
    stay = (stay if total is None else total[odd:] + stay).astype(jnp.bfloat16)
    shares = [stay, swap(away, "rep", 1)]
    half, k = odd // 2, 2
    while k < replicas:
        sent = sum(v[half : 2 * half].astype(jnp.float32) for v in shares).astype(jnp.bfloat16)
        shares.append(swap(sent, "rep", k))
        half, k = half // 2, 2 * k
    fresh = combine([(v, full((block, width))) for v in shares], pair[None], pairs)

    every = jnp.stack([every[k] for k in range(replicas)])
    updated = update(rep[None], count, every, params, min(rows, 256))
    updated = [from_lane_rows(a, master.shape[0], features) for a in updated]
    return (*updated, fresh)


def solution(mesh):
    in_specs = (
        P(("rep", "shard", "tp"), None),
        P(("rep", "shard")),
        P(("rep", "shard"), None, "tp"),
        P("shard", None, "tp"),
        P("shard", None, "tp"),
        P("shard", None, "tp"),
    )
    out_specs = (
        P("shard", None, "tp"),
        P("shard", None, "tp"),
        P("shard", None, "tp"),
        P(("rep", "shard"), None, "tp"),
    )
    return jax.shard_map(local, mesh=mesh, in_specs=in_specs, out_specs=out_specs, check_vma=False)
```

```python
import functools

import jax
import jax.numpy as jnp
from jax import lax
from jax.experimental import pallas as pl
from jax.experimental.pallas import tpu as pltpu
from jax.sharding import PartitionSpec as P

beta_one = 0.9
beta_two = 0.95
step_count = 20
rate = 0.002
decay = 0.1
epsilon = 1e-08

LANES = 128
GROUPS = 4
VMEM_BYTES = 56 * 1024 * 1024

SMEM = pl.BlockSpec(memory_space=pltpu.SMEM)


def adamw(master, moment_one, moment_two, grad):
    first = beta_one * moment_one + (1.0 - beta_one) * grad
    second = beta_two * moment_two + (1.0 - beta_two) * grad * grad
    first_hat = first / (1.0 - beta_one**step_count)
    second_hat = second / (1.0 - beta_two**step_count)
    updated = master - rate * (first_hat / (jnp.sqrt(second_hat) + epsilon) + decay * master)
    return (updated, first, second)


def lane_rows(array):
    rows, two, features = array.shape
    split = array.reshape(rows, two, features // LANES, LANES)
    return split.transpose(0, 2, 1, 3).reshape(rows * two * features // LANES, LANES)


def from_lane_rows(array, rows, features):
    split = array.reshape(rows, features // LANES, 2, LANES)
    return split.transpose(0, 2, 1, 3).reshape(rows, 2, features)


def slots(features):
    return [half * features + tile * LANES for tile in range(features // LANES) for half in range(2)]


def call(kernel, out_shape, flops, moved, **kwargs):
    return pl.pallas_call(
        kernel,
        out_shape=out_shape,
        cost_estimate=pl.CostEstimate(flops=flops, bytes_accessed=moved, transcendentals=0),
        compiler_params=pltpu.CompilerParams(vmem_limit_bytes=VMEM_BYTES),
        **kwargs,
    )


def full(shape):
    return pl.BlockSpec(shape, lambda *_: (0,) * len(shape))


def f32(ref):
    return ref[...].astype(jnp.float32)


def pack(hidden, rep, groups, replicas, rows):
    tokens = hidden.shape[0]
    specs, shapes, orders = [], [], []
    for start, part, order in groups:
        for k in range(replicas):
            for s in range(len(order)):

                def index(i, place, at=1 + len(orders) + s, k=k, start=start, part=part):
                    return (0, (place[at] * replicas + (place[0] ^ k)) * (rows // part) + start // part)

                specs.append(pl.BlockSpec((tokens, part), index))
            shapes.append((tokens, len(order) * part))
        orders += order

    def kernel(place, *refs):
        sources, outs = iter(refs[: len(specs)]), iter(refs[len(specs) :])
        for start, part, order in groups:
            for k in range(replicas):
                out = next(outs)
                for s in range(len(order)):
                    out[:, s * part : (s + 1) * part] = next(sources)[...]

    outs = call(
        kernel,
        [jax.ShapeDtypeStruct(shape, hidden.dtype) for shape in shapes],
        0,
        4 * sum(shape[0] * shape[1] for shape in shapes),
        grid_spec=pltpu.PrefetchScalarGridSpec(
            num_scalar_prefetch=1,
            grid=(1,),
            in_specs=specs,
            out_specs=[full(shape) for shape in shapes],
        ),
    )(jnp.stack([rep, *orders]), *[hidden] * len(specs))
    return [outs[i : i + replicas] for i in range(0, len(outs), replicas)]


def mask(cotan, place, pairs):
    block, _, features = cotan.shape
    width, tokens = 2 * features, block // pairs
    per = width // LANES

    def kernel(place, source, out, count, scratch):
        scratch[...] = source[...].astype(jnp.float32)
        count[...] = jnp.full(count.shape, place[0]).astype(jnp.float32)
        for o in range(pairs):
            start = (place[1] ^ o) * tokens
            row = lax.broadcasted_iota(jnp.int32, (tokens, LANES), 0) + start
            for slot, column in enumerate(slots(features)):
                rows = scratch[pl.ds(start * per + slot, tokens, stride=per), :]
                out[o * tokens : (o + 1) * tokens, column : column + LANES] = jnp.where(
                    row < place[0], rows, 0.0
                ).astype(out.dtype)

    return call(
        kernel,
        [jax.ShapeDtypeStruct((block, width), cotan.dtype), jax.ShapeDtypeStruct((8, LANES), jnp.float32)],
        0,
        4 * block * width,
        grid=(1,),
        in_specs=[SMEM, full((block * per, LANES))],
        out_specs=[full((block, width)), full((8, LANES))],
        scratch_shapes=[pltpu.VMEM((block * per, LANES), jnp.float32)],
    )(place, lane_rows(cotan))


def fresh_weights(place, count, shares, params):
    part, width = shares[0][1].block_shape
    per = width // LANES

    def kernel(place, count, *refs):
        sources = refs[: len(shares)]
        master, first, second, weights, grad, scratch = refs[len(shares) :]
        grad[...] = sum(f32(source) for source in sources).astype(grad.dtype)
        scale = 1.0 / count[0:1, 0:1]
        starts = slots(width // 2)
        for slot, start in enumerate(starts):
            scratch[pl.ds(slot, part, stride=per), :] = grad[:, start : start + LANES].astype(jnp.float32)
        updated, _, _ = adamw(master[...], first[...], second[...], scratch[...] * scale)
        scratch[...] = updated
        for slot, start in enumerate(starts):
            weights[:, start : start + LANES] = scratch[pl.ds(slot, part, stride=per), :].astype(weights.dtype)

    param_spec = pl.BlockSpec((part * per, LANES), lambda i, place: (place[0], 0))
    return call(
        kernel,
        [jax.ShapeDtypeStruct((part, width), jnp.bfloat16)] * 2,
        20 * part * width,
        20 * part * width,
        grid_spec=pltpu.PrefetchScalarGridSpec(
            num_scalar_prefetch=1,
            grid=(1,),
            in_specs=[full((8, LANES)), *[spec for _, spec in shares], param_spec, param_spec, param_spec],
            out_specs=[pl.BlockSpec((part, width), lambda i, place: (0, 0))] * 2,
            scratch_shapes=[pltpu.VMEM((part * per, LANES), jnp.float32)],
        ),
    )(place, count, *[a for a, _ in shares], *params)


def update_kernel(place, count, grad, master, first, second, new_master, new_first, new_second, scratch):
    rows, width = grad.shape
    per = width // LANES
    scale = 1.0 / count[0:1, 0:1]
    for slot, start in enumerate(slots(width // 2)):
        scratch[pl.ds(slot, rows, stride=per), :] = grad[:, start : start + LANES].astype(jnp.float32)
    updated, one, two = adamw(master[...], first[...], second[...], scratch[...] * scale)
    new_master[...] = updated
    new_first[...] = one
    new_second[...] = two


def update(me, count, grads, params, block):
    replicas, rows, width = grads.shape
    per = width // LANES
    steps = rows // block
    param_spec = pl.BlockSpec((block * per, LANES), lambda k, i, me: ((me[0] ^ k) * steps + i, 0))
    return call(
        update_kernel,
        [jax.ShapeDtypeStruct(params[0].shape, jnp.float32)] * 3,
        20 * replicas * rows * width,
        26 * replicas * rows * width,
        grid_spec=pltpu.PrefetchScalarGridSpec(
            num_scalar_prefetch=1,
            grid=(replicas, steps),
            in_specs=[
                full((8, LANES)),
                pl.BlockSpec((None, block, width), lambda k, i, me: (k, i, 0)),
                param_spec,
                param_spec,
                param_spec,
            ],
            out_specs=[param_spec] * 3,
            scratch_shapes=[pltpu.VMEM((block * per, LANES), jnp.float32)],
        ),
    )(me, count, grads, *params)


def combine(shares, pair, pairs):
    rows, width = shares[0][1].block_shape
    features, tokens = width // 2, rows // pairs
    per = width // LANES

    def kernel(pair, *refs):
        sources, out, scratch = refs[: len(shares)], refs[-2], refs[-1]
        for o in range(pairs):
            start = (pair[0] ^ o) * tokens
            for slot, column in enumerate(slots(features)):
                total = None
                for source in sources:
                    piece = source[o * tokens : (o + 1) * tokens, column : column + LANES].astype(jnp.float32)
                    total = piece if total is None else total + piece
                scratch[pl.ds(start * per + slot, tokens, stride=per), :] = total
        out[...] = scratch[...].astype(out.dtype)

    out = call(
        kernel,
        jax.ShapeDtypeStruct((rows * per, LANES), jnp.bfloat16),
        0,
        8 * rows * width,
        grid=(1,),
        in_specs=[SMEM] + [s for _, s in shares],
        out_specs=full((rows * per, LANES)),
        scratch_shapes=[pltpu.VMEM((rows * per, LANES), jnp.float32)],
    )(pair, *[a for a, _ in shares])
    return from_lane_rows(out, rows, features)


def after(value, *deps):
    return lax.optimization_barrier((value, *deps))[0] if deps else value


def swap(value, axis, k):
    if k == 0:
        return value
    return lax.ppermute(value, axis, [(i, i ^ k) for i in range(lax.axis_size(axis))])


def add(a, b):
    return (a.astype(jnp.float32) + b.astype(jnp.float32)).astype(jnp.bfloat16)


class Line:
    ends_to_inner = [(0, 1), (3, 2)]
    across = [(1, 2), (2, 1)]
    inner_to_ends = [(1, 0), (2, 3)]

    def __init__(self, shard):
        self.end = (shard == 0) | (shard == 3)
        low = shard < 2
        self.order = [jnp.where(low, 3, 0), jnp.where(low, 2, 1), shard ^ 1, shard]

    def reduce(self, away, last):
        part = last.shape[0] // 2
        far = add(away, lax.ppermute(away, "shard", self.ends_to_inner))
        got = lax.ppermute(far, "shard", self.across)
        near = add(last[:part], got[:part])
        return [last[part:], got[part:], swap(near, "shard", 1)], (far, near)

    def gather(self, own):
        side = jnp.concatenate([swap(own, "shard", 1), own], axis=0)
        got = lax.ppermute(side, "shard", self.across)
        far = lax.ppermute(got, "shard", self.inner_to_ends)
        return [jnp.where(self.end, far, got), side]


class Halves:
    def __init__(self, shard, shards):
        order, k = [0], shards // 2
        while k:
            order, k = [i + k for i in order] + order, k // 2
        self.shards = shards
        self.order = [shard ^ q for q in order]

    def reduce(self, away, last):
        shares, half, k = [last, swap(away, "shard", 1)], last.shape[0], 2
        while k < self.shards:
            half //= 2
            sent = sum(v[:half].astype(jnp.float32) for v in shares).astype(jnp.bfloat16)
            shares, k = [v[half:] for v in shares] + [swap(sent, "shard", k)], 2 * k
        return shares, (sent, sent)

    def gather(self, own):
        blocks, k = own, self.shards // 2
        while k > 1:
            blocks, k = jnp.concatenate([swap(blocks, "shard", k), blocks], axis=0), k // 2
        return [swap(blocks, "shard", 1), blocks]


def local(hidden_in, lengths, kv_grad_out, master, moment_one, moment_two):
    replicas, shards, pairs = (lax.axis_size(name) for name in ("rep", "shard", "tp"))
    rep, shard, pair = (lax.axis_index(name).astype(jnp.int32) for name in ("rep", "shard", "tp"))
    tokens, depth = hidden_in.shape
    block, _, features = kv_grad_out.shape
    width = 2 * features
    rows = depth // (shards * replicas)
    near = replicas // 2
    parities = [k for k in range(replicas) if k % 2] + [k for k in range(replicas) if not k % 2]
    odd = replicas // 2 * block

    count_of_groups = max(1, min(GROUPS, rows // LANES))
    part = rows // count_of_groups
    last_group = count_of_groups - 1
    ways = [Line(shard) if shards == 4 and g < last_group else Halves(shard, shards) for g in range(count_of_groups)]
    groups = [(g * part, part, way.order) for g, way in enumerate(ways)]
    contract = (((0,), (0,)), ((), ()))

    def terms(here):
        return lax.dot_general(here, cotans, contract, preferred_element_type=jnp.float32).astype(jnp.bfloat16)

    def project(here, weights):
        return jnp.dot(here, weights, preferred_element_type=jnp.float32)

    pieces = pack(hidden_in, rep, groups[:1], replicas, rows)
    cotan, count = mask(kv_grad_out, jnp.stack([lengths[0], pair]), pairs)
    if last_group:
        pieces += pack(hidden_in, rep, groups[1:], replicas, rows)
    arrived, sides, line = [], [], []

    def travel(g, *waits):
        arrived.append(
            [pieces[g][0]]
            + [swap(after(h, *waits) if k >= near else h, "rep", k) for k, h in enumerate(pieces[g]) if k]
        )
        sides.append([])

    def pair_up(g, ks, *waits):
        for k in ks:
            sent = after(arrived[g][k], *line[-2:-1], *waits)
            sides[g].append([arrived[g][k]] + [swap(sent, "tp", o) for o in range(1, pairs)])
            line.append(sides[g][-1][-1])

    def lay(g):
        return jnp.concatenate([p for k in parities for p in sides[g][k]], axis=0)

    low, high = range(near), range(near, replicas)
    travel(0)
    pair_up(0, low)
    pair_up(0, high, cotan)
    k = near
    while k:
        count, k = count + swap(count, "rep", k), k // 2
        if k == near // 2:
            early = count
    ready = [early, *arrived[0][near:], *line[:near], *(pieces[1] if last_group else [])]
    cotans = {0: cotan, near: swap(after(cotan, *ready), "rep", near)}
    for g in range(1, len(groups)):
        travel(g, *([cotans[near]] if g == 1 else arrived[g - 1][near:]))
    if last_group:
        pair_up(1, low)
    k = near // 2
    while k:
        for have in list(cotans):
            cotans[have ^ k] = swap(cotans[have], "rep", k)
        k //= 2
    if last_group > 1:
        pair_up(2, low, cotans[near], count)
    cotans = jnp.concatenate([cotans[k] for k in parities], axis=0)
    k = 1
    while k < shards:
        count, k = count + swap(count, "shard", k), 2 * k

    params = [lane_rows(a) for a in (master, moment_one, moment_two)]
    spec = pl.BlockSpec((part, width), lambda i, place: (0, 0))
    inputs, steps, grads, fresh, total = [], [], [], [], None
    for g, way in enumerate(ways):
        here = after(lay(g), count)
        if g > 0:
            here = after(here, steps[g - 1][0])
        if g > 1:
            here = after(here, steps[g - 2][1])
        if g > 2:
            here = after(here, fresh[g - 3])
        inputs.append(here)
        half = shards // 2 * part
        away = terms(here[:, :half])
        last = terms(after(here, away)[:, half:])
        if g + 1 <= last_group:
            pair_up(g + 1, high, last)
        if g + 3 <= last_group:
            pair_up(g + 3, low, last)
        shares, passed = way.reduce(away, last)
        steps.append(passed)
        place = (rep * len(groups) + g)[None]
        if g == last_group and g > 1:
            shares = [after(shares[0], total)] + shares[1:]
        weights, grad = fresh_weights(place, count, [(v, spec) for v in shares], params)
        fresh.append(weights)
        grads.append(grad)
        weights = way.gather(weights)
        if g < last_group:
            if g < 2:
                product = project(inputs[g], jnp.concatenate(weights, axis=0))
                total = product if total is None else total + product
            else:
                later = (inputs[g], weights)

    every = {0: jnp.concatenate(grads, axis=0)}
    k = near
    while k:
        for have in list(every):
            every[have ^ k] = swap(every[have], "rep", k)
        k //= 2

    if last_group > 1:
        total = total + project(later[0], jnp.concatenate(later[1], axis=0))
    half = weights[-1].shape[0]
    product = project(here[:, -half:], weights[-1])
    total = product if total is None else total + product
    here = after(here[:, :-half], every[near], total)
    weights = jnp.concatenate(weights[:-1], axis=0) if len(weights) > 2 else weights[0]
    away = (total[:odd] + project(here[:odd], weights)).astype(jnp.bfloat16)
    stay = (total[odd:] + project(after(here, away)[odd:], weights)).astype(jnp.bfloat16)
    shares = [stay, swap(away, "rep", 1)]
    half, k = odd // 2, 2
    while k < replicas:
        sent = sum(v[half : 2 * half].astype(jnp.float32) for v in shares).astype(jnp.bfloat16)
        shares.append(swap(sent, "rep", k))
        half, k = half // 2, 2 * k
    fresh = combine([(v, full((block, width))) for v in shares], pair[None], pairs)

    every = jnp.stack([every[k] for k in range(replicas)])
    updated = update(rep[None], count, every, params, min(rows, 256))
    updated = [from_lane_rows(a, master.shape[0], features) for a in updated]
    return (*updated, fresh)


def solution(mesh):
    in_specs = (
        P(("rep", "shard", "tp"), None),
        P(("rep", "shard")),
        P(("rep", "shard"), None, "tp"),
        P("shard", None, "tp"),
        P("shard", None, "tp"),
        P("shard", None, "tp"),
    )
    out_specs = (
        P("shard", None, "tp"),
        P("shard", None, "tp"),
        P("shard", None, "tp"),
        P(("rep", "shard"), None, "tp"),
    )
    return jax.shard_map(local, mesh=mesh, in_specs=in_specs, out_specs=out_specs, check_vma=False)
```

```python
import functools

import jax
import jax.numpy as jnp
from jax import lax
from jax.experimental import pallas as pl
from jax.experimental.pallas import tpu as pltpu
from jax.sharding import PartitionSpec as P

beta_one = 0.9
beta_two = 0.95
step_count = 20
rate = 0.002
decay = 0.1
epsilon = 1e-08

LANES = 128
VMEM_BYTES = 56 * 1024 * 1024

SMEM = pl.BlockSpec(memory_space=pltpu.SMEM)


def adamw(master, moment_one, moment_two, grad):
    first = beta_one * moment_one + (1.0 - beta_one) * grad
    second = beta_two * moment_two + (1.0 - beta_two) * grad * grad
    first_hat = first / (1.0 - beta_one**step_count)
    second_hat = second / (1.0 - beta_two**step_count)
    updated = master - rate * (first_hat / (jnp.sqrt(second_hat) + epsilon) + decay * master)
    return (updated, first, second)


def lane_rows(array):
    rows, two, features = array.shape
    split = array.reshape(rows, two, features // LANES, LANES)
    return split.transpose(0, 2, 1, 3).reshape(rows * two * features // LANES, LANES)


def from_lane_rows(array, rows, features):
    split = array.reshape(rows, features // LANES, 2, LANES)
    return split.transpose(0, 2, 1, 3).reshape(rows, 2, features)


def slots(features):
    return [half * features + tile * LANES for tile in range(features // LANES) for half in range(2)]


def call(kernel, out_shape, flops, moved, **kwargs):
    return pl.pallas_call(
        kernel,
        out_shape=out_shape,
        cost_estimate=pl.CostEstimate(flops=flops, bytes_accessed=moved, transcendentals=0),
        compiler_params=pltpu.CompilerParams(vmem_limit_bytes=VMEM_BYTES),
        **kwargs,
    )


def full(shape):
    return pl.BlockSpec(shape, lambda *_: (0,) * len(shape))


def f32(ref):
    return ref[...].astype(jnp.float32)


def pack(hidden, rep, loads, replicas, rows):
    tokens = hidden.shape[0]
    specs, shapes, orders = [], [], []
    for load in loads:
        for k in range(replicas):
            at = len(orders)
            for start, part, order in load:
                for _ in order:
                    at += 1

                    def index(i, place, at=at, k=k, start=start, part=part):
                        return (0, (place[at] * replicas + (place[0] ^ k)) * (rows // part) + start // part)

                    specs.append(pl.BlockSpec((tokens, part), index))
            shapes.append((sum(part * len(order) for _, part, order in load), tokens))
        orders += [shard for _, _, order in load for shard in order]

    def kernel(place, *refs):
        sources, outs = iter(refs[: len(specs)]), iter(refs[len(specs) :])
        for load in loads:
            for k in range(replicas):
                out, row = next(outs), 0
                for _, part, order in load:
                    for _ in order:
                        out[row : row + part, :] = next(sources)[...].T
                        row += part

    outs = call(
        kernel,
        [jax.ShapeDtypeStruct(shape, hidden.dtype) for shape in shapes],
        0,
        4 * sum(shape[0] * shape[1] for shape in shapes),
        grid_spec=pltpu.PrefetchScalarGridSpec(
            num_scalar_prefetch=1,
            grid=(1,),
            in_specs=specs,
            out_specs=[full(shape) for shape in shapes],
        ),
    )(jnp.stack([rep, *orders]), *[hidden] * len(specs))
    return [outs[i : i + replicas] for i in range(0, len(outs), replicas)]


def mask(cotan, place, pairs):
    block, _, features = cotan.shape
    width, tokens = 2 * features, block // pairs
    per = width // LANES

    def kernel(place, source, out, count, scratch):
        scratch[...] = source[...].astype(jnp.float32)
        count[...] = jnp.full(count.shape, place[0]).astype(jnp.float32)
        for o in range(pairs):
            start = (place[1] ^ o) * tokens
            row = lax.broadcasted_iota(jnp.int32, (tokens, LANES), 0) + start
            for slot, column in enumerate(slots(features)):
                rows = scratch[pl.ds(start * per + slot, tokens, stride=per), :]
                out[o * tokens : (o + 1) * tokens, column : column + LANES] = jnp.where(
                    row < place[0], rows, 0.0
                ).astype(out.dtype)

    return call(
        kernel,
        [jax.ShapeDtypeStruct((block, width), cotan.dtype), jax.ShapeDtypeStruct((8, LANES), jnp.float32)],
        0,
        4 * block * width,
        grid=(1,),
        in_specs=[SMEM, full((block * per, LANES))],
        out_specs=[full((block, width)), full((8, LANES))],
        scratch_shapes=[pltpu.VMEM((block * per, LANES), jnp.float32)],
    )(place, lane_rows(cotan))


def fresh_weights(place, count, shares, params, part, halves, features):
    per = 2 * features // LANES
    width = len(halves) * features
    columns = [
        (slot, start - halves[0] * features)
        for slot, start in enumerate(slots(features))
        if start // features in halves
    ]

    def kernel(place, count, *refs):
        sources = refs[: len(shares)]
        master, first, second, weights, grad = refs[len(shares) :]
        scale = 1.0 / count[0:1, 0:1]
        for slot, start in columns:
            at = slice(start, start + LANES)
            share = sum(source[:, at].astype(jnp.float32) for source in sources).astype(grad.dtype)
            grad[:, at] = share
            rows = pl.ds(slot, part, stride=per)
            updated, _, _ = adamw(master[rows, :], first[rows, :], second[rows, :], share.astype(jnp.float32) * scale)
            weights[:, at] = updated.astype(weights.dtype)

    param_spec = pl.BlockSpec((part * per, LANES), lambda i, place: (place[0], 0))
    specs = [pl.BlockSpec((part, width), lambda i, place, row=row: (row, 0)) for _, row in shares]
    return call(
        kernel,
        [jax.ShapeDtypeStruct((part, width), jnp.bfloat16)] * 2,
        20 * part * width,
        20 * part * width,
        grid_spec=pltpu.PrefetchScalarGridSpec(
            num_scalar_prefetch=1,
            grid=(1,),
            in_specs=[full((8, LANES)), *specs, param_spec, param_spec, param_spec],
            out_specs=[pl.BlockSpec((part, width), lambda i, place: (0, 0))] * 2,
        ),
    )(place, count, *[v for v, _ in shares], *params)


def update(place, count, grads, params, per_replica, before):
    part, width = grads[0].shape
    per = width // LANES

    def kernel(place, count, *refs):
        sources = refs[: len(grads)]
        master, first, second = refs[len(grads) : len(grads) + 3]
        new_master, new_first, new_second, scratch = refs[-4:]
        scale = 1.0 / count[0:1, 0:1]
        for j, grad in enumerate(sources):

            @pl.when(pl.program_id(0) == j)
            def _(grad=grad):
                for slot, start in enumerate(slots(width // 2)):
                    scratch[pl.ds(slot, part, stride=per), :] = grad[:, start : start + LANES].astype(jnp.float32)

        updated, one, two = adamw(master[...], first[...], second[...], scratch[...] * scale)
        new_master[...] = updated
        new_first[...] = one
        new_second[...] = two

    param_spec = pl.BlockSpec((part * per, LANES), lambda k, place: ((place[0] ^ k) * per_replica + place[1], 0))
    size = len(grads) * part * width
    return call(
        kernel,
        [jax.ShapeDtypeStruct(params[0].shape, jnp.float32)] * 3,
        20 * size,
        26 * size,
        grid_spec=pltpu.PrefetchScalarGridSpec(
            num_scalar_prefetch=1,
            grid=(len(grads),),
            in_specs=[full((8, LANES))]
            + [full((part, width))] * len(grads)
            + [param_spec] * 3
            + [pl.BlockSpec(memory_space=pl.ANY)] * len(before),
            out_specs=[param_spec] * 3,
            scratch_shapes=[pltpu.VMEM((part * per, LANES), jnp.float32)],
        ),
        input_output_aliases={2 + len(grads) + 3 + i: i for i in range(len(before))},
    )(place, count, *grads, *params, *before)


def combine(shares, pair, pairs, rows):
    features = shares[0][0].shape[1]
    tokens, per = rows // pairs, 2 * features // LANES
    each = len(shares[0])

    def kernel(pair, *refs):
        out, scratch = refs[-2], refs[-1]
        for o in range(pairs):
            start = (pair[0] ^ o) * tokens
            for slot, column in enumerate(slots(features)):
                half, at = divmod(column, features)
                total = sum(
                    source[o * tokens : (o + 1) * tokens, at : at + LANES].astype(jnp.float32)
                    for source in refs[half * each : (half + 1) * each]
                )
                scratch[pl.ds(start * per + slot, tokens, stride=per), :] = total
        out[...] = scratch[...].astype(out.dtype)

    out = call(
        kernel,
        jax.ShapeDtypeStruct((rows * per, LANES), jnp.bfloat16),
        0,
        16 * rows * features,
        grid=(1,),
        in_specs=[SMEM] + [full((rows, features))] * (2 * each),
        out_specs=full((rows * per, LANES)),
        scratch_shapes=[pltpu.VMEM((rows * per, LANES), jnp.float32)],
    )(pair, *shares[0], *shares[1])
    return from_lane_rows(out, rows, features)


def after(value, *deps):
    return lax.optimization_barrier((value, *deps))[0] if deps else value


def swap(value, axis, k):
    if k == 0:
        return value
    return lax.ppermute(value, axis, [(i, i ^ k) for i in range(lax.axis_size(axis))])


def to_bf16(value):
    return value.astype(jnp.bfloat16)


def plus(*values):
    return to_bf16(sum(v.astype(jnp.float32) for v in values))


def exchange(value, axis, size):
    have, k = {0: value}, size // 2
    while k:
        for j in list(have):
            have[j ^ k] = swap(have[j], axis, k)
        k //= 2
    return [have[k] for k in range(size)]


def local(hidden_in, lengths, kv_grad_out, master, moment_one, moment_two):
    replicas, shards, pairs = (lax.axis_size(name) for name in ("rep", "shard", "tp"))
    rep, shard, pair = (lax.axis_index(name).astype(jnp.int32) for name in ("rep", "shard", "tp"))
    tokens, depth = hidden_in.shape
    block, _, features = kv_grad_out.shape
    width = 2 * features
    rows = depth // (shards * replicas)
    near = replicas // 2
    parities = [k for k in range(replicas) if k % 2] + [k for k in range(replicas) if not k % 2]
    odd = replicas // 2 * block

    two = rows % (4 * LANES) == 0
    part = rows // 2 if two else rows
    order = [shard ^ q for q in range(shards)]
    loads = [[(start, part, order)] for start in range(0, rows, part)]
    by_rows = (((0,), (0,)), ((), ()))

    def project(rows, weights):
        return lax.dot_general(rows, weights, by_rows, preferred_element_type=jnp.float32)

    def term(rows, cotans):
        return to_bf16(jnp.dot(rows, cotans, preferred_element_type=jnp.float32))

    pieces = pack(hidden_in, rep, loads[:1], replicas, rows)
    cotan, count = mask(kv_grad_out, jnp.stack([lengths[0], pair]), pairs)
    if len(loads) > 1:
        pieces += pack(hidden_in, rep, loads[1:], replicas, rows)
    arrived, sides, line = [], [], []

    def travel(n, *waits):
        arrived.append(
            [pieces[n][0]]
            + [swap(after(h, *waits) if k >= near else h, "rep", k) for k, h in enumerate(pieces[n]) if k]
        )
        sides.append([])

    def pair_up(n, ks, *waits):
        for k in ks:
            sent = after(arrived[n][k], *line[-2:-1], *waits)
            sides[n].append([arrived[n][k]] + [swap(sent, "tp", o) for o in range(1, pairs)])
            line.append(sides[n][-1][-1])

    def lay(n):
        return jnp.concatenate([p for k in parities for p in sides[n][k]], axis=1)

    low, high = range(near), range(near, replicas)
    travel(0)
    pair_up(0, low)
    pair_up(0, high, cotan)
    k = near
    while k:
        count, k = count + swap(count, "rep", k), k // 2
    k = 1
    while k < shards:
        count, k = count + swap(count, "shard", k), 2 * k
    ready = [count, *arrived[0][near:], *line[:near], *(pieces[1] if two else [])]
    cotans = {0: cotan, near: swap(after(cotan, *ready), "rep", near)}
    if two:
        travel(1, cotans[near])
        pair_up(1, low)
    k = near // 2
    while k:
        for have in list(cotans):
            cotans[have ^ k] = swap(cotans[have], "rep", k)
        k //= 2
    cotans = jnp.concatenate([cotans[k] for k in parities], axis=0)

    params = [lane_rows(a) for a in (master, moment_one, moment_two)]
    halves = (slice(0, features), slice(features, width))
    laid, fresh, updated, all_grads, passed = [], [], [], [], []
    for n in range(len(loads)):
        rows_of = lay(n)
        if n == 0 and two:
            rows_of = after(rows_of, line[replicas])
        laid.append(rows_of)
        fresh.append([])
        grads = []
        for j, side in enumerate(halves):
            here = rows_of
            if n:
                here = after(here, fresh[0][j][0])
            blocks = []
            for q in reversed(range(shards)):
                now = after(here[q * part : (q + 1) * part], *blocks[-1:])
                blocks.append(term(now, cotans[:, side]))
            if n == 0 and two:
                if j == 0:
                    pair_up(1, range(near, near + 1), blocks[-1])
                else:
                    pair_up(1, range(near + 1, replicas), blocks[-1])
            blocks = blocks[::-1]
            shares = [blocks[0]] + [swap(b, "shard", q) for q, b in enumerate(blocks) if q]
            shares[0] = after(shares[0], *passed)
            place = (rep * (rows // part) + n)[None]
            own, grad = fresh_weights(place, count, [(v, 0) for v in shares], params, part, (j,), features)
            grads.append(grad)
            gathered, k = {0: own}, shards // 2
            while k:
                for q in list(gathered):
                    gathered[q ^ k] = swap(gathered[q], "shard", k)
                k //= 2
            fresh[n].append([gathered[q] for q in range(shards)])
            if n:
                passed = [fresh[0][j][-1], fresh[0][1][2], *all_grads[0][near:near + 1]]
        all_grads.append(exchange(jnp.concatenate(grads, axis=1), "rep", replicas))

    updated = update(jnp.stack([rep, jnp.int32(0)]), count, all_grads[0], params, rows // part, [])
    sums, turn = [], updated[0]
    final = (shards - 1) * part
    for j in range(2):
        total = None
        if two:
            total = project(laid[0], jnp.concatenate(fresh[0][j], axis=0))
        product = project(laid[-1][:final], jnp.concatenate(fresh[-1][j][:-1], axis=0))
        total = product if total is None else total + product
        last = after(laid[-1][final:], turn, total, *([all_grads[-1][near]] if j else []))
        away = project(last[:, :odd], fresh[-1][j][-1])
        away = to_bf16(total[:odd] + away)
        stay = project(after(last, away)[:, odd:], fresh[-1][j][-1])
        stay = to_bf16(total[odd:] + stay)
        shares = [stay, swap(away, "rep", 1)]
        size, k = odd // 2, 2
        while k < replicas:
            sent = plus(*[v[size : 2 * size] for v in shares])
            turn = sent
            shares.append(swap(sent, "rep", k))
            size, k = size // 2, 2 * k
        sums.append(shares)
    fresh_kv = combine(sums, pair[None], pairs, block)
    if two:
        others = [after(all_grads[1][0], turn)] + all_grads[1][1:]
        updated = update(jnp.stack([rep, jnp.int32(1)]), count, others, params, rows // part, updated)
    updated = [from_lane_rows(a, master.shape[0], features) for a in updated]
    return (*updated, fresh_kv)


def solution(mesh):
    in_specs = (
        P(("rep", "shard", "tp"), None),
        P(("rep", "shard")),
        P(("rep", "shard"), None, "tp"),
        P("shard", None, "tp"),
        P("shard", None, "tp"),
        P("shard", None, "tp"),
    )
    out_specs = (
        P("shard", None, "tp"),
        P("shard", None, "tp"),
        P("shard", None, "tp"),
        P(("rep", "shard"), None, "tp"),
    )
    return jax.shard_map(local, mesh=mesh, in_specs=in_specs, out_specs=out_specs, check_vma=False)
```

```python
import functools

import jax
import jax.numpy as jnp
from jax import lax
from jax.experimental import pallas as pl
from jax.experimental.pallas import tpu as pltpu
from jax.sharding import PartitionSpec as P

beta_one = 0.9
beta_two = 0.95
step_count = 20
rate = 0.002
decay = 0.1
epsilon = 1e-08

LANES = 128
GROUPS = 4
LOADS = 2
VMEM_BYTES = 56 * 1024 * 1024

SMEM = pl.BlockSpec(memory_space=pltpu.SMEM)


def adamw(master, moment_one, moment_two, grad):
    first = beta_one * moment_one + (1.0 - beta_one) * grad
    second = beta_two * moment_two + (1.0 - beta_two) * grad * grad
    first_hat = first / (1.0 - beta_one**step_count)
    second_hat = second / (1.0 - beta_two**step_count)
    updated = master - rate * (first_hat / (jnp.sqrt(second_hat) + epsilon) + decay * master)
    return (updated, first, second)


def lane_rows(array):
    rows, two, features = array.shape
    split = array.reshape(rows, two, features // LANES, LANES)
    return split.transpose(0, 2, 1, 3).reshape(rows * two * features // LANES, LANES)


def from_lane_rows(array, rows, features):
    split = array.reshape(rows, features // LANES, 2, LANES)
    return split.transpose(0, 2, 1, 3).reshape(rows, 2, features)


def slots(features):
    return [half * features + tile * LANES for tile in range(features // LANES) for half in range(2)]


def call(kernel, out_shape, flops, moved, **kwargs):
    return pl.pallas_call(
        kernel,
        out_shape=out_shape,
        cost_estimate=pl.CostEstimate(flops=flops, bytes_accessed=moved, transcendentals=0),
        compiler_params=pltpu.CompilerParams(vmem_limit_bytes=VMEM_BYTES),
        **kwargs,
    )


def full(shape):
    return pl.BlockSpec(shape, lambda *_: (0,) * len(shape))


def f32(ref):
    return ref[...].astype(jnp.float32)


def pack(hidden, rep, loads, replicas, rows):
    tokens = hidden.shape[0]
    specs, shapes, orders = [], [], []
    for load in loads:
        for k in range(replicas):
            at = len(orders)
            for start, part, order in load:
                for _ in order:
                    at += 1

                    def index(i, place, at=at, k=k, start=start, part=part):
                        return (0, (place[at] * replicas + (place[0] ^ k)) * (rows // part) + start // part)

                    specs.append(pl.BlockSpec((tokens, part), index))
            shapes.append((sum(part * len(order) for _, part, order in load), tokens))
        orders += [shard for _, _, order in load for shard in order]

    def kernel(place, *refs):
        sources, outs = iter(refs[: len(specs)]), iter(refs[len(specs) :])
        for load in loads:
            for k in range(replicas):
                out, row = next(outs), 0
                for _, part, order in load:
                    for _ in order:
                        out[row : row + part, :] = next(sources)[...].T
                        row += part

    outs = call(
        kernel,
        [jax.ShapeDtypeStruct(shape, hidden.dtype) for shape in shapes],
        0,
        4 * sum(shape[0] * shape[1] for shape in shapes),
        grid_spec=pltpu.PrefetchScalarGridSpec(
            num_scalar_prefetch=1,
            grid=(1,),
            in_specs=specs,
            out_specs=[full(shape) for shape in shapes],
        ),
    )(jnp.stack([rep, *orders]), *[hidden] * len(specs))
    return [outs[i : i + replicas] for i in range(0, len(outs), replicas)]


def mask(cotan, place, pairs):
    block, _, features = cotan.shape
    width, tokens = 2 * features, block // pairs
    per = width // LANES

    def kernel(place, source, out, count, scratch):
        scratch[...] = source[...].astype(jnp.float32)
        count[...] = jnp.full(count.shape, place[0]).astype(jnp.float32)
        for o in range(pairs):
            start = (place[1] ^ o) * tokens
            row = lax.broadcasted_iota(jnp.int32, (tokens, LANES), 0) + start
            for slot, column in enumerate(slots(features)):
                rows = scratch[pl.ds(start * per + slot, tokens, stride=per), :]
                out[o * tokens : (o + 1) * tokens, column : column + LANES] = jnp.where(
                    row < place[0], rows, 0.0
                ).astype(out.dtype)

    return call(
        kernel,
        [jax.ShapeDtypeStruct((block, width), cotan.dtype), jax.ShapeDtypeStruct((8, LANES), jnp.float32)],
        0,
        4 * block * width,
        grid=(1,),
        in_specs=[SMEM, full((block * per, LANES))],
        out_specs=[full((block, width)), full((8, LANES))],
        scratch_shapes=[pltpu.VMEM((block * per, LANES), jnp.float32)],
    )(place, lane_rows(cotan))


def fresh_weights(place, count, shares, params):
    part, width = shares[0][1].block_shape
    per = width // LANES

    def kernel(place, count, *refs):
        sources = refs[: len(shares)]
        master, first, second, weights, grad, scratch = refs[len(shares) :]
        grad[...] = sum(f32(source) for source in sources).astype(grad.dtype)
        scale = 1.0 / count[0:1, 0:1]
        starts = slots(width // 2)
        for slot, start in enumerate(starts):
            scratch[pl.ds(slot, part, stride=per), :] = grad[:, start : start + LANES].astype(jnp.float32)
        updated, _, _ = adamw(master[...], first[...], second[...], scratch[...] * scale)
        scratch[...] = updated
        for slot, start in enumerate(starts):
            weights[:, start : start + LANES] = scratch[pl.ds(slot, part, stride=per), :].astype(weights.dtype)

    param_spec = pl.BlockSpec((part * per, LANES), lambda i, place: (place[0], 0))
    return call(
        kernel,
        [jax.ShapeDtypeStruct((part, width), jnp.bfloat16)] * 2,
        20 * part * width,
        20 * part * width,
        grid_spec=pltpu.PrefetchScalarGridSpec(
            num_scalar_prefetch=1,
            grid=(1,),
            in_specs=[full((8, LANES)), *[spec for _, spec in shares], param_spec, param_spec, param_spec],
            out_specs=[pl.BlockSpec((part, width), lambda i, place: (0, 0))] * 2,
            scratch_shapes=[pltpu.VMEM((part * per, LANES), jnp.float32)],
        ),
    )(place, count, *[a for a, _ in shares], *params)


def update(me, count, grads, params, ks, block, before):
    rows, width = grads[0].shape
    per = width // LANES
    steps = rows // block
    first_k = min(ks)

    def kernel(place, count, *refs):
        sources = refs[: len(grads)]
        master, first, second = refs[len(grads) : len(grads) + 3]
        new_master, new_first, new_second, scratch = refs[-4:]
        scale = 1.0 / count[0:1, 0:1]
        for j, grad in enumerate(sources):

            @pl.when(pl.program_id(0) == j)
            def _(grad=grad):
                for slot, start in enumerate(slots(width // 2)):
                    scratch[pl.ds(slot, block, stride=per), :] = grad[:, start : start + LANES].astype(jnp.float32)

        updated, one, two = adamw(master[...], first[...], second[...], scratch[...] * scale)
        new_master[...] = updated
        new_first[...] = one
        new_second[...] = two

    def grad_spec(j):
        return pl.BlockSpec(
            (block, width), lambda k, i, me: (jnp.where(k == j, i, jnp.where(k < j, 0, steps - 1)), 0)
        )

    param_spec = pl.BlockSpec((block * per, LANES), lambda k, i, me: ((me[0] ^ (k + first_k)) * steps + i, 0))
    size = len(ks) * rows * width
    return call(
        kernel,
        [jax.ShapeDtypeStruct(params[0].shape, jnp.float32)] * 3,
        20 * size,
        26 * size,
        grid_spec=pltpu.PrefetchScalarGridSpec(
            num_scalar_prefetch=1,
            grid=(len(ks), steps),
            in_specs=[full((8, LANES))]
            + [grad_spec(j) for j in range(len(grads))]
            + [param_spec] * 3
            + [pl.BlockSpec(memory_space=pl.ANY)] * len(before),
            out_specs=[param_spec] * 3,
            scratch_shapes=[pltpu.VMEM((block * per, LANES), jnp.float32)],
        ),
        input_output_aliases={2 + len(grads) + 3 + i: i for i in range(len(before))},
    )(me, count, *grads, *params, *before)


def combine(shares, pair, pairs, rows):
    features = shares[0][0].shape[1]
    tokens, per = rows // pairs, 2 * features // LANES
    each = len(shares[0])

    def kernel(pair, *refs):
        out, scratch = refs[-2], refs[-1]
        for o in range(pairs):
            start = (pair[0] ^ o) * tokens
            for slot, column in enumerate(slots(features)):
                half, at = divmod(column, features)
                total = sum(
                    source[o * tokens : (o + 1) * tokens, at : at + LANES].astype(jnp.float32)
                    for source in refs[half * each : (half + 1) * each]
                )
                scratch[pl.ds(start * per + slot, tokens, stride=per), :] = total
        out[...] = scratch[...].astype(out.dtype)

    out = call(
        kernel,
        jax.ShapeDtypeStruct((rows * per, LANES), jnp.bfloat16),
        0,
        16 * rows * features,
        grid=(1,),
        in_specs=[SMEM] + [full((rows, features))] * (2 * each),
        out_specs=full((rows * per, LANES)),
        scratch_shapes=[pltpu.VMEM((rows * per, LANES), jnp.float32)],
    )(pair, *shares[0], *shares[1])
    return from_lane_rows(out, rows, features)


def after(value, *deps):
    return lax.optimization_barrier((value, *deps))[0] if deps else value


def swap(value, axis, k):
    if k == 0:
        return value
    return lax.ppermute(value, axis, [(i, i ^ k) for i in range(lax.axis_size(axis))])


def add(a, b):
    return (a.astype(jnp.float32) + b.astype(jnp.float32)).astype(jnp.bfloat16)


class Line:
    ends_to_inner = [(0, 1), (3, 2)]
    across = [(1, 2), (2, 1)]
    inner_to_ends = [(1, 0), (2, 3)]

    def __init__(self, shard):
        self.end = (shard == 0) | (shard == 3)
        low = shard < 2
        self.order = [jnp.where(low, 3, 0), jnp.where(low, 2, 1), shard ^ 1, shard]

    def reduce(self, away, last, soon):
        part = last.shape[0] // 2
        far = add(away, after(lax.ppermute(away, "shard", self.ends_to_inner), *soon))
        got = lax.ppermute(far, "shard", self.across)
        near = add(last[:part], got[:part])
        return [(last, 1), (got, 1), (swap(near, "shard", 1), 0)], (far, near)

    def gather(self, own):
        side = jnp.concatenate([swap(own, "shard", 1), own], axis=0)
        got = lax.ppermute(side, "shard", self.across)
        far = lax.ppermute(got, "shard", self.inner_to_ends)
        return [jnp.where(self.end, far, got), side]


class Halves:
    def __init__(self, shard, shards):
        order, k = [0], shards // 2
        while k:
            order, k = [i + k for i in order] + order, k // 2
        self.shards = shards
        self.order = [shard ^ q for q in order]

    def reduce(self, away, last, soon):
        shares, half, k = [last, swap(away, "shard", 1)], last.shape[0], 2
        while k < self.shards:
            sent = sum(v[v.shape[0] - half : v.shape[0] - half // 2].astype(jnp.float32) for v in shares)
            sent, half, k = sent.astype(jnp.bfloat16), half // 2, 2 * k
            shares.append(swap(sent, "shard", k // 2))
        return [(v, v.shape[0] // half - 1) for v in shares], (sent, sent)

    def gather(self, own):
        blocks, k = own, self.shards // 2
        while k > 1:
            blocks, k = jnp.concatenate([swap(blocks, "shard", k), blocks], axis=0), k // 2
        return [swap(blocks, "shard", 1), blocks]


def local(hidden_in, lengths, kv_grad_out, master, moment_one, moment_two):
    replicas, shards, pairs = (lax.axis_size(name) for name in ("rep", "shard", "tp"))
    rep, shard, pair = (lax.axis_index(name).astype(jnp.int32) for name in ("rep", "shard", "tp"))
    tokens, depth = hidden_in.shape
    block, _, features = kv_grad_out.shape
    width = 2 * features
    rows = depth // (shards * replicas)
    near = replicas // 2
    parities = [k for k in range(replicas) if k % 2] + [k for k in range(replicas) if not k % 2]
    odd = replicas // 2 * block

    number = max(1, min(GROUPS, rows // LANES))
    part = rows // number
    ways = [Line(shard) if shards == 4 and g < number - 1 else Halves(shard, shards) for g in range(number)]
    groups = [(g * part, part, way.order) for g, way in enumerate(ways)]
    each = max(1, number // LOADS)
    loads = [groups[g : g + each] for g in range(0, number, each)]
    by_rows = (((0,), (0,)), ((), ()))

    count, k = jnp.full((8, LANES), lengths[0]).astype(jnp.float32), near
    count = count + swap(count, "rep", k)
    early, k = count, k // 2
    while k:
        count, k = count + swap(count, "rep", k), k // 2
    k = 1
    while k < shards:
        count, k = count + swap(count, "shard", k), 2 * k
    pieces = pack(hidden_in, rep, loads[:1], replicas, rows)
    cotan, _ = mask(kv_grad_out, jnp.stack([lengths[0], pair]), pairs)
    if len(loads) > 1:
        pieces += pack(hidden_in, after(rep, count), loads[1:], replicas, rows)
    arrived, sides, line = [], [], []

    def travel(n, *waits):
        arrived.append(
            [pieces[n][0]]
            + [swap(after(h, *waits) if k >= near else h, "rep", k) for k, h in enumerate(pieces[n]) if k]
        )
        sides.append([])

    def pair_up(n, ks, *waits):
        for k in ks:
            sent = after(arrived[n][k], *line[-2:-1], *waits)
            sides[n].append([arrived[n][k]] + [swap(sent, "tp", o) for o in range(1, pairs)])
            line.append(sides[n][-1][-1])

    def lay(n):
        return jnp.concatenate([p for k in parities for p in sides[n][k]], axis=1)

    low, high = range(near), range(near, replicas)
    travel(0, early)
    pair_up(0, low)
    pair_up(0, high, cotan)
    ready = [*arrived[0][near:], *line[:near], *(pieces[1] if len(loads) > 1 else [])]
    cotans = {0: cotan, near: swap(after(cotan, *ready), "rep", near)}
    for n in range(1, len(loads)):
        travel(n, *([cotans[near]] if n == 1 else arrived[n - 1][near:]))
        if n == 1:
            pair_up(1, low)
    k = near // 2
    while k:
        for have in list(cotans):
            cotans[have ^ k] = swap(cotans[have], "rep", k)
        k //= 2
    cotans = jnp.concatenate([cotans[k] for k in parities], axis=0)

    params = [lane_rows(a) for a in (master, moment_one, moment_two)]
    steps, grads, fresh, total, kept, last = [], [], [], None, None, None

    def project(rows, weights):
        return lax.dot_general(rows, weights, by_rows, preferred_element_type=jnp.float32)

    for g, way in enumerate(ways):
        n, inside = divmod(g, each)
        if inside == 0:
            laid = lay(n)
            if n:
                laid = after(laid, fresh[(n - 1) * each], *[passed[1] for passed in steps])
        if last is not None:
            laid = after(laid, last)
        if n + 1 < len(loads) and inside == 1:
            laid = after(laid, line[(n + 1) * replicas])
        if n and inside:
            laid = after(laid, fresh[n * each - 1])
        half, first_row = shards // 2 * part, inside * shards * part
        here = laid[first_row : first_row + 2 * half]
        away = jnp.dot(here[:half], cotans, preferred_element_type=jnp.float32).astype(jnp.bfloat16)
        laid = after(laid, away)
        last = laid[first_row + half : first_row + 2 * half]
        last = jnp.dot(last, cotans, preferred_element_type=jnp.float32).astype(jnp.bfloat16)
        soon = arrived[n + 1][near:] if n + 1 < len(loads) and inside else []
        if not n and inside:
            away = after(away, steps[-1][0])
        shares, passed = way.reduce(away, last, soon)
        steps.append(passed)
        if n + 1 < len(loads):
            pair_up(n + 1, range(near + inside, near + inside + 1 if inside < each - 1 else replicas), passed[0])
        place = (rep * number + g)[None]
        specs = [
            (v, pl.BlockSpec((part, width), lambda i, place, row=row: (row, 0))) for v, row in shares
        ]
        if g >= each and total is not None:
            specs[0] = (after(specs[0][0], total), specs[0][1])
        weights, grad = fresh_weights(place, count, specs, params)
        fresh.append(weights)
        grads.append(grad)
        weights = way.gather(weights)
        if kept is not None:
            product = project(kept[0], jnp.concatenate(kept[1], axis=0))
            total = product if total is None else total + product
        kept = (laid[first_row : first_row + 2 * half], weights)

    every = {0: jnp.concatenate(grads, axis=0)}
    k = near
    while k:
        for have in list(every):
            every[have ^ k] = swap(every[have], "rep", k)
        k //= 2

    own = update(rep[None], count, [every[0]], params, range(1), min(rows, 256), [])
    here, weights = kept
    half = weights[-1].shape[0]
    product = project(here[-half:], weights[-1])
    total = product if total is None else total + product
    here = after(here[:-half], every[near], total, own[0])
    weights = jnp.concatenate(weights[:-1], axis=0) if len(weights) > 2 else weights[0]
    sums, turn = [], here
    for side in (slice(0, features), slice(features, width)):
        here = after(here, turn)
        away = (total[:odd, side] + project(here[:, :odd], weights[:, side])).astype(jnp.bfloat16)
        here = after(here, away)
        stay = (total[odd:, side] + project(here[:, odd:], weights[:, side])).astype(jnp.bfloat16)
        shares, turn = [stay, swap(away, "rep", 1)], stay
        size, k = odd // 2, 2
        while k < replicas:
            sent = sum(v[size : 2 * size].astype(jnp.float32) for v in shares).astype(jnp.bfloat16)
            shares.append(swap(sent, "rep", k))
            size, k = size // 2, 2 * k
        sums.append(shares)
    fresh = combine(sums, pair[None], pairs, block)

    others = [every[k] for k in range(1, replicas)]
    others[0] = after(others[0], sent)
    updated = update(rep[None], count, others, params, range(1, replicas), min(rows, 256), own)
    updated = [from_lane_rows(a, master.shape[0], features) for a in updated]
    return (*updated, fresh)


def solution(mesh):
    in_specs = (
        P(("rep", "shard", "tp"), None),
        P(("rep", "shard")),
        P(("rep", "shard"), None, "tp"),
        P("shard", None, "tp"),
        P("shard", None, "tp"),
        P("shard", None, "tp"),
    )
    out_specs = (
        P("shard", None, "tp"),
        P("shard", None, "tp"),
        P("shard", None, "tp"),
        P(("rep", "shard"), None, "tp"),
    )
    return jax.shard_map(local, mesh=mesh, in_specs=in_specs, out_specs=out_specs, check_vma=False)
```

```python
import functools

import jax
import jax.numpy as jnp
from jax import lax
from jax.experimental import pallas as pl
from jax.experimental.pallas import tpu as pltpu
from jax.sharding import PartitionSpec as P

beta_one = 0.9
beta_two = 0.95
step_count = 20
rate = 0.002
decay = 0.1
epsilon = 1e-08

LANES = 128
GROUPS = 4
LOADS = 2
VMEM_BYTES = 56 * 1024 * 1024

SMEM = pl.BlockSpec(memory_space=pltpu.SMEM)


def adamw(master, moment_one, moment_two, grad):
    first = beta_one * moment_one + (1.0 - beta_one) * grad
    second = beta_two * moment_two + (1.0 - beta_two) * grad * grad
    first_hat = first / (1.0 - beta_one**step_count)
    second_hat = second / (1.0 - beta_two**step_count)
    updated = master - rate * (first_hat / (jnp.sqrt(second_hat) + epsilon) + decay * master)
    return (updated, first, second)


def lane_rows(array):
    rows, two, features = array.shape
    split = array.reshape(rows, two, features // LANES, LANES)
    return split.transpose(0, 2, 1, 3).reshape(rows * two * features // LANES, LANES)


def from_lane_rows(array, rows, features):
    split = array.reshape(rows, features // LANES, 2, LANES)
    return split.transpose(0, 2, 1, 3).reshape(rows, 2, features)


def slots(features):
    return [half * features + tile * LANES for tile in range(features // LANES) for half in range(2)]


def call(kernel, out_shape, flops, moved, **kwargs):
    return pl.pallas_call(
        kernel,
        out_shape=out_shape,
        cost_estimate=pl.CostEstimate(flops=flops, bytes_accessed=moved, transcendentals=0),
        compiler_params=pltpu.CompilerParams(vmem_limit_bytes=VMEM_BYTES),
        **kwargs,
    )


def full(shape):
    return pl.BlockSpec(shape, lambda *_: (0,) * len(shape))


def f32(ref):
    return ref[...].astype(jnp.float32)


def pack(hidden, rep, loads, replicas, rows):
    tokens = hidden.shape[0]
    specs, shapes, orders = [], [], []
    for load in loads:
        for k in range(replicas):
            at = len(orders)
            for start, part, order in load:
                for _ in order:
                    at += 1

                    def index(i, place, at=at, k=k, start=start, part=part):
                        return (0, (place[at] * replicas + (place[0] ^ k)) * (rows // part) + start // part)

                    specs.append(pl.BlockSpec((tokens, part), index))
            shapes.append((sum(part * len(order) for _, part, order in load), tokens))
        orders += [shard for _, _, order in load for shard in order]

    def kernel(place, *refs):
        sources, outs = iter(refs[: len(specs)]), iter(refs[len(specs) :])
        for load in loads:
            for k in range(replicas):
                out, row = next(outs), 0
                for _, part, order in load:
                    for _ in order:
                        out[row : row + part, :] = next(sources)[...].T
                        row += part

    outs = call(
        kernel,
        [jax.ShapeDtypeStruct(shape, hidden.dtype) for shape in shapes],
        0,
        4 * sum(shape[0] * shape[1] for shape in shapes),
        grid_spec=pltpu.PrefetchScalarGridSpec(
            num_scalar_prefetch=1,
            grid=(1,),
            in_specs=specs,
            out_specs=[full(shape) for shape in shapes],
        ),
    )(jnp.stack([rep, *orders]), *[hidden] * len(specs))
    return [outs[i : i + replicas] for i in range(0, len(outs), replicas)]


def mask(cotan, place, pairs):
    block, _, features = cotan.shape
    width, tokens = 2 * features, block // pairs
    per = width // LANES

    def kernel(place, source, out, count, scratch):
        scratch[...] = source[...].astype(jnp.float32)
        count[...] = jnp.full(count.shape, place[0]).astype(jnp.float32)
        for o in range(pairs):
            start = (place[1] ^ o) * tokens
            row = lax.broadcasted_iota(jnp.int32, (tokens, LANES), 0) + start
            for slot, column in enumerate(slots(features)):
                rows = scratch[pl.ds(start * per + slot, tokens, stride=per), :]
                out[o * tokens : (o + 1) * tokens, column : column + LANES] = jnp.where(
                    row < place[0], rows, 0.0
                ).astype(out.dtype)

    return call(
        kernel,
        [jax.ShapeDtypeStruct((block, width), cotan.dtype), jax.ShapeDtypeStruct((8, LANES), jnp.float32)],
        0,
        4 * block * width,
        grid=(1,),
        in_specs=[SMEM, full((block * per, LANES))],
        out_specs=[full((block, width)), full((8, LANES))],
        scratch_shapes=[pltpu.VMEM((block * per, LANES), jnp.float32)],
    )(place, lane_rows(cotan))


def fresh_weights(place, count, shares, params):
    part, width = shares[0][1].block_shape
    per = width // LANES

    def kernel(place, count, *refs):
        sources = refs[: len(shares)]
        master, first, second, weights, grad, scratch = refs[len(shares) :]
        grad[...] = sum(f32(source) for source in sources).astype(grad.dtype)
        scale = 1.0 / count[0:1, 0:1]
        starts = slots(width // 2)
        for slot, start in enumerate(starts):
            scratch[pl.ds(slot, part, stride=per), :] = grad[:, start : start + LANES].astype(jnp.float32)
        updated, _, _ = adamw(master[...], first[...], second[...], scratch[...] * scale)
        scratch[...] = updated
        for slot, start in enumerate(starts):
            weights[:, start : start + LANES] = scratch[pl.ds(slot, part, stride=per), :].astype(weights.dtype)

    param_spec = pl.BlockSpec((part * per, LANES), lambda i, place: (place[0], 0))
    return call(
        kernel,
        [jax.ShapeDtypeStruct((part, width), jnp.bfloat16)] * 2,
        20 * part * width,
        20 * part * width,
        grid_spec=pltpu.PrefetchScalarGridSpec(
            num_scalar_prefetch=1,
            grid=(1,),
            in_specs=[full((8, LANES)), *[spec for _, spec in shares], param_spec, param_spec, param_spec],
            out_specs=[pl.BlockSpec((part, width), lambda i, place: (0, 0))] * 2,
            scratch_shapes=[pltpu.VMEM((part * per, LANES), jnp.float32)],
        ),
    )(place, count, *[a for a, _ in shares], *params)


def update(me, count, grads, params, ks, block, before):
    rows, width = grads[0].shape
    per = width // LANES
    steps = rows // block
    first_k = min(ks)

    def kernel(place, count, *refs):
        sources = refs[: len(grads)]
        master, first, second = refs[len(grads) : len(grads) + 3]
        new_master, new_first, new_second, scratch = refs[-4:]
        scale = 1.0 / count[0:1, 0:1]
        for j, grad in enumerate(sources):

            @pl.when(pl.program_id(0) == j)
            def _(grad=grad):
                for slot, start in enumerate(slots(width // 2)):
                    scratch[pl.ds(slot, block, stride=per), :] = grad[:, start : start + LANES].astype(jnp.float32)

        updated, one, two = adamw(master[...], first[...], second[...], scratch[...] * scale)
        new_master[...] = updated
        new_first[...] = one
        new_second[...] = two

    def grad_spec(j):
        return pl.BlockSpec(
            (block, width), lambda k, i, me: (jnp.where(k == j, i, jnp.where(k < j, 0, steps - 1)), 0)
        )

    param_spec = pl.BlockSpec((block * per, LANES), lambda k, i, me: ((me[0] ^ (k + first_k)) * steps + i, 0))
    size = len(ks) * rows * width
    return call(
        kernel,
        [jax.ShapeDtypeStruct(params[0].shape, jnp.float32)] * 3,
        20 * size,
        26 * size,
        grid_spec=pltpu.PrefetchScalarGridSpec(
            num_scalar_prefetch=1,
            grid=(len(ks), steps),
            in_specs=[full((8, LANES))]
            + [grad_spec(j) for j in range(len(grads))]
            + [param_spec] * 3
            + [pl.BlockSpec(memory_space=pl.ANY)] * len(before),
            out_specs=[param_spec] * 3,
            scratch_shapes=[pltpu.VMEM((block * per, LANES), jnp.float32)],
        ),
        input_output_aliases={2 + len(grads) + 3 + i: i for i in range(len(before))},
    )(me, count, *grads, *params, *before)


def combine(shares, pair, pairs, rows):
    features = shares[0][0].shape[1]
    tokens, per = rows // pairs, 2 * features // LANES
    each = len(shares[0])

    def kernel(pair, *refs):
        out, scratch = refs[-2], refs[-1]
        for o in range(pairs):
            start = (pair[0] ^ o) * tokens
            for slot, column in enumerate(slots(features)):
                half, at = divmod(column, features)
                total = sum(
                    source[o * tokens : (o + 1) * tokens, at : at + LANES].astype(jnp.float32)
                    for source in refs[half * each : (half + 1) * each]
                )
                scratch[pl.ds(start * per + slot, tokens, stride=per), :] = total
        out[...] = scratch[...].astype(out.dtype)

    out = call(
        kernel,
        jax.ShapeDtypeStruct((rows * per, LANES), jnp.bfloat16),
        0,
        16 * rows * features,
        grid=(1,),
        in_specs=[SMEM] + [full((rows, features))] * (2 * each),
        out_specs=full((rows * per, LANES)),
        scratch_shapes=[pltpu.VMEM((rows * per, LANES), jnp.float32)],
    )(pair, *shares[0], *shares[1])
    return from_lane_rows(out, rows, features)


def after(value, *deps):
    return lax.optimization_barrier((value, *deps))[0] if deps else value


def swap(value, axis, k):
    if k == 0:
        return value
    return lax.ppermute(value, axis, [(i, i ^ k) for i in range(lax.axis_size(axis))])


def add(a, b):
    return (a.astype(jnp.float32) + b.astype(jnp.float32)).astype(jnp.bfloat16)


class Line:
    ends_to_inner = [(0, 1), (3, 2)]
    across = [(1, 2), (2, 1)]
    inner_to_ends = [(1, 0), (2, 3)]

    def __init__(self, shard):
        self.end = (shard == 0) | (shard == 3)
        low = shard < 2
        self.order = [jnp.where(low, 3, 0), jnp.where(low, 2, 1), shard ^ 1, shard]

    def send(self, away, soon):
        return add(away, after(lax.ppermute(away, "shard", self.ends_to_inner), *soon))

    def settle(self, far, last, soon):
        part = last.shape[0] // 2
        got = lax.ppermute(far, "shard", self.across)
        near = add(last[:part], after(got, *soon)[:part])
        return [(last, 1), (got, 1), (swap(near, "shard", 1), 0)], near

    def gather(self, own, *waits):
        side = after(jnp.concatenate([swap(own, "shard", 1), own], axis=0), *waits)
        got = lax.ppermute(side, "shard", self.across)
        far = lax.ppermute(got, "shard", self.inner_to_ends)
        return [jnp.where(self.end, far, got), side]


class Halves:
    def __init__(self, shard, shards):
        order, k = [0], shards // 2
        while k:
            order, k = [i + k for i in order] + order, k // 2
        self.shards = shards
        self.order = [shard ^ q for q in order]

    def send(self, away, soon):
        return after(swap(away, "shard", 1), *soon)

    def settle(self, far, last, soon):
        shares, half, k, sent = [last, far], last.shape[0], 2, far
        while k < self.shards:
            sent = sum(v[v.shape[0] - half : v.shape[0] - half // 2].astype(jnp.float32) for v in shares)
            sent, half, k = sent.astype(jnp.bfloat16), half // 2, 2 * k
            shares.append(swap(sent, "shard", k // 2))
        return [(v, v.shape[0] // half - 1) for v in shares], sent

    def gather(self, own, *waits):
        blocks, k = own, self.shards // 2
        while k > 1:
            blocks, k = jnp.concatenate([swap(blocks, "shard", k), blocks], axis=0), k // 2
        return [swap(blocks, "shard", 1), blocks]


def local(hidden_in, lengths, kv_grad_out, master, moment_one, moment_two):
    replicas, shards, pairs = (lax.axis_size(name) for name in ("rep", "shard", "tp"))
    rep, shard, pair = (lax.axis_index(name).astype(jnp.int32) for name in ("rep", "shard", "tp"))
    tokens, depth = hidden_in.shape
    block, _, features = kv_grad_out.shape
    width = 2 * features
    rows = depth // (shards * replicas)
    near = replicas // 2
    parities = [k for k in range(replicas) if k % 2] + [k for k in range(replicas) if not k % 2]
    odd = replicas // 2 * block

    number = max(1, min(GROUPS, rows // LANES))
    part = rows // number
    ways = [Line(shard) if shards == 4 and g < number - 1 else Halves(shard, shards) for g in range(number)]
    groups = [(g * part, part, way.order) for g, way in enumerate(ways)]
    each = max(1, number // LOADS)
    loads = [groups[g : g + each] for g in range(0, number, each)]
    by_rows = (((0,), (0,)), ((), ()))

    count, k = jnp.full((8, LANES), lengths[0]).astype(jnp.float32), near
    count = count + swap(count, "rep", k)
    early, k = count, k // 2
    while k:
        count, k = count + swap(count, "rep", k), k // 2
    k = 1
    while k < shards:
        count, k = count + swap(count, "shard", k), 2 * k
    pieces = pack(hidden_in, rep, loads[:1], replicas, rows)
    cotan, _ = mask(kv_grad_out, jnp.stack([lengths[0], pair]), pairs)
    if len(loads) > 1:
        pieces += pack(hidden_in, after(rep, count), loads[1:], replicas, rows)
    arrived, sides, line = [], [], []

    def travel(n, *waits):
        arrived.append(
            [pieces[n][0]]
            + [swap(after(h, *waits) if k >= near else h, "rep", k) for k, h in enumerate(pieces[n]) if k]
        )
        sides.append([])

    def pair_up(n, ks, *waits):
        for k in ks:
            sent = after(arrived[n][k], *line[-2:-1], *waits)
            sides[n].append([arrived[n][k]] + [swap(sent, "tp", o) for o in range(1, pairs)])
            line.append(sides[n][-1][-1])

    def lay(n):
        return jnp.concatenate([p for k in parities for p in sides[n][k]], axis=1)

    low, high = range(near), range(near, replicas)
    travel(0, early)
    pair_up(0, low)
    pair_up(0, high, cotan)
    ready = [*arrived[0][near:], *line[:near], *(pieces[1] if len(loads) > 1 else [])]
    cotans = {0: cotan, near: swap(after(cotan, *ready), "rep", near)}
    for n in range(1, len(loads)):
        travel(n, *([cotans[near]] if n == 1 else arrived[n - 1][near:]))
        if n == 1:
            pair_up(1, low)
    k = near // 2
    while k:
        for have in list(cotans):
            cotans[have ^ k] = swap(cotans[have], "rep", k)
        k //= 2
    cotans = jnp.concatenate([cotans[k] for k in parities], axis=0)

    params = [lane_rows(a) for a in (master, moment_one, moment_two)]
    steps, summed, grads, fresh, gathered, inputs, last = [], [], [], [], [], [], None

    def project(rows, weights):
        return lax.dot_general(rows, weights, by_rows, preferred_element_type=jnp.float32)

    half = shards // 2 * part
    for n, load in enumerate(loads):
        laid = lay(n)
        if n:
            laid = after(laid, fresh[(n - 1) * each], *steps)
        for inside in range(len(load)):
            g, way = n * each + inside, ways[n * each + inside]
            if last is not None:
                laid = after(laid, last)
            if n + 1 < len(loads) and inside == 1:
                laid = after(laid, line[(n + 1) * replicas])
            if n and inside:
                laid = after(laid, fresh[n * each - 1])
            row = inside * 2 * half
            away = jnp.dot(laid[row : row + half], cotans, preferred_element_type=jnp.float32)
            away = away.astype(jnp.bfloat16)
            laid = after(laid, away)
            last = jnp.dot(laid[row + half : row + 2 * half], cotans, preferred_element_type=jnp.float32)
            last = last.astype(jnp.bfloat16)
            soon, then = [], []
            if not n and inside:
                away = after(away, far)
            if n + 1 < len(loads) and inside:
                soon = arrived[n + 1][near:]
            far = way.send(away, soon)
            if n + 1 < len(loads):
                pair_up(n + 1, range(near + inside, near + inside + 1 if inside < each - 1 else replicas), far)
                then = line[-1:]
            shares, passed = way.settle(far, last, then)
            steps.append(passed)
            summed.append(shares)
        for inside in range(len(load)):
            g = n * each + inside
            inputs.append(laid[inside * 2 * half : (inside + 1) * 2 * half])
            shares = summed[g]
            if n and inside == 0:
                shares = [(after(shares[0][0], steps[-1]), shares[0][1])] + shares[1:]
            if n and inside == 1:
                first = project(inputs[0], jnp.concatenate(gathered[0], axis=0))
                shares = [(after(shares[0][0], first), shares[0][1])] + shares[1:]
            place = (rep * number + g)[None]
            specs = [
                (v, pl.BlockSpec((part, width), lambda i, place, row=row: (row, 0))) for v, row in shares
            ]
            weights, grad = fresh_weights(place, count, specs, params)
            fresh.append(weights)
            grads.append(grad)
            if n + 1 == len(loads) or inside == 0:
                gathered.append(ways[g].gather(weights))
            if n and inside == 0:
                gathered.insert(1, ways[1].gather(fresh[1], steps[2]))

    every = {0: jnp.concatenate(grads, axis=0)}
    k = near
    while k:
        for have in list(every):
            every[have ^ k] = swap(every[have], "rep", k)
        k //= 2

    own = update(rep[None], count, [every[0]], params, range(1), min(rows, 256), [])
    total, ends = None, []
    for g, weights in enumerate(gathered):
        if g < number - each:
            product = first if g == 0 else project(inputs[g], jnp.concatenate(weights, axis=0))
        else:
            product = project(inputs[g][half:], weights[1])
            ends.append((inputs[g][:half], weights[0]))
        total = product if total is None else total + product
    here = after(ends[-1][0], every[near], total, own[0])
    sums, turn = [], here
    for side in (slice(0, features), slice(features, width)):
        here = after(here, turn)
        away, stay = total[:odd, side], total[odd:, side]
        for rows_of, weights in ends[:-1]:
            away = away + project(rows_of[:, :odd], weights[:, side])
        away = (away + project(here[:, :odd], ends[-1][1][:, side])).astype(jnp.bfloat16)
        here = after(here, away)
        for rows_of, weights in ends[:-1]:
            stay = stay + project(rows_of[:, odd:], weights[:, side])
        stay = (stay + project(here[:, odd:], ends[-1][1][:, side])).astype(jnp.bfloat16)
        shares, turn = [stay, swap(away, "rep", 1)], stay
        size, k = odd // 2, 2
        while k < replicas:
            sent = sum(v[size : 2 * size].astype(jnp.float32) for v in shares).astype(jnp.bfloat16)
            shares.append(swap(sent, "rep", k))
            size, k = size // 2, 2 * k
        sums.append(shares)
    fresh = combine(sums, pair[None], pairs, block)

    others = [every[k] for k in range(1, replicas)]
    others[0] = after(others[0], sent)
    updated = update(rep[None], count, others, params, range(1, replicas), min(rows, 256), own)
    updated = [from_lane_rows(a, master.shape[0], features) for a in updated]
    return (*updated, fresh)


def solution(mesh):
    in_specs = (
        P(("rep", "shard", "tp"), None),
        P(("rep", "shard")),
        P(("rep", "shard"), None, "tp"),
        P("shard", None, "tp"),
        P("shard", None, "tp"),
        P("shard", None, "tp"),
    )
    out_specs = (
        P("shard", None, "tp"),
        P("shard", None, "tp"),
        P("shard", None, "tp"),
        P(("rep", "shard"), None, "tp"),
    )
    return jax.shard_map(local, mesh=mesh, in_specs=in_specs, out_specs=out_specs, check_vma=False)
```

```python
import functools

import jax
import jax.numpy as jnp
from jax import lax
from jax.experimental import pallas as pl
from jax.experimental.pallas import tpu as pltpu
from jax.sharding import PartitionSpec as P

beta_one = 0.9
beta_two = 0.95
step_count = 20
rate = 0.002
decay = 0.1
epsilon = 1e-08

LANES = 128
GROUPS = 4
LOADS = 2
VMEM_BYTES = 56 * 1024 * 1024

SMEM = pl.BlockSpec(memory_space=pltpu.SMEM)


def adamw(master, moment_one, moment_two, grad):
    first = beta_one * moment_one + (1.0 - beta_one) * grad
    second = beta_two * moment_two + (1.0 - beta_two) * grad * grad
    first_hat = first / (1.0 - beta_one**step_count)
    second_hat = second / (1.0 - beta_two**step_count)
    updated = master - rate * (first_hat / (jnp.sqrt(second_hat) + epsilon) + decay * master)
    return (updated, first, second)


def lane_rows(array):
    rows, two, features = array.shape
    split = array.reshape(rows, two, features // LANES, LANES)
    return split.transpose(0, 2, 1, 3).reshape(rows * two * features // LANES, LANES)


def from_lane_rows(array, rows, features):
    split = array.reshape(rows, features // LANES, 2, LANES)
    return split.transpose(0, 2, 1, 3).reshape(rows, 2, features)


def slots(features):
    return [half * features + tile * LANES for tile in range(features // LANES) for half in range(2)]


def call(kernel, out_shape, flops, moved, **kwargs):
    return pl.pallas_call(
        kernel,
        out_shape=out_shape,
        cost_estimate=pl.CostEstimate(flops=flops, bytes_accessed=moved, transcendentals=0),
        compiler_params=pltpu.CompilerParams(vmem_limit_bytes=VMEM_BYTES),
        **kwargs,
    )


def full(shape):
    return pl.BlockSpec(shape, lambda *_: (0,) * len(shape))


def f32(ref):
    return ref[...].astype(jnp.float32)


def pack(hidden, rep, loads, replicas, rows):
    tokens = hidden.shape[0]
    specs, shapes, orders = [], [], []
    for load in loads:
        for k in range(replicas):
            at = len(orders)
            for start, part, order in load:
                for _ in order:
                    at += 1

                    def index(i, place, at=at, k=k, start=start, part=part):
                        return (0, (place[at] * replicas + (place[0] ^ k)) * (rows // part) + start // part)

                    specs.append(pl.BlockSpec((tokens, part), index))
            shapes.append((sum(part * len(order) for _, part, order in load), tokens))
        orders += [shard for _, _, order in load for shard in order]

    def kernel(place, *refs):
        sources, outs = iter(refs[: len(specs)]), iter(refs[len(specs) :])
        for load in loads:
            for k in range(replicas):
                out, row = next(outs), 0
                for _, part, order in load:
                    for _ in order:
                        out[row : row + part, :] = next(sources)[...].T
                        row += part

    outs = call(
        kernel,
        [jax.ShapeDtypeStruct(shape, hidden.dtype) for shape in shapes],
        0,
        4 * sum(shape[0] * shape[1] for shape in shapes),
        grid_spec=pltpu.PrefetchScalarGridSpec(
            num_scalar_prefetch=1,
            grid=(1,),
            in_specs=specs,
            out_specs=[full(shape) for shape in shapes],
        ),
    )(jnp.stack([rep, *orders]), *[hidden] * len(specs))
    return [outs[i : i + replicas] for i in range(0, len(outs), replicas)]


def mask(cotan, place, pairs):
    block, _, features = cotan.shape
    width, tokens = 2 * features, block // pairs
    per = width // LANES

    def kernel(place, source, out, count, scratch):
        scratch[...] = source[...].astype(jnp.float32)
        count[...] = jnp.full(count.shape, place[0]).astype(jnp.float32)
        for o in range(pairs):
            start = (place[1] ^ o) * tokens
            row = lax.broadcasted_iota(jnp.int32, (tokens, LANES), 0) + start
            for slot, column in enumerate(slots(features)):
                rows = scratch[pl.ds(start * per + slot, tokens, stride=per), :]
                out[o * tokens : (o + 1) * tokens, column : column + LANES] = jnp.where(
                    row < place[0], rows, 0.0
                ).astype(out.dtype)

    return call(
        kernel,
        [jax.ShapeDtypeStruct((block, width), cotan.dtype), jax.ShapeDtypeStruct((8, LANES), jnp.float32)],
        0,
        4 * block * width,
        grid=(1,),
        in_specs=[SMEM, full((block * per, LANES))],
        out_specs=[full((block, width)), full((8, LANES))],
        scratch_shapes=[pltpu.VMEM((block * per, LANES), jnp.float32)],
    )(place, lane_rows(cotan))


def fresh_weights(place, count, shares, params):
    part, width = shares[0][1].block_shape
    per = width // LANES

    def kernel(place, count, *refs):
        sources = refs[: len(shares)]
        master, first, second, weights, grad, scratch = refs[len(shares) :]
        grad[...] = sum(f32(source) for source in sources).astype(grad.dtype)
        scale = 1.0 / count[0:1, 0:1]
        starts = slots(width // 2)
        for slot, start in enumerate(starts):
            scratch[pl.ds(slot, part, stride=per), :] = grad[:, start : start + LANES].astype(jnp.float32)
        updated, _, _ = adamw(master[...], first[...], second[...], scratch[...] * scale)
        scratch[...] = updated
        for slot, start in enumerate(starts):
            weights[:, start : start + LANES] = scratch[pl.ds(slot, part, stride=per), :].astype(weights.dtype)

    param_spec = pl.BlockSpec((part * per, LANES), lambda i, place: (place[0], 0))
    return call(
        kernel,
        [jax.ShapeDtypeStruct((part, width), jnp.bfloat16)] * 2,
        20 * part * width,
        20 * part * width,
        grid_spec=pltpu.PrefetchScalarGridSpec(
            num_scalar_prefetch=1,
            grid=(1,),
            in_specs=[full((8, LANES)), *[spec for _, spec in shares], param_spec, param_spec, param_spec],
            out_specs=[pl.BlockSpec((part, width), lambda i, place: (0, 0))] * 2,
            scratch_shapes=[pltpu.VMEM((part * per, LANES), jnp.float32)],
        ),
    )(place, count, *[a for a, _ in shares], *params)


def update(me, count, grads, params, ks, block, before):
    rows, width = grads[0].shape
    per = width // LANES
    steps = rows // block
    first_k = min(ks)

    def kernel(place, count, *refs):
        sources = refs[: len(grads)]
        master, first, second = refs[len(grads) : len(grads) + 3]
        new_master, new_first, new_second, scratch = refs[-4:]
        scale = 1.0 / count[0:1, 0:1]
        for j, grad in enumerate(sources):

            @pl.when(pl.program_id(0) == j)
            def _(grad=grad):
                for slot, start in enumerate(slots(width // 2)):
                    scratch[pl.ds(slot, block, stride=per), :] = grad[:, start : start + LANES].astype(jnp.float32)

        updated, one, two = adamw(master[...], first[...], second[...], scratch[...] * scale)
        new_master[...] = updated
        new_first[...] = one
        new_second[...] = two

    def grad_spec(j):
        return pl.BlockSpec(
            (block, width), lambda k, i, me: (jnp.where(k == j, i, jnp.where(k < j, 0, steps - 1)), 0)
        )

    param_spec = pl.BlockSpec((block * per, LANES), lambda k, i, me: ((me[0] ^ (k + first_k)) * steps + i, 0))
    size = len(ks) * rows * width
    return call(
        kernel,
        [jax.ShapeDtypeStruct(params[0].shape, jnp.float32)] * 3,
        20 * size,
        26 * size,
        grid_spec=pltpu.PrefetchScalarGridSpec(
            num_scalar_prefetch=1,
            grid=(len(ks), steps),
            in_specs=[full((8, LANES))]
            + [grad_spec(j) for j in range(len(grads))]
            + [param_spec] * 3
            + [pl.BlockSpec(memory_space=pl.ANY)] * len(before),
            out_specs=[param_spec] * 3,
            scratch_shapes=[pltpu.VMEM((block * per, LANES), jnp.float32)],
        ),
        input_output_aliases={2 + len(grads) + 3 + i: i for i in range(len(before))},
    )(me, count, *grads, *params, *before)


def combine(shares, pair, pairs, rows):
    features = shares[0][0].shape[1]
    tokens, per = rows // pairs, 2 * features // LANES
    each = len(shares[0])

    def kernel(pair, *refs):
        out, scratch = refs[-2], refs[-1]
        for o in range(pairs):
            start = (pair[0] ^ o) * tokens
            for slot, column in enumerate(slots(features)):
                half, at = divmod(column, features)
                total = sum(
                    source[o * tokens : (o + 1) * tokens, at : at + LANES].astype(jnp.float32)
                    for source in refs[half * each : (half + 1) * each]
                )
                scratch[pl.ds(start * per + slot, tokens, stride=per), :] = total
        out[...] = scratch[...].astype(out.dtype)

    out = call(
        kernel,
        jax.ShapeDtypeStruct((rows * per, LANES), jnp.bfloat16),
        0,
        16 * rows * features,
        grid=(1,),
        in_specs=[SMEM] + [full((rows, features))] * (2 * each),
        out_specs=full((rows * per, LANES)),
        scratch_shapes=[pltpu.VMEM((rows * per, LANES), jnp.float32)],
    )(pair, *shares[0], *shares[1])
    return from_lane_rows(out, rows, features)


def after(value, *deps):
    return lax.optimization_barrier((value, *deps))[0] if deps else value


def swap(value, axis, k):
    if k == 0:
        return value
    return lax.ppermute(value, axis, [(i, i ^ k) for i in range(lax.axis_size(axis))])


def add(a, b):
    return (a.astype(jnp.float32) + b.astype(jnp.float32)).astype(jnp.bfloat16)


class Line:
    ends_to_inner = [(0, 1), (3, 2)]
    across = [(1, 2), (2, 1)]
    inner_to_ends = [(1, 0), (2, 3)]

    away_first = True

    def __init__(self, shard):
        self.end = (shard == 0) | (shard == 3)
        low = shard < 2
        self.order = [jnp.where(low, 3, 0), jnp.where(low, 2, 1), shard ^ 1, shard]

    def send(self, away, soon):
        return add(away, after(lax.ppermute(away, "shard", self.ends_to_inner), *soon))

    def settle(self, far, last, soon):
        part = last.shape[0] // 2
        got = lax.ppermute(far, "shard", self.across)
        near = add(last[:part], after(got, *soon)[:part])
        return [(last, 1), (got, 1), (swap(near, "shard", 1), 0)], near

    def gather(self, own, *waits):
        side = after(jnp.concatenate([swap(own, "shard", 1), own], axis=0), *waits)
        got = lax.ppermute(side, "shard", self.across)
        far = lax.ppermute(got, "shard", self.inner_to_ends)
        return [jnp.where(self.end, far, got), side]


class Halves:
    away_first = False

    def __init__(self, shard, shards):
        order, k = [0], shards // 2
        while k:
            order, k = [i + k for i in order] + order, k // 2
        self.shards = shards
        self.order = [shard ^ q for q in order[shards // 2 :] + order[: shards // 2]]

    def send(self, away, soon):
        return after(swap(away, "shard", 1), *soon)

    def settle(self, far, last, soon):
        shares, half, k, sent = [last, far], last.shape[0], 2, far
        while k < self.shards:
            sent = sum(v[v.shape[0] - half : v.shape[0] - half // 2].astype(jnp.float32) for v in shares)
            sent, half, k = sent.astype(jnp.bfloat16), half // 2, 2 * k
            shares.append(swap(sent, "shard", k // 2))
        return [(v, v.shape[0] // half - 1) for v in shares], sent

    def gather(self, own, *waits):
        blocks, k = own, self.shards // 2
        while k > 1:
            blocks, k = jnp.concatenate([swap(blocks, "shard", k), blocks], axis=0), k // 2
        return [swap(blocks, "shard", 1), blocks]


def local(hidden_in, lengths, kv_grad_out, master, moment_one, moment_two):
    replicas, shards, pairs = (lax.axis_size(name) for name in ("rep", "shard", "tp"))
    rep, shard, pair = (lax.axis_index(name).astype(jnp.int32) for name in ("rep", "shard", "tp"))
    tokens, depth = hidden_in.shape
    block, _, features = kv_grad_out.shape
    width = 2 * features
    rows = depth // (shards * replicas)
    near = replicas // 2
    parities = [k for k in range(replicas) if k % 2] + [k for k in range(replicas) if not k % 2]
    odd = replicas // 2 * block

    number = max(1, min(GROUPS, rows // LANES))
    part = rows // number
    ways = [Line(shard) if shards == 4 and g < number - 1 else Halves(shard, shards) for g in range(number)]
    groups = [(g * part, part, way.order) for g, way in enumerate(ways)]
    each = max(1, number // LOADS)
    loads = [groups[g : g + each] for g in range(0, number, each)]
    by_rows = (((0,), (0,)), ((), ()))

    count, k = jnp.full((8, LANES), lengths[0]).astype(jnp.float32), near
    count = count + swap(count, "rep", k)
    early, k = count, k // 2
    while k:
        count, k = count + swap(count, "rep", k), k // 2
    k = 1
    while k < shards:
        count, k = count + swap(count, "shard", k), 2 * k
    pieces = pack(hidden_in, rep, loads[:1], replicas, rows)
    cotan, _ = mask(kv_grad_out, jnp.stack([lengths[0], pair]), pairs)
    if len(loads) > 1:
        pieces += pack(hidden_in, after(rep, count), loads[1:], replicas, rows)
    arrived, sides, line = [], [], []

    def travel(n, *waits):
        arrived.append(
            [pieces[n][0]]
            + [swap(after(h, *waits) if k >= near else h, "rep", k) for k, h in enumerate(pieces[n]) if k]
        )
        sides.append([])

    def pair_up(n, ks, *waits):
        for k in ks:
            sent = after(arrived[n][k], *line[-2:-1], *waits)
            sides[n].append([arrived[n][k]] + [swap(sent, "tp", o) for o in range(1, pairs)])
            line.append(sides[n][-1][-1])

    def lay(n):
        return jnp.concatenate([p for k in parities for p in sides[n][k]], axis=1)

    low, high = range(near), range(near, replicas)
    travel(0, early)
    pair_up(0, low)
    pair_up(0, high, cotan)
    ready = [*arrived[0][near:], *line[:near], *(pieces[1] if len(loads) > 1 else [])]
    cotans = {0: cotan, near: swap(after(cotan, *ready), "rep", near)}
    for n in range(1, len(loads)):
        travel(n, *([cotans[near]] if n == 1 else arrived[n - 1][near:]))
        if n == 1:
            pair_up(1, low)
    k = near // 2
    while k:
        for have in list(cotans):
            cotans[have ^ k] = swap(cotans[have], "rep", k)
        k //= 2
    cotans = jnp.concatenate([cotans[k] for k in parities], axis=0)

    params = [lane_rows(a) for a in (master, moment_one, moment_two)]
    steps, summed, grads, fresh, gathered, places, inputs, last = [], [], [], [], [], [], [], None

    def project(rows, weights):
        return lax.dot_general(rows, weights, by_rows, preferred_element_type=jnp.float32)

    half = shards // 2 * part
    for n, load in enumerate(loads):
        laid = lay(n)
        if n:
            laid = after(laid, fresh[(n - 1) * each], *steps)
        for inside in range(len(load)):
            g, way = n * each + inside, ways[n * each + inside]
            if last is not None:
                laid = after(laid, last)
            if n + 1 < len(loads) and inside == 1:
                laid = after(laid, line[(n + 1) * replicas])
            row = inside * 2 * half
            far_row, near_row = (row, row + half) if way.away_first else (row + half, row)
            places.append((far_row, near_row))
            away = jnp.dot(laid[far_row : far_row + half], cotans, preferred_element_type=jnp.float32)
            away = away.astype(jnp.bfloat16)
            laid = after(laid, away)
            last = jnp.dot(laid[near_row : near_row + half], cotans, preferred_element_type=jnp.float32)
            last = last.astype(jnp.bfloat16)
            soon, then = [], []
            if not n and inside:
                away = after(away, far)
            if n + 1 < len(loads) and inside:
                soon = arrived[n + 1][near:]
            far = way.send(away, soon)
            if n + 1 < len(loads):
                pair_up(n + 1, range(near + inside, near + inside + 1 if inside < each - 1 else replicas), far)
                then = line[-1:]
            shares, passed = way.settle(far, last, then)
            steps.append(passed)
            summed.append(shares)
        for inside in range(len(load)):
            g = n * each + inside
            shares = summed[g]
            if n and inside == 0:
                shares = [(after(shares[0][0], steps[-1], *fresh[each - 1 : each]), shares[0][1])] + shares[1:]
            place = (rep * number + g)[None]
            specs = [
                (v, pl.BlockSpec((part, width), lambda i, place, row=row: (row, 0))) for v, row in shares
            ]
            weights, grad = fresh_weights(place, count, specs, params)
            fresh.append(weights)
            grads.append(grad)
            if n + 1 == len(loads) or inside == 0:
                gathered.append(ways[g].gather(weights))
            if n and inside == 0:
                gathered.insert(1, ways[1].gather(fresh[1], steps[2]))
        inputs.append(laid)

    every = {0: jnp.concatenate(grads, axis=0)}
    k = near
    while k:
        for have in list(every):
            every[have ^ k] = swap(every[have], "rep", k)
        k //= 2

    own = update(rep[None], count, [every[0]], params, range(1), min(rows, 256), [])
    total = None
    if len(loads) > 1:
        total = project(inputs[0], jnp.concatenate([w for g in range(each) for w in gathered[g]], axis=0))
    held = range(number - each, number)
    begin = min(places[g][1] for g in held)
    assert all(places[g][1] == begin + i * half for i, g in enumerate(held))
    product = project(
        inputs[-1][begin : begin + each * half], jnp.concatenate([gathered[g][1] for g in held], axis=0)
    )
    total = product if total is None else total + product
    here = after(inputs[-1], every[near], total, own[0])
    sums, turn = [], here
    for side in (slice(0, features), slice(features, width)):
        here = after(here, turn)
        ends = []
        for columns in (slice(0, odd), slice(odd, 2 * odd)):
            end = total[columns, side]
            for g in held:
                row = places[g][0]
                end = end + project(here[row : row + half, columns], gathered[g][0][:, side])
            ends.append(end.astype(jnp.bfloat16))
            here = after(here, ends[0])
        away, stay = ends
        shares, turn = [stay, swap(away, "rep", 1)], stay
        size, k = odd // 2, 2
        while k < replicas:
            sent = sum(v[size : 2 * size].astype(jnp.float32) for v in shares).astype(jnp.bfloat16)
            shares.append(swap(sent, "rep", k))
            size, k = size // 2, 2 * k
        sums.append(shares)
    fresh = combine(sums, pair[None], pairs, block)

    others = [every[k] for k in range(1, replicas)]
    others[0] = after(others[0], sent)
    updated = update(rep[None], count, others, params, range(1, replicas), min(rows, 256), own)
    updated = [from_lane_rows(a, master.shape[0], features) for a in updated]
    return (*updated, fresh)


def solution(mesh):
    in_specs = (
        P(("rep", "shard", "tp"), None),
        P(("rep", "shard")),
        P(("rep", "shard"), None, "tp"),
        P("shard", None, "tp"),
        P("shard", None, "tp"),
        P("shard", None, "tp"),
    )
    out_specs = (
        P("shard", None, "tp"),
        P("shard", None, "tp"),
        P("shard", None, "tp"),
        P(("rep", "shard"), None, "tp"),
    )
    return jax.shard_map(local, mesh=mesh, in_specs=in_specs, out_specs=out_specs, check_vma=False)
```

```python
import functools

import jax
import jax.numpy as jnp
from jax import lax
from jax.experimental import pallas as pl
from jax.experimental.pallas import tpu as pltpu
from jax.sharding import PartitionSpec as P

beta_one = 0.9
beta_two = 0.95
step_count = 20
rate = 0.002
decay = 0.1
epsilon = 1e-08

LANES = 128
GROUPS = 4
LOADS = 2
VMEM_BYTES = 56 * 1024 * 1024

SMEM = pl.BlockSpec(memory_space=pltpu.SMEM)


def adamw(master, moment_one, moment_two, grad):
    first = beta_one * moment_one + (1.0 - beta_one) * grad
    second = beta_two * moment_two + (1.0 - beta_two) * grad * grad
    first_hat = first / (1.0 - beta_one**step_count)
    second_hat = second / (1.0 - beta_two**step_count)
    updated = master - rate * (first_hat / (jnp.sqrt(second_hat) + epsilon) + decay * master)
    return (updated, first, second)


def lane_rows(array):
    rows, two, features = array.shape
    split = array.reshape(rows, two, features // LANES, LANES)
    return split.transpose(0, 2, 1, 3).reshape(rows * two * features // LANES, LANES)


def from_lane_rows(array, rows, features):
    split = array.reshape(rows, features // LANES, 2, LANES)
    return split.transpose(0, 2, 1, 3).reshape(rows, 2, features)


def slots(features):
    return [half * features + tile * LANES for tile in range(features // LANES) for half in range(2)]


def call(kernel, out_shape, flops, moved, **kwargs):
    return pl.pallas_call(
        kernel,
        out_shape=out_shape,
        cost_estimate=pl.CostEstimate(flops=flops, bytes_accessed=moved, transcendentals=0),
        compiler_params=pltpu.CompilerParams(vmem_limit_bytes=VMEM_BYTES),
        **kwargs,
    )


def full(shape):
    return pl.BlockSpec(shape, lambda *_: (0,) * len(shape))


def f32(ref):
    return ref[...].astype(jnp.float32)


def pack(hidden, rep, loads, replicas, rows):
    tokens = hidden.shape[0]
    specs, shapes, orders = [], [], []
    for load in loads:
        for k in range(replicas):
            at = len(orders)
            for start, part, order in load:
                for _ in order:
                    at += 1

                    def index(i, place, at=at, k=k, start=start, part=part):
                        return (0, (place[at] * replicas + (place[0] ^ k)) * (rows // part) + start // part)

                    specs.append(pl.BlockSpec((tokens, part), index))
            shapes.append((sum(part * len(order) for _, part, order in load), tokens))
        orders += [shard for _, _, order in load for shard in order]

    def kernel(place, *refs):
        sources, outs = iter(refs[: len(specs)]), iter(refs[len(specs) :])
        for load in loads:
            for k in range(replicas):
                out, row = next(outs), 0
                for _, part, order in load:
                    for _ in order:
                        out[row : row + part, :] = next(sources)[...].T
                        row += part

    outs = call(
        kernel,
        [jax.ShapeDtypeStruct(shape, hidden.dtype) for shape in shapes],
        0,
        4 * sum(shape[0] * shape[1] for shape in shapes),
        grid_spec=pltpu.PrefetchScalarGridSpec(
            num_scalar_prefetch=1,
            grid=(1,),
            in_specs=specs,
            out_specs=[full(shape) for shape in shapes],
        ),
    )(jnp.stack([rep, *orders]), *[hidden] * len(specs))
    return [outs[i : i + replicas] for i in range(0, len(outs), replicas)]


def mask(cotan, place, pairs):
    block, _, features = cotan.shape
    width, tokens = 2 * features, block // pairs
    per = width // LANES

    def kernel(place, source, out, count, scratch):
        scratch[...] = source[...].astype(jnp.float32)
        count[...] = jnp.full(count.shape, place[0]).astype(jnp.float32)
        for o in range(pairs):
            start = (place[1] ^ o) * tokens
            row = lax.broadcasted_iota(jnp.int32, (tokens, LANES), 0) + start
            for slot, column in enumerate(slots(features)):
                rows = scratch[pl.ds(start * per + slot, tokens, stride=per), :]
                out[o * tokens : (o + 1) * tokens, column : column + LANES] = jnp.where(
                    row < place[0], rows, 0.0
                ).astype(out.dtype)

    return call(
        kernel,
        [jax.ShapeDtypeStruct((block, width), cotan.dtype), jax.ShapeDtypeStruct((8, LANES), jnp.float32)],
        0,
        4 * block * width,
        grid=(1,),
        in_specs=[SMEM, full((block * per, LANES))],
        out_specs=[full((block, width)), full((8, LANES))],
        scratch_shapes=[pltpu.VMEM((block * per, LANES), jnp.float32)],
    )(place, lane_rows(cotan))


def fresh_weights(place, count, shares, params):
    part, width = shares[0][1].block_shape
    per = width // LANES

    def kernel(place, count, *refs):
        sources = refs[: len(shares)]
        master, first, second, weights, grad, scratch = refs[len(shares) :]
        grad[...] = sum(f32(source) for source in sources).astype(grad.dtype)
        scale = 1.0 / count[0:1, 0:1]
        starts = slots(width // 2)
        for slot, start in enumerate(starts):
            scratch[pl.ds(slot, part, stride=per), :] = grad[:, start : start + LANES].astype(jnp.float32)
        updated, _, _ = adamw(master[...], first[...], second[...], scratch[...] * scale)
        scratch[...] = updated
        for slot, start in enumerate(starts):
            weights[:, start : start + LANES] = scratch[pl.ds(slot, part, stride=per), :].astype(weights.dtype)

    param_spec = pl.BlockSpec((part * per, LANES), lambda i, place: (place[0], 0))
    return call(
        kernel,
        [jax.ShapeDtypeStruct((part, width), jnp.bfloat16)] * 2,
        20 * part * width,
        20 * part * width,
        grid_spec=pltpu.PrefetchScalarGridSpec(
            num_scalar_prefetch=1,
            grid=(1,),
            in_specs=[full((8, LANES)), *[spec for _, spec in shares], param_spec, param_spec, param_spec],
            out_specs=[pl.BlockSpec((part, width), lambda i, place: (0, 0))] * 2,
            scratch_shapes=[pltpu.VMEM((part * per, LANES), jnp.float32)],
        ),
    )(place, count, *[a for a, _ in shares], *params)


def update(me, count, grads, params, ks, block, before):
    rows, width = grads[0].shape
    per = width // LANES
    steps = rows // block
    first_k = min(ks)

    def kernel(place, count, *refs):
        sources = refs[: len(grads)]
        master, first, second = refs[len(grads) : len(grads) + 3]
        new_master, new_first, new_second, scratch = refs[-4:]
        scale = 1.0 / count[0:1, 0:1]
        for j, grad in enumerate(sources):

            @pl.when(pl.program_id(0) == j)
            def _(grad=grad):
                for slot, start in enumerate(slots(width // 2)):
                    scratch[pl.ds(slot, block, stride=per), :] = grad[:, start : start + LANES].astype(jnp.float32)

        updated, one, two = adamw(master[...], first[...], second[...], scratch[...] * scale)
        new_master[...] = updated
        new_first[...] = one
        new_second[...] = two

    def grad_spec(j):
        return pl.BlockSpec(
            (block, width), lambda k, i, me: (jnp.where(k == j, i, jnp.where(k < j, 0, steps - 1)), 0)
        )

    param_spec = pl.BlockSpec((block * per, LANES), lambda k, i, me: ((me[0] ^ (k + first_k)) * steps + i, 0))
    size = len(ks) * rows * width
    return call(
        kernel,
        [jax.ShapeDtypeStruct(params[0].shape, jnp.float32)] * 3,
        20 * size,
        26 * size,
        grid_spec=pltpu.PrefetchScalarGridSpec(
            num_scalar_prefetch=1,
            grid=(len(ks), steps),
            in_specs=[full((8, LANES))]
            + [grad_spec(j) for j in range(len(grads))]
            + [param_spec] * 3
            + [pl.BlockSpec(memory_space=pl.ANY)] * len(before),
            out_specs=[param_spec] * 3,
            scratch_shapes=[pltpu.VMEM((block * per, LANES), jnp.float32)],
        ),
        input_output_aliases={2 + len(grads) + 3 + i: i for i in range(len(before))},
    )(me, count, *grads, *params, *before)


def combine(shares, pair, pairs, rows):
    features = shares[0][0].shape[1]
    tokens, per = rows // pairs, 2 * features // LANES
    each = len(shares[0])

    def kernel(pair, *refs):
        out, scratch = refs[-2], refs[-1]
        for o in range(pairs):
            start = (pair[0] ^ o) * tokens
            for slot, column in enumerate(slots(features)):
                half, at = divmod(column, features)
                total = sum(
                    source[o * tokens : (o + 1) * tokens, at : at + LANES].astype(jnp.float32)
                    for source in refs[half * each : (half + 1) * each]
                )
                scratch[pl.ds(start * per + slot, tokens, stride=per), :] = total
        out[...] = scratch[...].astype(out.dtype)

    out = call(
        kernel,
        jax.ShapeDtypeStruct((rows * per, LANES), jnp.bfloat16),
        0,
        16 * rows * features,
        grid=(1,),
        in_specs=[SMEM] + [full((rows, features))] * (2 * each),
        out_specs=full((rows * per, LANES)),
        scratch_shapes=[pltpu.VMEM((rows * per, LANES), jnp.float32)],
    )(pair, *shares[0], *shares[1])
    return from_lane_rows(out, rows, features)


def after(value, *deps):
    return lax.optimization_barrier((value, *deps))[0] if deps else value


def swap(value, axis, k):
    if k == 0:
        return value
    return lax.ppermute(value, axis, [(i, i ^ k) for i in range(lax.axis_size(axis))])


def add(a, b):
    return (a.astype(jnp.float32) + b.astype(jnp.float32)).astype(jnp.bfloat16)


class Line:
    ends_to_inner = [(0, 1), (3, 2)]
    across = [(1, 2), (2, 1)]
    inner_to_ends = [(1, 0), (2, 3)]

    def __init__(self, shard, away_first):
        self.away_first = away_first
        self.end = (shard == 0) | (shard == 3)
        low = shard < 2
        away, near = [jnp.where(low, 3, 0), jnp.where(low, 2, 1)], [shard ^ 1, shard]
        self.order = away + near if away_first else near + away

    def send(self, away, soon):
        return add(away, after(lax.ppermute(away, "shard", self.ends_to_inner), *soon))

    def settle(self, far, last, soon):
        part = last.shape[0] // 2
        got = lax.ppermute(far, "shard", self.across)
        near = add(last[:part], after(got, *soon)[:part])
        return [(last, 1), (got, 1), (swap(near, "shard", 1), 0)], near

    def gather(self, own, *waits):
        side = after(jnp.concatenate([swap(own, "shard", 1), own], axis=0), *waits)
        got = lax.ppermute(side, "shard", self.across)
        far = lax.ppermute(got, "shard", self.inner_to_ends)
        return [jnp.where(self.end, far, got), side]


class Halves:
    away_first = False

    def __init__(self, shard, shards):
        order, k = [0], shards // 2
        while k:
            order, k = [i + k for i in order] + order, k // 2
        self.shards = shards
        self.order = [shard ^ q for q in order[shards // 2 :] + order[: shards // 2]]

    def send(self, away, soon):
        return after(swap(away, "shard", 1), *soon)

    def settle(self, far, last, soon):
        shares, half, k, sent = [last, far], last.shape[0], 2, far
        while k < self.shards:
            sent = sum(v[v.shape[0] - half : v.shape[0] - half // 2].astype(jnp.float32) for v in shares)
            sent, half, k = sent.astype(jnp.bfloat16), half // 2, 2 * k
            shares.append(swap(sent, "shard", k // 2))
        return [(v, v.shape[0] // half - 1) for v in shares], sent

    def gather(self, own, *waits):
        blocks, k = own, self.shards // 2
        while k > 1:
            blocks, k = jnp.concatenate([swap(blocks, "shard", k), blocks], axis=0), k // 2
        return [swap(blocks, "shard", 1), blocks]


def local(hidden_in, lengths, kv_grad_out, master, moment_one, moment_two):
    replicas, shards, pairs = (lax.axis_size(name) for name in ("rep", "shard", "tp"))
    rep, shard, pair = (lax.axis_index(name).astype(jnp.int32) for name in ("rep", "shard", "tp"))
    tokens, depth = hidden_in.shape
    block, _, features = kv_grad_out.shape
    width = 2 * features
    rows = depth // (shards * replicas)
    near = replicas // 2
    parities = [k for k in range(replicas) if k % 2] + [k for k in range(replicas) if not k % 2]
    odd = replicas // 2 * block

    number = max(1, min(GROUPS, rows // LANES))
    part = rows // number
    ways = [Line(shard, g + 1 < number) if shards == 4 else Halves(shard, shards) for g in range(number)]
    groups = [(g * part, part, way.order) for g, way in enumerate(ways)]
    each = max(1, number // LOADS)
    loads = [groups[g : g + each] for g in range(0, number, each)]
    by_rows = (((0,), (0,)), ((), ()))

    count, k = jnp.full((8, LANES), lengths[0]).astype(jnp.float32), near
    count = count + swap(count, "rep", k)
    early, k = count, k // 2
    while k:
        count, k = count + swap(count, "rep", k), k // 2
    k = 1
    while k < shards:
        count, k = count + swap(count, "shard", k), 2 * k
    pieces = pack(hidden_in, rep, loads[:1], replicas, rows)
    cotan, _ = mask(kv_grad_out, jnp.stack([lengths[0], pair]), pairs)
    if len(loads) > 1:
        pieces += pack(hidden_in, after(rep, count), loads[1:], replicas, rows)
    arrived, sides, line = [], [], []

    def travel(n, *waits):
        arrived.append(
            [pieces[n][0]]
            + [swap(after(h, *waits) if k >= near else h, "rep", k) for k, h in enumerate(pieces[n]) if k]
        )
        sides.append([])

    def pair_up(n, ks, *waits):
        for k in ks:
            sent = after(arrived[n][k], *line[-2:-1], *waits)
            sides[n].append([arrived[n][k]] + [swap(sent, "tp", o) for o in range(1, pairs)])
            line.append(sides[n][-1][-1])

    def lay(n):
        return jnp.concatenate([p for k in parities for p in sides[n][k]], axis=1)

    low, high = range(near), range(near, replicas)
    travel(0, early)
    pair_up(0, low)
    pair_up(0, high, cotan)
    ready = [*arrived[0][near:], *line[:near], *(pieces[1] if len(loads) > 1 else [])]
    cotans = {0: cotan, near: swap(after(cotan, *ready), "rep", near)}
    for n in range(1, len(loads)):
        travel(n, *([cotans[near]] if n == 1 else arrived[n - 1][near:]))
        if n == 1:
            pair_up(1, low)
    k = near // 2
    while k:
        for have in list(cotans):
            cotans[have ^ k] = swap(cotans[have], "rep", k)
        k //= 2
    cotans = jnp.concatenate([cotans[k] for k in parities], axis=0)

    params = [lane_rows(a) for a in (master, moment_one, moment_two)]
    steps, summed, grads, fresh, gathered, places, inputs, last = [], [], [], [], [], [], [], None

    def project(rows, weights):
        return lax.dot_general(rows, weights, by_rows, preferred_element_type=jnp.float32)

    half = shards // 2 * part
    for n, load in enumerate(loads):
        laid = lay(n)
        if n:
            laid = after(laid, fresh[(n - 1) * each], *steps)
        for inside in range(len(load)):
            g, way = n * each + inside, ways[n * each + inside]
            if last is not None:
                laid = after(laid, last)
            if n + 1 < len(loads) and inside == 1:
                laid = after(laid, line[(n + 1) * replicas])
            row = inside * 2 * half
            far_row, near_row = (row, row + half) if way.away_first else (row + half, row)
            places.append((far_row, near_row))
            away = jnp.dot(laid[far_row : far_row + half], cotans, preferred_element_type=jnp.float32)
            away = away.astype(jnp.bfloat16)
            laid = after(laid, away)
            last = jnp.dot(laid[near_row : near_row + half], cotans, preferred_element_type=jnp.float32)
            last = last.astype(jnp.bfloat16)
            soon, then = [], []
            if inside:
                away = after(away, far)
                soon = [steps[-1]]
            elif n:
                soon = fresh[each - 1 : each]
            if n + 1 < len(loads) and inside:
                soon = soon + arrived[n + 1][near:] + line[-1:]
            far = way.send(away, soon)
            if n + 1 < len(loads):
                pair_up(n + 1, range(near + inside, near + inside + 1 if inside < each - 1 else replicas), far)
                then = line[-1:] if inside else []
            shares, passed = way.settle(far, last, then)
            steps.append(passed)
            summed.append(shares)
        for inside in range(len(load)):
            g = n * each + inside
            shares = summed[g]
            if n and inside == 0:
                shares = [(after(shares[0][0], steps[-1], gathered[0][0]), shares[0][1])] + shares[1:]
            place = (rep * number + g)[None]
            specs = [
                (v, pl.BlockSpec((part, width), lambda i, place, row=row: (row, 0))) for v, row in shares
            ]
            weights, grad = fresh_weights(place, count, specs, params)
            fresh.append(weights)
            grads.append(grad)
            if n + 1 == len(loads) or inside == 0:
                gathered.append(ways[g].gather(weights))
            if n and inside == 0:
                gathered.insert(1, ways[1].gather(fresh[1], steps[-1]))
        inputs.append(laid)

    every = {0: jnp.concatenate(grads, axis=0)}
    k = near
    while k:
        for have in list(every):
            every[have ^ k] = swap(every[have], "rep", k)
        k //= 2

    own = update(rep[None], count, [every[0]], params, range(1), min(rows, 256), [])
    total = None
    if len(loads) > 1:
        total = project(inputs[0], jnp.concatenate([w for g in range(each) for w in gathered[g]], axis=0))
    held = range(number - each, number)
    begin = min(places[g][1] for g in held)
    assert all(places[g][1] == begin + i * half for i, g in enumerate(held))
    product = project(
        inputs[-1][begin : begin + each * half], jnp.concatenate([gathered[g][1] for g in held], axis=0)
    )
    total = product if total is None else total + product
    here = after(inputs[-1], every[near], total, own[0])
    sums, turn = [], here
    for side in (slice(0, features), slice(features, width)):
        here = after(here, turn)
        ends = []
        for columns in (slice(0, odd), slice(odd, 2 * odd)):
            end = total[columns, side]
            for g in held:
                row = places[g][0]
                end = end + project(here[row : row + half, columns], gathered[g][0][:, side])
            ends.append(end.astype(jnp.bfloat16))
            here = after(here, ends[0])
        away, stay = ends
        shares, turn = [stay, swap(away, "rep", 1)], stay
        size, k = odd // 2, 2
        while k < replicas:
            sent = sum(v[size : 2 * size].astype(jnp.float32) for v in shares).astype(jnp.bfloat16)
            shares.append(swap(sent, "rep", k))
            size, k = size // 2, 2 * k
        sums.append(shares)
    fresh = combine(sums, pair[None], pairs, block)

    others = [every[k] for k in range(1, replicas)]
    others[0] = after(others[0], sent)
    updated = update(rep[None], count, others, params, range(1, replicas), min(rows, 256), own)
    updated = [from_lane_rows(a, master.shape[0], features) for a in updated]
    return (*updated, fresh)


def solution(mesh):
    in_specs = (
        P(("rep", "shard", "tp"), None),
        P(("rep", "shard")),
        P(("rep", "shard"), None, "tp"),
        P("shard", None, "tp"),
        P("shard", None, "tp"),
        P("shard", None, "tp"),
    )
    out_specs = (
        P("shard", None, "tp"),
        P("shard", None, "tp"),
        P("shard", None, "tp"),
        P(("rep", "shard"), None, "tp"),
    )
    return jax.shard_map(local, mesh=mesh, in_specs=in_specs, out_specs=out_specs, check_vma=False)
```

```python
import functools

import jax
import jax.numpy as jnp
from jax import lax
from jax.experimental import pallas as pl
from jax.experimental.pallas import tpu as pltpu
from jax.sharding import PartitionSpec as P

beta_one = 0.9
beta_two = 0.95
step_count = 20
rate = 0.002
decay = 0.1
epsilon = 1e-08

LANES = 128
GROUPS = 4
LOADS = 2
VMEM_BYTES = 56 * 1024 * 1024

SMEM = pl.BlockSpec(memory_space=pltpu.SMEM)


def adamw(master, moment_one, moment_two, grad):
    first = beta_one * moment_one + (1.0 - beta_one) * grad
    second = beta_two * moment_two + (1.0 - beta_two) * grad * grad
    first_hat = first / (1.0 - beta_one**step_count)
    second_hat = second / (1.0 - beta_two**step_count)
    updated = master - rate * (first_hat / (jnp.sqrt(second_hat) + epsilon) + decay * master)
    return (updated, first, second)


def lane_rows(array):
    rows, two, features = array.shape
    split = array.reshape(rows, two, features // LANES, LANES)
    return split.transpose(0, 2, 1, 3).reshape(rows * two * features // LANES, LANES)


def from_lane_rows(array, rows, features):
    split = array.reshape(rows, features // LANES, 2, LANES)
    return split.transpose(0, 2, 1, 3).reshape(rows, 2, features)


def slots(features):
    return [half * features + tile * LANES for tile in range(features // LANES) for half in range(2)]


def call(kernel, out_shape, flops, moved, **kwargs):
    return pl.pallas_call(
        kernel,
        out_shape=out_shape,
        cost_estimate=pl.CostEstimate(flops=flops, bytes_accessed=moved, transcendentals=0),
        compiler_params=pltpu.CompilerParams(vmem_limit_bytes=VMEM_BYTES),
        **kwargs,
    )


def full(shape):
    return pl.BlockSpec(shape, lambda *_: (0,) * len(shape))


def f32(ref):
    return ref[...].astype(jnp.float32)


def pack(hidden, rep, loads, replicas, rows):
    tokens = hidden.shape[0]
    specs, shapes, orders = [], [], []
    for load in loads:
        for k in range(replicas):
            at = len(orders)
            for start, part, order in load:
                for _ in order:
                    at += 1

                    def index(i, place, at=at, k=k, start=start, part=part):
                        return (0, (place[at] * replicas + (place[0] ^ k)) * (rows // part) + start // part)

                    specs.append(pl.BlockSpec((tokens, part), index))
            shapes.append((sum(part * len(order) for _, part, order in load), tokens))
        orders += [shard for _, _, order in load for shard in order]

    def kernel(place, *refs):
        sources, outs = iter(refs[: len(specs)]), iter(refs[len(specs) :])
        for load in loads:
            for k in range(replicas):
                out, row = next(outs), 0
                for _, part, order in load:
                    for _ in order:
                        out[row : row + part, :] = next(sources)[...].T
                        row += part

    outs = call(
        kernel,
        [jax.ShapeDtypeStruct(shape, hidden.dtype) for shape in shapes],
        0,
        4 * sum(shape[0] * shape[1] for shape in shapes),
        grid_spec=pltpu.PrefetchScalarGridSpec(
            num_scalar_prefetch=1,
            grid=(1,),
            in_specs=specs,
            out_specs=[full(shape) for shape in shapes],
        ),
    )(jnp.stack([rep, *orders]), *[hidden] * len(specs))
    return [outs[i : i + replicas] for i in range(0, len(outs), replicas)]


def mask(cotan, place, pairs):
    block, _, features = cotan.shape
    width, tokens = 2 * features, block // pairs
    per = width // LANES

    def kernel(place, source, out, count, scratch):
        scratch[...] = source[...].astype(jnp.float32)
        count[...] = jnp.full(count.shape, place[0]).astype(jnp.float32)
        for o in range(pairs):
            start = (place[1] ^ o) * tokens
            row = lax.broadcasted_iota(jnp.int32, (tokens, LANES), 0) + start
            for slot, column in enumerate(slots(features)):
                rows = scratch[pl.ds(start * per + slot, tokens, stride=per), :]
                out[o * tokens : (o + 1) * tokens, column : column + LANES] = jnp.where(
                    row < place[0], rows, 0.0
                ).astype(out.dtype)

    return call(
        kernel,
        [jax.ShapeDtypeStruct((block, width), cotan.dtype), jax.ShapeDtypeStruct((8, LANES), jnp.float32)],
        0,
        4 * block * width,
        grid=(1,),
        in_specs=[SMEM, full((block * per, LANES))],
        out_specs=[full((block, width)), full((8, LANES))],
        scratch_shapes=[pltpu.VMEM((block * per, LANES), jnp.float32)],
    )(place, lane_rows(cotan))


def fresh_weights(place, count, shares, params):
    part, width = shares[0][1].block_shape
    per = width // LANES

    def kernel(place, count, *refs):
        sources = refs[: len(shares)]
        master, first, second, weights, grad, scratch = refs[len(shares) :]
        grad[...] = sum(f32(source) for source in sources).astype(grad.dtype)
        scale = 1.0 / count[0:1, 0:1]
        starts = slots(width // 2)
        for slot, start in enumerate(starts):
            scratch[pl.ds(slot, part, stride=per), :] = grad[:, start : start + LANES].astype(jnp.float32)
        updated, _, _ = adamw(master[...], first[...], second[...], scratch[...] * scale)
        scratch[...] = updated
        for slot, start in enumerate(starts):
            weights[:, start : start + LANES] = scratch[pl.ds(slot, part, stride=per), :].astype(weights.dtype)

    param_spec = pl.BlockSpec((part * per, LANES), lambda i, place: (place[0], 0))
    return call(
        kernel,
        [jax.ShapeDtypeStruct((part, width), jnp.bfloat16)] * 2,
        20 * part * width,
        20 * part * width,
        grid_spec=pltpu.PrefetchScalarGridSpec(
            num_scalar_prefetch=1,
            grid=(1,),
            in_specs=[full((8, LANES)), *[spec for _, spec in shares], param_spec, param_spec, param_spec],
            out_specs=[pl.BlockSpec((part, width), lambda i, place: (0, 0))] * 2,
            scratch_shapes=[pltpu.VMEM((part * per, LANES), jnp.float32)],
        ),
    )(place, count, *[a for a, _ in shares], *params)


def update(me, count, grads, params, ks, block, before):
    rows, width = grads[0].shape
    per = width // LANES
    steps = rows // block
    first_k = min(ks)

    def kernel(place, count, *refs):
        sources = refs[: len(grads)]
        master, first, second = refs[len(grads) : len(grads) + 3]
        new_master, new_first, new_second, scratch = refs[-4:]
        scale = 1.0 / count[0:1, 0:1]
        for j, grad in enumerate(sources):

            @pl.when(pl.program_id(0) == j)
            def _(grad=grad):
                for slot, start in enumerate(slots(width // 2)):
                    scratch[pl.ds(slot, block, stride=per), :] = grad[:, start : start + LANES].astype(jnp.float32)

        updated, one, two = adamw(master[...], first[...], second[...], scratch[...] * scale)
        new_master[...] = updated
        new_first[...] = one
        new_second[...] = two

    def grad_spec(j):
        return pl.BlockSpec(
            (block, width), lambda k, i, me: (jnp.where(k == j, i, jnp.where(k < j, 0, steps - 1)), 0)
        )

    param_spec = pl.BlockSpec((block * per, LANES), lambda k, i, me: ((me[0] ^ (k + first_k)) * steps + i, 0))
    size = len(ks) * rows * width
    return call(
        kernel,
        [jax.ShapeDtypeStruct(params[0].shape, jnp.float32)] * 3,
        20 * size,
        26 * size,
        grid_spec=pltpu.PrefetchScalarGridSpec(
            num_scalar_prefetch=1,
            grid=(len(ks), steps),
            in_specs=[full((8, LANES))]
            + [grad_spec(j) for j in range(len(grads))]
            + [param_spec] * 3
            + [pl.BlockSpec(memory_space=pl.ANY)] * len(before),
            out_specs=[param_spec] * 3,
            scratch_shapes=[pltpu.VMEM((block * per, LANES), jnp.float32)],
        ),
        input_output_aliases={2 + len(grads) + 3 + i: i for i in range(len(before))},
    )(me, count, *grads, *params, *before)


def combine(shares, pair, pairs, rows):
    features = shares[0][0].shape[1]
    tokens, per = rows // pairs, 2 * features // LANES
    each = len(shares[0])

    def kernel(pair, *refs):
        out, scratch = refs[-2], refs[-1]
        for o in range(pairs):
            start = (pair[0] ^ o) * tokens
            for slot, column in enumerate(slots(features)):
                half, at = divmod(column, features)
                total = sum(
                    source[o * tokens : (o + 1) * tokens, at : at + LANES].astype(jnp.float32)
                    for source in refs[half * each : (half + 1) * each]
                )
                scratch[pl.ds(start * per + slot, tokens, stride=per), :] = total
        out[...] = scratch[...].astype(out.dtype)

    out = call(
        kernel,
        jax.ShapeDtypeStruct((rows * per, LANES), jnp.bfloat16),
        0,
        16 * rows * features,
        grid=(1,),
        in_specs=[SMEM] + [full((rows, features))] * (2 * each),
        out_specs=full((rows * per, LANES)),
        scratch_shapes=[pltpu.VMEM((rows * per, LANES), jnp.float32)],
    )(pair, *shares[0], *shares[1])
    return from_lane_rows(out, rows, features)


def after(value, *deps):
    return lax.optimization_barrier((value, *deps))[0] if deps else value


def swap(value, axis, k):
    if k == 0:
        return value
    return lax.ppermute(value, axis, [(i, i ^ k) for i in range(lax.axis_size(axis))])


def add(a, b):
    return (a.astype(jnp.float32) + b.astype(jnp.float32)).astype(jnp.bfloat16)


class Line:
    ends_to_inner = [(0, 1), (3, 2)]
    across = [(1, 2), (2, 1)]
    inner_to_ends = [(1, 0), (2, 3)]

    away_first = True

    def __init__(self, shard):
        self.end = (shard == 0) | (shard == 3)
        low = shard < 2
        self.order = [jnp.where(low, 3, 0), jnp.where(low, 2, 1), shard ^ 1, shard]

    def send(self, away, soon):
        return add(away, after(lax.ppermute(away, "shard", self.ends_to_inner), *soon))

    def settle(self, far, last, soon):
        part = last.shape[0] // 2
        got = lax.ppermute(far, "shard", self.across)
        near = add(last[:part], after(got, *soon)[:part])
        return [(last, 1), (got, 1), (swap(near, "shard", 1), 0)], near

    def gather(self, own, *waits):
        side = after(jnp.concatenate([swap(own, "shard", 1), own], axis=0), *waits)
        got = lax.ppermute(side, "shard", self.across)
        far = lax.ppermute(got, "shard", self.inner_to_ends)
        return [jnp.where(self.end, far, got), side]


class Halves:
    away_first = False

    def __init__(self, shard, shards):
        order, k = [0], shards // 2
        while k:
            order, k = [i + k for i in order] + order, k // 2
        self.shards = shards
        self.order = [shard ^ q for q in order[shards // 2 :] + order[: shards // 2]]

    def send(self, away, soon):
        return after(swap(away, "shard", 1), *soon)

    def settle(self, far, last, soon):
        shares, half, k, sent = [last, far], last.shape[0], 2, far
        while k < self.shards:
            sent = sum(v[v.shape[0] - half : v.shape[0] - half // 2].astype(jnp.float32) for v in shares)
            sent, half, k = sent.astype(jnp.bfloat16), half // 2, 2 * k
            shares.append(swap(sent, "shard", k // 2))
        return [(v, v.shape[0] // half - 1) for v in shares], sent

    def gather(self, own, *waits):
        blocks, k = own, self.shards // 2
        while k > 1:
            blocks, k = jnp.concatenate([swap(blocks, "shard", k), blocks], axis=0), k // 2
        blocks = after(blocks, *waits)
        return [swap(blocks, "shard", 1), blocks]


def local(hidden_in, lengths, kv_grad_out, master, moment_one, moment_two):
    replicas, shards, pairs = (lax.axis_size(name) for name in ("rep", "shard", "tp"))
    rep, shard, pair = (lax.axis_index(name).astype(jnp.int32) for name in ("rep", "shard", "tp"))
    tokens, depth = hidden_in.shape
    block, _, features = kv_grad_out.shape
    width = 2 * features
    rows = depth // (shards * replicas)
    near = replicas // 2
    parities = [k for k in range(replicas) if k % 2] + [k for k in range(replicas) if not k % 2]
    odd = replicas // 2 * block

    number = max(1, min(GROUPS, rows // LANES))
    part = rows // number
    ways = [Line(shard) if shards == 4 and g < number - 1 else Halves(shard, shards) for g in range(number)]
    groups = [(g * part, part, way.order) for g, way in enumerate(ways)]
    each = max(1, number // LOADS)
    loads = [groups[g : g + each] for g in range(0, number, each)]
    by_rows = (((0,), (0,)), ((), ()))

    count, k = jnp.full((8, LANES), lengths[0]).astype(jnp.float32), near
    count = count + swap(count, "rep", k)
    early, k = count, k // 2
    while k:
        count, k = count + swap(count, "rep", k), k // 2
    k = 1
    while k < shards:
        count, k = count + swap(count, "shard", k), 2 * k
    pieces = pack(hidden_in, rep, loads[:1], replicas, rows)
    cotan, _ = mask(kv_grad_out, jnp.stack([lengths[0], pair]), pairs)
    if len(loads) > 1:
        pieces += pack(hidden_in, after(rep, count), loads[1:], replicas, rows)
    arrived, sides, line = [], [], []

    def travel(n, *waits):
        arrived.append(
            [pieces[n][0]]
            + [swap(after(h, *waits) if k >= near else h, "rep", k) for k, h in enumerate(pieces[n]) if k]
        )
        sides.append([])

    def pair_up(n, ks, *waits):
        for k in ks:
            sent = after(arrived[n][k], *line[-2:-1], *waits)
            sides[n].append([arrived[n][k]] + [swap(sent, "tp", o) for o in range(1, pairs)])
            line.append(sides[n][-1][-1])

    def lay(n):
        return jnp.concatenate([p for k in parities for p in sides[n][k]], axis=1)

    low, high = range(near), range(near, replicas)
    travel(0, early)
    pair_up(0, low)
    pair_up(0, high, cotan)
    ready = [*arrived[0][near:], *line[:near], *(pieces[1] if len(loads) > 1 else [])]
    cotans = {0: cotan, near: swap(after(cotan, *ready), "rep", near)}
    for n in range(1, len(loads)):
        travel(n, *([cotans[near]] if n == 1 else arrived[n - 1][near:]))
        if n == 1:
            pair_up(1, low)
    k = near // 2
    while k:
        for have in list(cotans):
            cotans[have ^ k] = swap(cotans[have], "rep", k)
        k //= 2
    cotans = jnp.concatenate([cotans[k] for k in parities], axis=0)

    params = [lane_rows(a) for a in (master, moment_one, moment_two)]
    steps, summed, grads, fresh, gathered, places, inputs, last = [], [], [], [], [], [], [], None

    def project(rows, weights):
        return lax.dot_general(rows, weights, by_rows, preferred_element_type=jnp.float32)

    half = shards // 2 * part
    for n, load in enumerate(loads):
        laid = lay(n)
        if n:
            laid = after(laid, fresh[(n - 1) * each], *steps)
        for inside in range(len(load)):
            g, way = n * each + inside, ways[n * each + inside]
            if last is not None:
                laid = after(laid, last)
            if n + 1 < len(loads) and inside == 1:
                laid = after(laid, line[(n + 1) * replicas])
            row = inside * 2 * half
            far_row, near_row = (row, row + half) if way.away_first else (row + half, row)
            places.append((far_row, near_row))
            away = jnp.dot(laid[far_row : far_row + half], cotans, preferred_element_type=jnp.float32)
            away = away.astype(jnp.bfloat16)
            laid = after(laid, away)
            last = jnp.dot(laid[near_row : near_row + half], cotans, preferred_element_type=jnp.float32)
            last = last.astype(jnp.bfloat16)
            soon, then = [], []
            if not n and inside:
                away = after(away, far)
            if n + 1 < len(loads) and inside:
                soon = arrived[n + 1][near:]
            far = way.send(away, soon)
            if n + 1 < len(loads):
                if inside == 0:
                    begun = far
                pair_up(n + 1, range(near + inside, near + inside + 1 if inside < each - 1 else replicas), begun)
                then = line[-1:]
            shares, passed = way.settle(far, last, then)
            steps.append(passed)
            summed.append(shares)
        for inside in range(len(load)):
            g = n * each + inside
            shares = summed[g]
            if n and inside == 0:
                shares = [(after(shares[0][0], steps[-1], *fresh[each - 1 : each]), shares[0][1])] + shares[1:]
            if n and inside:
                shares = [(after(shares[0][0], steps[-2]), shares[0][1])] + shares[1:]
            place = (rep * number + g)[None]
            specs = [
                (v, pl.BlockSpec((part, width), lambda i, place, row=row: (row, 0))) for v, row in shares
            ]
            weights, grad = fresh_weights(place, count, specs, params)
            fresh.append(weights)
            grads.append(grad)
            if n + 1 == len(loads) or inside == 0:
                gathered.append(ways[g].gather(weights, *(fresh[-2:-1] if n and inside else [])))
            if n and inside == 0:
                gathered.insert(1, ways[1].gather(fresh[1], steps[2]))
        inputs.append(laid)

    every = {0: jnp.concatenate(grads, axis=0)}
    k = near
    while k:
        for have in list(every):
            every[have ^ k] = swap(every[have], "rep", k)
        k //= 2

    own = update(rep[None], count, [every[0]], params, range(1), min(rows, 256), [])
    total = None
    if len(loads) > 1:
        total = project(inputs[0], jnp.concatenate([w for g in range(each) for w in gathered[g]], axis=0))
    held = range(number - each, number)
    begin = min(places[g][1] for g in held)
    assert all(places[g][1] == begin + i * half for i, g in enumerate(held))
    product = project(
        inputs[-1][begin : begin + each * half], jnp.concatenate([gathered[g][1] for g in held], axis=0)
    )
    total = product if total is None else total + product
    here = after(inputs[-1], every[near], total, own[0])
    sums, turn = [], here
    for side in (slice(0, features), slice(features, width)):
        here = after(here, turn)
        ends = []
        for columns in (slice(0, odd), slice(odd, 2 * odd)):
            end = total[columns, side]
            for g in held:
                row = places[g][0]
                end = end + project(here[row : row + half, columns], gathered[g][0][:, side])
            ends.append(end.astype(jnp.bfloat16))
            here = after(here, ends[0])
        away, stay = ends
        shares, turn = [stay, swap(away, "rep", 1)], stay
        size, k = odd // 2, 2
        while k < replicas:
            sent = sum(v[size : 2 * size].astype(jnp.float32) for v in shares).astype(jnp.bfloat16)
            shares.append(swap(sent, "rep", k))
            size, k = size // 2, 2 * k
        sums.append(shares)
    fresh = combine(sums, pair[None], pairs, block)

    others = [every[k] for k in range(1, replicas)]
    others[0] = after(others[0], sent)
    updated = update(rep[None], count, others, params, range(1, replicas), min(rows, 256), own)
    updated = [from_lane_rows(a, master.shape[0], features) for a in updated]
    return (*updated, fresh)


def solution(mesh):
    in_specs = (
        P(("rep", "shard", "tp"), None),
        P(("rep", "shard")),
        P(("rep", "shard"), None, "tp"),
        P("shard", None, "tp"),
        P("shard", None, "tp"),
        P("shard", None, "tp"),
    )
    out_specs = (
        P("shard", None, "tp"),
        P("shard", None, "tp"),
        P("shard", None, "tp"),
        P(("rep", "shard"), None, "tp"),
    )
    return jax.shard_map(local, mesh=mesh, in_specs=in_specs, out_specs=out_specs, check_vma=False)
```

```python
import functools

import jax
import jax.numpy as jnp
from jax import lax
from jax.experimental import pallas as pl
from jax.experimental.pallas import tpu as pltpu
from jax.sharding import PartitionSpec as P

beta_one = 0.9
beta_two = 0.95
step_count = 20
rate = 0.002
decay = 0.1
epsilon = 1e-08

LANES = 128
GROUPS = 4
LOADS = 2
VMEM_BYTES = 56 * 1024 * 1024

SMEM = pl.BlockSpec(memory_space=pltpu.SMEM)


def adamw(master, moment_one, moment_two, grad):
    first = beta_one * moment_one + (1.0 - beta_one) * grad
    second = beta_two * moment_two + (1.0 - beta_two) * grad * grad
    first_hat = first / (1.0 - beta_one**step_count)
    second_hat = second / (1.0 - beta_two**step_count)
    updated = master - rate * (first_hat / (jnp.sqrt(second_hat) + epsilon) + decay * master)
    return (updated, first, second)


def lane_rows(array):
    rows, two, features = array.shape
    split = array.reshape(rows, two, features // LANES, LANES)
    return split.transpose(0, 2, 1, 3).reshape(rows * two * features // LANES, LANES)


def from_lane_rows(array, rows, features):
    split = array.reshape(rows, features // LANES, 2, LANES)
    return split.transpose(0, 2, 1, 3).reshape(rows, 2, features)


def slots(features):
    return [half * features + tile * LANES for tile in range(features // LANES) for half in range(2)]


def call(kernel, out_shape, flops, moved, **kwargs):
    return pl.pallas_call(
        kernel,
        out_shape=out_shape,
        cost_estimate=pl.CostEstimate(flops=flops, bytes_accessed=moved, transcendentals=0),
        compiler_params=pltpu.CompilerParams(vmem_limit_bytes=VMEM_BYTES),
        **kwargs,
    )


def full(shape):
    return pl.BlockSpec(shape, lambda *_: (0,) * len(shape))


def f32(ref):
    return ref[...].astype(jnp.float32)


def pack(hidden, rep, loads, replicas, rows):
    tokens = hidden.shape[0]
    specs, shapes, orders = [], [], []
    for load in loads:
        for k in range(replicas):
            at = len(orders)
            for start, part, order in load:
                for _ in order:
                    at += 1

                    def index(i, place, at=at, k=k, start=start, part=part):
                        return (0, (place[at] * replicas + (place[0] ^ k)) * (rows // part) + start // part)

                    specs.append(pl.BlockSpec((tokens, part), index))
            shapes.append((sum(part * len(order) for _, part, order in load), tokens))
        orders += [shard for _, _, order in load for shard in order]

    def kernel(place, *refs):
        sources, outs = iter(refs[: len(specs)]), iter(refs[len(specs) :])
        for load in loads:
            for k in range(replicas):
                out, row = next(outs), 0
                for _, part, order in load:
                    for _ in order:
                        out[row : row + part, :] = next(sources)[...].T
                        row += part

    outs = call(
        kernel,
        [jax.ShapeDtypeStruct(shape, hidden.dtype) for shape in shapes],
        0,
        4 * sum(shape[0] * shape[1] for shape in shapes),
        grid_spec=pltpu.PrefetchScalarGridSpec(
            num_scalar_prefetch=1,
            grid=(1,),
            in_specs=specs,
            out_specs=[full(shape) for shape in shapes],
        ),
    )(jnp.stack([rep, *orders]), *[hidden] * len(specs))
    return [outs[i : i + replicas] for i in range(0, len(outs), replicas)]


def mask(cotan, place, pairs):
    block, _, features = cotan.shape
    width, tokens = 2 * features, block // pairs
    per = width // LANES

    def kernel(place, source, out, count, scratch):
        scratch[...] = source[...].astype(jnp.float32)
        count[...] = jnp.full(count.shape, place[0]).astype(jnp.float32)
        for o in range(pairs):
            start = (place[1] ^ o) * tokens
            row = lax.broadcasted_iota(jnp.int32, (tokens, LANES), 0) + start
            for slot, column in enumerate(slots(features)):
                rows = scratch[pl.ds(start * per + slot, tokens, stride=per), :]
                out[o * tokens : (o + 1) * tokens, column : column + LANES] = jnp.where(
                    row < place[0], rows, 0.0
                ).astype(out.dtype)

    return call(
        kernel,
        [jax.ShapeDtypeStruct((block, width), cotan.dtype), jax.ShapeDtypeStruct((8, LANES), jnp.float32)],
        0,
        4 * block * width,
        grid=(1,),
        in_specs=[SMEM, full((block * per, LANES))],
        out_specs=[full((block, width)), full((8, LANES))],
        scratch_shapes=[pltpu.VMEM((block * per, LANES), jnp.float32)],
    )(place, lane_rows(cotan))


def fresh_weights(place, count, shares, params):
    part, width = shares[0][1].block_shape
    per = width // LANES

    def kernel(place, count, *refs):
        sources = refs[: len(shares)]
        master, first, second, weights, grad, scratch = refs[len(shares) :]
        grad[...] = sum(f32(source) for source in sources).astype(grad.dtype)
        scale = 1.0 / count[0:1, 0:1]
        starts = slots(width // 2)
        for slot, start in enumerate(starts):
            scratch[pl.ds(slot, part, stride=per), :] = grad[:, start : start + LANES].astype(jnp.float32)
        updated, _, _ = adamw(master[...], first[...], second[...], scratch[...] * scale)
        scratch[...] = updated
        for slot, start in enumerate(starts):
            weights[:, start : start + LANES] = scratch[pl.ds(slot, part, stride=per), :].astype(weights.dtype)

    param_spec = pl.BlockSpec((part * per, LANES), lambda i, place: (place[0], 0))
    return call(
        kernel,
        [jax.ShapeDtypeStruct((part, width), jnp.bfloat16)] * 2,
        20 * part * width,
        20 * part * width,
        grid_spec=pltpu.PrefetchScalarGridSpec(
            num_scalar_prefetch=1,
            grid=(1,),
            in_specs=[full((8, LANES)), *[spec for _, spec in shares], param_spec, param_spec, param_spec],
            out_specs=[pl.BlockSpec((part, width), lambda i, place: (0, 0))] * 2,
            scratch_shapes=[pltpu.VMEM((part * per, LANES), jnp.float32)],
        ),
    )(place, count, *[a for a, _ in shares], *params)


def update(me, count, grads, params, ks, block, before):
    rows, width = grads[0].shape
    per = width // LANES
    steps = rows // block
    first_k = min(ks)

    def kernel(place, count, *refs):
        sources = refs[: len(grads)]
        master, first, second = refs[len(grads) : len(grads) + 3]
        new_master, new_first, new_second, scratch = refs[-4:]
        scale = 1.0 / count[0:1, 0:1]
        for j, grad in enumerate(sources):

            @pl.when(pl.program_id(0) == j)
            def _(grad=grad):
                for slot, start in enumerate(slots(width // 2)):
                    scratch[pl.ds(slot, block, stride=per), :] = grad[:, start : start + LANES].astype(jnp.float32)

        updated, one, two = adamw(master[...], first[...], second[...], scratch[...] * scale)
        new_master[...] = updated
        new_first[...] = one
        new_second[...] = two

    def grad_spec(j):
        return pl.BlockSpec(
            (block, width), lambda k, i, me: (jnp.where(k == j, i, jnp.where(k < j, 0, steps - 1)), 0)
        )

    param_spec = pl.BlockSpec((block * per, LANES), lambda k, i, me: ((me[0] ^ (k + first_k)) * steps + i, 0))
    size = len(ks) * rows * width
    return call(
        kernel,
        [jax.ShapeDtypeStruct(params[0].shape, jnp.float32)] * 3,
        20 * size,
        26 * size,
        grid_spec=pltpu.PrefetchScalarGridSpec(
            num_scalar_prefetch=1,
            grid=(len(ks), steps),
            in_specs=[full((8, LANES))]
            + [grad_spec(j) for j in range(len(grads))]
            + [param_spec] * 3
            + [pl.BlockSpec(memory_space=pl.ANY)] * len(before),
            out_specs=[param_spec] * 3,
            scratch_shapes=[pltpu.VMEM((block * per, LANES), jnp.float32)],
        ),
        input_output_aliases={2 + len(grads) + 3 + i: i for i in range(len(before))},
    )(me, count, *grads, *params, *before)


def combine(shares, pair, pairs, rows):
    features = shares[0][0].shape[1]
    tokens, per = rows // pairs, 2 * features // LANES
    each = len(shares[0])

    def kernel(pair, *refs):
        out, scratch = refs[-2], refs[-1]
        for o in range(pairs):
            start = (pair[0] ^ o) * tokens
            for slot, column in enumerate(slots(features)):
                half, at = divmod(column, features)
                total = sum(
                    source[o * tokens : (o + 1) * tokens, at : at + LANES].astype(jnp.float32)
                    for source in refs[half * each : (half + 1) * each]
                )
                scratch[pl.ds(start * per + slot, tokens, stride=per), :] = total
        out[...] = scratch[...].astype(out.dtype)

    out = call(
        kernel,
        jax.ShapeDtypeStruct((rows * per, LANES), jnp.bfloat16),
        0,
        16 * rows * features,
        grid=(1,),
        in_specs=[SMEM] + [full((rows, features))] * (2 * each),
        out_specs=full((rows * per, LANES)),
        scratch_shapes=[pltpu.VMEM((rows * per, LANES), jnp.float32)],
    )(pair, *shares[0], *shares[1])
    return from_lane_rows(out, rows, features)


def after(value, *deps):
    return lax.optimization_barrier((value, *deps))[0] if deps else value


def swap(value, axis, k):
    if k == 0:
        return value
    return lax.ppermute(value, axis, [(i, i ^ k) for i in range(lax.axis_size(axis))])


def add(a, b):
    return (a.astype(jnp.float32) + b.astype(jnp.float32)).astype(jnp.bfloat16)


class Line:
    ends_to_inner = [(0, 1), (3, 2)]
    across = [(1, 2), (2, 1)]
    inner_to_ends = [(1, 0), (2, 3)]

    away_first = True

    def __init__(self, shard):
        self.end = (shard == 0) | (shard == 3)
        low = shard < 2
        self.order = [jnp.where(low, 3, 0), jnp.where(low, 2, 1), shard ^ 1, shard]

    def send(self, away, soon):
        return add(away, after(lax.ppermute(away, "shard", self.ends_to_inner), *soon))

    def settle(self, far, last, soon):
        part = last.shape[0] // 2
        got = lax.ppermute(far, "shard", self.across)
        near = add(last[:part], after(got, *soon)[:part])
        return [(last, 1), (got, 1), (swap(near, "shard", 1), 0)], near

    def gather(self, own, *waits):
        side = after(jnp.concatenate([swap(own, "shard", 1), own], axis=0), *waits)
        got = lax.ppermute(side, "shard", self.across)
        far = lax.ppermute(got, "shard", self.inner_to_ends)
        return [jnp.where(self.end, far, got), side]


class Halves:
    away_first = False

    def __init__(self, shard, shards):
        order, k = [0], shards // 2
        while k:
            order, k = [i + k for i in order] + order, k // 2
        self.shards = shards
        self.order = [shard ^ q for q in order[shards // 2 :] + order[: shards // 2]]

    def send(self, away, soon):
        return after(swap(away, "shard", 1), *soon)

    def settle(self, far, last, soon):
        shares, half, k, sent = [last, far], last.shape[0], 2, far
        while k < self.shards:
            sent = sum(v[v.shape[0] - half : v.shape[0] - half // 2].astype(jnp.float32) for v in shares)
            sent, half, k = sent.astype(jnp.bfloat16), half // 2, 2 * k
            shares.append(swap(sent, "shard", k // 2))
        return [(v, v.shape[0] // half - 1) for v in shares], sent

    def gather(self, own, *waits):
        blocks, k = own, self.shards // 2
        while k > 1:
            blocks, k = jnp.concatenate([swap(blocks, "shard", k), blocks], axis=0), k // 2
        return [swap(blocks, "shard", 1), blocks]


def local(hidden_in, lengths, kv_grad_out, master, moment_one, moment_two):
    replicas, shards, pairs = (lax.axis_size(name) for name in ("rep", "shard", "tp"))
    rep, shard, pair = (lax.axis_index(name).astype(jnp.int32) for name in ("rep", "shard", "tp"))
    tokens, depth = hidden_in.shape
    block, _, features = kv_grad_out.shape
    width = 2 * features
    rows = depth // (shards * replicas)
    near = replicas // 2
    parities = [k for k in range(replicas) if k % 2] + [k for k in range(replicas) if not k % 2]
    odd = replicas // 2 * block

    number = max(1, min(GROUPS, rows // LANES))
    part = rows // number
    ways = [Line(shard) if shards == 4 and g < number - 1 else Halves(shard, shards) for g in range(number)]
    groups = [(g * part, part, way.order) for g, way in enumerate(ways)]
    each = max(1, number // LOADS)
    loads = [groups[g : g + each] for g in range(0, number, each)]
    by_rows = (((0,), (0,)), ((), ()))

    count, k = jnp.full((8, LANES), lengths[0]).astype(jnp.float32), near
    count = count + swap(count, "rep", k)
    early, k = count, k // 2
    while k:
        count, k = count + swap(count, "rep", k), k // 2
    k = 1
    while k < shards:
        count, k = count + swap(count, "shard", k), 2 * k
    pieces = pack(hidden_in, rep, loads[:1], replicas, rows)
    cotan, _ = mask(kv_grad_out, jnp.stack([lengths[0], pair]), pairs)
    if len(loads) > 1:
        pieces += pack(hidden_in, after(rep, count), loads[1:], replicas, rows)
    arrived, sides, line = [], [], []

    def travel(n, *waits):
        arrived.append(
            [pieces[n][0]]
            + [swap(after(h, *waits) if k >= near else h, "rep", k) for k, h in enumerate(pieces[n]) if k]
        )
        sides.append([])

    def pair_up(n, ks, *waits):
        for k in ks:
            sent = after(arrived[n][k], *line[-2:-1], *waits)
            sides[n].append([arrived[n][k]] + [swap(sent, "tp", o) for o in range(1, pairs)])
            line.append(sides[n][-1][-1])

    def lay(n):
        return jnp.concatenate([p for k in parities for p in sides[n][k]], axis=1)

    low, high = range(near), range(near, replicas)
    travel(0, early)
    pair_up(0, low)
    pair_up(0, high, cotan)
    ready = [*arrived[0][near:], *line[:near], *(pieces[1] if len(loads) > 1 else [])]
    cotans = {0: cotan, near: swap(after(cotan, *ready), "rep", near)}
    for n in range(1, len(loads)):
        travel(n, *([cotans[near]] if n == 1 else arrived[n - 1][near:]))
        if n == 1:
            pair_up(1, low)
    k = near // 2
    while k:
        for have in list(cotans):
            cotans[have ^ k] = swap(cotans[have], "rep", k)
        k //= 2
    cotans = jnp.concatenate([cotans[k] for k in parities], axis=0)

    params = [lane_rows(a) for a in (master, moment_one, moment_two)]
    steps, summed, grads, fresh, gathered, places, inputs, last = [], [], [], [], [], [], [], None

    def project(rows, weights):
        return lax.dot_general(rows, weights, by_rows, preferred_element_type=jnp.float32)

    half = shards // 2 * part
    for n, load in enumerate(loads):
        laid = lay(n)
        if n:
            laid = after(laid, fresh[(n - 1) * each], *steps)
        for inside in range(len(load)):
            g, way = n * each + inside, ways[n * each + inside]
            if last is not None:
                laid = after(laid, last)
            if n + 1 < len(loads) and inside == 1:
                laid = after(laid, line[(n + 1) * replicas])
            row = inside * 2 * half
            far_row, near_row = (row, row + half) if way.away_first else (row + half, row)
            places.append((far_row, near_row))
            away = jnp.dot(laid[far_row : far_row + half], cotans, preferred_element_type=jnp.float32)
            away = away.astype(jnp.bfloat16)
            laid = after(laid, away)
            last = jnp.dot(laid[near_row : near_row + half], cotans, preferred_element_type=jnp.float32)
            last = last.astype(jnp.bfloat16)
            soon, then = [], []
            if not n and inside:
                away = after(away, far)
            if n + 1 < len(loads) and inside:
                soon = arrived[n + 1][near:]
            far = way.send(away, soon)
            if n + 1 < len(loads):
                pair_up(n + 1, range(near + inside, near + inside + 1 if inside < each - 1 else replicas), far)
                then = line[-1:]
            shares, passed = way.settle(far, last, then)
            steps.append(passed)
            summed.append(shares)
        for inside in range(len(load)):
            g = n * each + inside
            shares = summed[g]
            if n and inside == 0:
                shares = [(after(shares[0][0], steps[-1], *fresh[each - 1 : each]), shares[0][1])] + shares[1:]
            if not n and inside:
                shares = [(after(shares[0][0], gathered[0][0]), shares[0][1])] + shares[1:]
            place = (rep * number + g)[None]
            specs = [
                (v, pl.BlockSpec((part, width), lambda i, place, row=row: (row, 0))) for v, row in shares
            ]
            weights, grad = fresh_weights(place, count, specs, params)
            fresh.append(weights)
            grads.append(grad)
            if n + 1 == len(loads) or inside == 0:
                gathered.append(ways[g].gather(weights))
            if n and inside == 0:
                gathered.insert(1, ways[1].gather(fresh[1], steps[2]))
        inputs.append(laid)

    every = {0: jnp.concatenate(grads, axis=0)}
    k = near
    while k:
        for have in list(every):
            every[have ^ k] = swap(every[have], "rep", k)
        k //= 2

    mine = after(every[0], *[weights[1] for weights in gathered])
    own = update(rep[None], count, [mine], params, range(1), min(rows, 256), [])
    total = None
    if len(loads) > 1:
        total = project(inputs[0], jnp.concatenate([w for g in range(each) for w in gathered[g]], axis=0))
    held = range(number - each, number)
    begin = min(places[g][1] for g in held)
    assert all(places[g][1] == begin + i * half for i, g in enumerate(held))
    product = project(
        inputs[-1][begin : begin + each * half], jnp.concatenate([gathered[g][1] for g in held], axis=0)
    )
    total = product if total is None else total + product
    here = after(inputs[-1], every[near], total, own[0])
    sums, turn = [], here
    for side in (slice(0, features), slice(features, width)):
        here = after(here, turn)
        ends = []
        for columns in (slice(0, odd), slice(odd, 2 * odd)):
            end = total[columns, side]
            for g in held:
                row = places[g][0]
                end = end + project(here[row : row + half, columns], gathered[g][0][:, side])
            ends.append(end.astype(jnp.bfloat16))
            here = after(here, ends[0])
        away, stay = ends
        shares, turn = [stay, swap(away, "rep", 1)], stay
        size, k = odd // 2, 2
        while k < replicas:
            sent = sum(v[size : 2 * size].astype(jnp.float32) for v in shares).astype(jnp.bfloat16)
            shares.append(swap(sent, "rep", k))
            size, k = size // 2, 2 * k
        sums.append(shares)
    fresh = combine(sums, pair[None], pairs, block)

    others = [every[k] for k in range(1, replicas)]
    others[0] = after(others[0], sent)
    updated = update(rep[None], count, others, params, range(1, replicas), min(rows, 256), own)
    updated = [from_lane_rows(a, master.shape[0], features) for a in updated]
    return (*updated, fresh)


def solution(mesh):
    in_specs = (
        P(("rep", "shard", "tp"), None),
        P(("rep", "shard")),
        P(("rep", "shard"), None, "tp"),
        P("shard", None, "tp"),
        P("shard", None, "tp"),
        P("shard", None, "tp"),
    )
    out_specs = (
        P("shard", None, "tp"),
        P("shard", None, "tp"),
        P("shard", None, "tp"),
        P(("rep", "shard"), None, "tp"),
    )
    return jax.shard_map(local, mesh=mesh, in_specs=in_specs, out_specs=out_specs, check_vma=False)
```

```python
import functools

import jax
import jax.numpy as jnp
from jax import lax
from jax.experimental import pallas as pl
from jax.experimental.pallas import tpu as pltpu
from jax.sharding import PartitionSpec as P

beta_one = 0.9
beta_two = 0.95
step_count = 20
rate = 0.002
decay = 0.1
epsilon = 1e-08

LANES = 128
GROUPS = 4
LOADS = 2
VMEM_BYTES = 56 * 1024 * 1024

SMEM = pl.BlockSpec(memory_space=pltpu.SMEM)


def adamw(master, moment_one, moment_two, grad):
    first = beta_one * moment_one + (1.0 - beta_one) * grad
    second = beta_two * moment_two + (1.0 - beta_two) * grad * grad
    first_hat = first / (1.0 - beta_one**step_count)
    second_hat = second / (1.0 - beta_two**step_count)
    updated = master - rate * (first_hat / (jnp.sqrt(second_hat) + epsilon) + decay * master)
    return (updated, first, second)


def lane_rows(array):
    rows, two, features = array.shape
    split = array.reshape(rows, two, features // LANES, LANES)
    return split.transpose(0, 2, 1, 3).reshape(rows * two * features // LANES, LANES)


def from_lane_rows(array, rows, features):
    split = array.reshape(rows, features // LANES, 2, LANES)
    return split.transpose(0, 2, 1, 3).reshape(rows, 2, features)


def slots(features):
    return [half * features + tile * LANES for tile in range(features // LANES) for half in range(2)]


def call(kernel, out_shape, flops, moved, **kwargs):
    return pl.pallas_call(
        kernel,
        out_shape=out_shape,
        cost_estimate=pl.CostEstimate(flops=flops, bytes_accessed=moved, transcendentals=0),
        compiler_params=pltpu.CompilerParams(vmem_limit_bytes=VMEM_BYTES),
        **kwargs,
    )


def full(shape):
    return pl.BlockSpec(shape, lambda *_: (0,) * len(shape))


def f32(ref):
    return ref[...].astype(jnp.float32)


def pack(hidden, rep, loads, replicas, rows):
    tokens = hidden.shape[0]
    specs, shapes, orders = [], [], []
    for load in loads:
        for k in range(replicas):
            at = len(orders)
            for start, part, order in load:
                for _ in order:
                    at += 1

                    def index(i, place, at=at, k=k, start=start, part=part):
                        return (0, (place[at] * replicas + (place[0] ^ k)) * (rows // part) + start // part)

                    specs.append(pl.BlockSpec((tokens, part), index))
            shapes.append((sum(part * len(order) for _, part, order in load), tokens))
        orders += [shard for _, _, order in load for shard in order]

    def kernel(place, *refs):
        sources, outs = iter(refs[: len(specs)]), iter(refs[len(specs) :])
        for load in loads:
            for k in range(replicas):
                out, row = next(outs), 0
                for _, part, order in load:
                    for _ in order:
                        out[row : row + part, :] = next(sources)[...].T
                        row += part

    outs = call(
        kernel,
        [jax.ShapeDtypeStruct(shape, hidden.dtype) for shape in shapes],
        0,
        4 * sum(shape[0] * shape[1] for shape in shapes),
        grid_spec=pltpu.PrefetchScalarGridSpec(
            num_scalar_prefetch=1,
            grid=(1,),
            in_specs=specs,
            out_specs=[full(shape) for shape in shapes],
        ),
    )(jnp.stack([rep, *orders]), *[hidden] * len(specs))
    return [outs[i : i + replicas] for i in range(0, len(outs), replicas)]


def mask(cotan, place, pairs):
    block, _, features = cotan.shape
    width, tokens = 2 * features, block // pairs
    per = width // LANES

    def kernel(place, source, out, count, scratch):
        scratch[...] = source[...].astype(jnp.float32)
        count[...] = jnp.full(count.shape, place[0]).astype(jnp.float32)
        for o in range(pairs):
            start = (place[1] ^ o) * tokens
            row = lax.broadcasted_iota(jnp.int32, (tokens, LANES), 0) + start
            for slot, column in enumerate(slots(features)):
                rows = scratch[pl.ds(start * per + slot, tokens, stride=per), :]
                out[o * tokens : (o + 1) * tokens, column : column + LANES] = jnp.where(
                    row < place[0], rows, 0.0
                ).astype(out.dtype)

    return call(
        kernel,
        [jax.ShapeDtypeStruct((block, width), cotan.dtype), jax.ShapeDtypeStruct((8, LANES), jnp.float32)],
        0,
        4 * block * width,
        grid=(1,),
        in_specs=[SMEM, full((block * per, LANES))],
        out_specs=[full((block, width)), full((8, LANES))],
        scratch_shapes=[pltpu.VMEM((block * per, LANES), jnp.float32)],
    )(place, lane_rows(cotan))


def fresh_weights(place, count, shares, params):
    part, width = shares[0][1].block_shape
    per = width // LANES

    def kernel(place, count, *refs):
        sources = refs[: len(shares)]
        master, first, second, weights, grad, scratch = refs[len(shares) :]
        grad[...] = sum(f32(source) for source in sources).astype(grad.dtype)
        scale = 1.0 / count[0:1, 0:1]
        starts = slots(width // 2)
        for slot, start in enumerate(starts):
            scratch[pl.ds(slot, part, stride=per), :] = grad[:, start : start + LANES].astype(jnp.float32)
        updated, _, _ = adamw(master[...], first[...], second[...], scratch[...] * scale)
        scratch[...] = updated
        for slot, start in enumerate(starts):
            weights[:, start : start + LANES] = scratch[pl.ds(slot, part, stride=per), :].astype(weights.dtype)

    param_spec = pl.BlockSpec((part * per, LANES), lambda i, place: (place[0], 0))
    return call(
        kernel,
        [jax.ShapeDtypeStruct((part, width), jnp.bfloat16)] * 2,
        20 * part * width,
        20 * part * width,
        grid_spec=pltpu.PrefetchScalarGridSpec(
            num_scalar_prefetch=1,
            grid=(1,),
            in_specs=[full((8, LANES)), *[spec for _, spec in shares], param_spec, param_spec, param_spec],
            out_specs=[pl.BlockSpec((part, width), lambda i, place: (0, 0))] * 2,
            scratch_shapes=[pltpu.VMEM((part * per, LANES), jnp.float32)],
        ),
    )(place, count, *[a for a, _ in shares], *params)


def update(me, count, grads, params, ks, block, before):
    rows, width = grads[0].shape
    per = width // LANES
    steps = rows // block
    first_k = min(ks)

    def kernel(place, count, *refs):
        sources = refs[: len(grads)]
        master, first, second = refs[len(grads) : len(grads) + 3]
        new_master, new_first, new_second, scratch = refs[-4:]
        scale = 1.0 / count[0:1, 0:1]
        for j, grad in enumerate(sources):

            @pl.when(pl.program_id(0) == j)
            def _(grad=grad):
                for slot, start in enumerate(slots(width // 2)):
                    scratch[pl.ds(slot, block, stride=per), :] = grad[:, start : start + LANES].astype(jnp.float32)

        updated, one, two = adamw(master[...], first[...], second[...], scratch[...] * scale)
        new_master[...] = updated
        new_first[...] = one
        new_second[...] = two

    def grad_spec(j):
        return pl.BlockSpec(
            (block, width), lambda k, i, me: (jnp.where(k == j, i, jnp.where(k < j, 0, steps - 1)), 0)
        )

    param_spec = pl.BlockSpec((block * per, LANES), lambda k, i, me: ((me[0] ^ (k + first_k)) * steps + i, 0))
    size = len(ks) * rows * width
    return call(
        kernel,
        [jax.ShapeDtypeStruct(params[0].shape, jnp.float32)] * 3,
        20 * size,
        26 * size,
        grid_spec=pltpu.PrefetchScalarGridSpec(
            num_scalar_prefetch=1,
            grid=(len(ks), steps),
            in_specs=[full((8, LANES))]
            + [grad_spec(j) for j in range(len(grads))]
            + [param_spec] * 3
            + [pl.BlockSpec(memory_space=pl.ANY)] * len(before),
            out_specs=[param_spec] * 3,
            scratch_shapes=[pltpu.VMEM((block * per, LANES), jnp.float32)],
        ),
        input_output_aliases={2 + len(grads) + 3 + i: i for i in range(len(before))},
    )(me, count, *grads, *params, *before)


def combine(shares, pair, pairs, rows):
    features = shares[0][0].shape[1]
    tokens, per = rows // pairs, 2 * features // LANES
    each = len(shares[0])

    def kernel(pair, *refs):
        out, scratch = refs[-2], refs[-1]
        for o in range(pairs):
            start = (pair[0] ^ o) * tokens
            for slot, column in enumerate(slots(features)):
                half, at = divmod(column, features)
                total = sum(
                    source[o * tokens : (o + 1) * tokens, at : at + LANES].astype(jnp.float32)
                    for source in refs[half * each : (half + 1) * each]
                )
                scratch[pl.ds(start * per + slot, tokens, stride=per), :] = total
        out[...] = scratch[...].astype(out.dtype)

    out = call(
        kernel,
        jax.ShapeDtypeStruct((rows * per, LANES), jnp.bfloat16),
        0,
        16 * rows * features,
        grid=(1,),
        in_specs=[SMEM] + [full((rows, features))] * (2 * each),
        out_specs=full((rows * per, LANES)),
        scratch_shapes=[pltpu.VMEM((rows * per, LANES), jnp.float32)],
    )(pair, *shares[0], *shares[1])
    return from_lane_rows(out, rows, features)


def after(value, *deps):
    return lax.optimization_barrier((value, *deps))[0] if deps else value


def swap(value, axis, k):
    if k == 0:
        return value
    return lax.ppermute(value, axis, [(i, i ^ k) for i in range(lax.axis_size(axis))])


def add(a, b):
    return (a.astype(jnp.float32) + b.astype(jnp.float32)).astype(jnp.bfloat16)


class Line:
    ends_to_inner = [(0, 1), (3, 2)]
    across = [(1, 2), (2, 1)]
    inner_to_ends = [(1, 0), (2, 3)]

    away_first = True

    def __init__(self, shard):
        self.end = (shard == 0) | (shard == 3)
        low = shard < 2
        self.order = [jnp.where(low, 3, 0), jnp.where(low, 2, 1), shard ^ 1, shard]

    def send(self, away, soon):
        return add(away, after(lax.ppermute(away, "shard", self.ends_to_inner), *soon))

    def settle(self, far, last, soon):
        part = last.shape[0] // 2
        got = lax.ppermute(far, "shard", self.across)
        near = add(last[:part], after(got, *soon)[:part])
        return [(last, 1), (got, 1), (swap(near, "shard", 1), 0)], near

    def gather(self, own, *waits):
        side = after(jnp.concatenate([swap(own, "shard", 1), own], axis=0), *waits)
        got = lax.ppermute(side, "shard", self.across)
        far = lax.ppermute(got, "shard", self.inner_to_ends)
        return [jnp.where(self.end, far, got), side]


class Halves:
    away_first = False

    def __init__(self, shard, shards):
        order, k = [0], shards // 2
        while k:
            order, k = [i + k for i in order] + order, k // 2
        self.shards = shards
        self.order = [shard ^ q for q in order[shards // 2 :] + order[: shards // 2]]

    def send(self, away, soon):
        return after(swap(away, "shard", 1), *soon)

    def settle(self, far, last, soon):
        shares, half, k, sent = [last, far], last.shape[0], 2, far
        while k < self.shards:
            sent = sum(v[v.shape[0] - half : v.shape[0] - half // 2].astype(jnp.float32) for v in shares)
            sent, half, k = sent.astype(jnp.bfloat16), half // 2, 2 * k
            shares.append(swap(sent, "shard", k // 2))
        return [(v, v.shape[0] // half - 1) for v in shares], sent

    def gather(self, own, *waits):
        blocks, k = own, self.shards // 2
        while k > 1:
            blocks, k = jnp.concatenate([swap(blocks, "shard", k), blocks], axis=0), k // 2
        return [swap(blocks, "shard", 1), blocks]


def local(hidden_in, lengths, kv_grad_out, master, moment_one, moment_two):
    replicas, shards, pairs = (lax.axis_size(name) for name in ("rep", "shard", "tp"))
    rep, shard, pair = (lax.axis_index(name).astype(jnp.int32) for name in ("rep", "shard", "tp"))
    tokens, depth = hidden_in.shape
    block, _, features = kv_grad_out.shape
    width = 2 * features
    rows = depth // (shards * replicas)
    near = replicas // 2
    parities = [k for k in range(replicas) if k % 2] + [k for k in range(replicas) if not k % 2]
    odd = replicas // 2 * block

    number = max(1, min(GROUPS, rows // LANES))
    part = rows // number
    ways = [Line(shard) if shards == 4 and g < number - 1 else Halves(shard, shards) for g in range(number)]
    groups = [(g * part, part, way.order) for g, way in enumerate(ways)]
    each = max(1, number // LOADS)
    loads = [groups[g : g + each] for g in range(0, number, each)]
    by_rows = (((0,), (0,)), ((), ()))

    count, k = jnp.full((8, LANES), lengths[0]).astype(jnp.float32), near
    count = count + swap(count, "rep", k)
    early, k = count, k // 2
    while k:
        count, k = count + swap(count, "rep", k), k // 2
    k = 1
    while k < shards:
        count, k = count + swap(count, "shard", k), 2 * k
    pieces = pack(hidden_in, rep, loads[:1], replicas, rows)
    cotan, _ = mask(kv_grad_out, jnp.stack([lengths[0], pair]), pairs)
    if len(loads) > 1:
        pieces += pack(hidden_in, after(rep, count), loads[1:], replicas, rows)
    arrived, sides, line = [], [], []

    def travel(n, *waits):
        arrived.append(
            [pieces[n][0]]
            + [swap(after(h, *waits) if k >= near else h, "rep", k) for k, h in enumerate(pieces[n]) if k]
        )
        sides.append([])

    def pair_up(n, ks, *waits):
        for k in ks:
            sent = after(arrived[n][k], *line[-2:-1], *waits)
            sides[n].append([arrived[n][k]] + [swap(sent, "tp", o) for o in range(1, pairs)])
            line.append(sides[n][-1][-1])

    def lay(n):
        return jnp.concatenate([p for k in parities for p in sides[n][k]], axis=1)

    low, high = range(near), range(near, replicas)
    travel(0, early)
    pair_up(0, low)
    pair_up(0, high, cotan)
    ready = [*arrived[0][near:], *line[:near], *(pieces[1] if len(loads) > 1 else [])]
    cotans = {0: cotan, near: swap(after(cotan, *ready), "rep", near)}
    for n in range(1, len(loads)):
        travel(n, *([cotans[near]] if n == 1 else arrived[n - 1][near:]))
        if n == 1:
            pair_up(1, low)
    k = near // 2
    while k:
        for have in list(cotans):
            cotans[have ^ k] = swap(cotans[have], "rep", k)
        k //= 2
    cotans = jnp.concatenate([cotans[k] for k in parities], axis=0)

    params = [lane_rows(a) for a in (master, moment_one, moment_two)]
    steps, summed, grads, fresh, gathered, places, inputs, last = [], [], [], [], [], [], [], None

    def project(rows, weights):
        return lax.dot_general(rows, weights, by_rows, preferred_element_type=jnp.float32)

    half = shards // 2 * part
    for n, load in enumerate(loads):
        laid = lay(n)
        if n:
            laid = after(laid, fresh[(n - 1) * each], *steps)
        for inside in range(len(load)):
            g, way = n * each + inside, ways[n * each + inside]
            if last is not None:
                laid = after(laid, last)
            if n + 1 < len(loads) and inside == 1:
                laid = after(laid, line[(n + 1) * replicas])
            row = inside * 2 * half
            far_row, near_row = (row, row + half) if way.away_first else (row + half, row)
            places.append((far_row, near_row))
            away = jnp.dot(laid[far_row : far_row + half], cotans, preferred_element_type=jnp.float32)
            away = away.astype(jnp.bfloat16)
            laid = after(laid, away)
            last = jnp.dot(laid[near_row : near_row + half], cotans, preferred_element_type=jnp.float32)
            last = last.astype(jnp.bfloat16)
            soon, then = [], []
            if not n and inside:
                away = after(away, far)
            if n + 1 < len(loads) and inside:
                soon = arrived[n + 1][near:]
            if n and inside:
                soon = [summed[each - 1][-1][0]]
            far = way.send(away, soon)
            if n + 1 < len(loads):
                pair_up(n + 1, range(near + inside, near + inside + 1 if inside < each - 1 else replicas), far)
                then = line[-1:]
            shares, passed = way.settle(far, last, then)
            steps.append(passed)
            summed.append(shares)
        for inside in range(len(load)):
            g = n * each + inside
            shares = summed[g]
            if n and inside == 0:
                shares = [(after(shares[0][0], steps[-1], *fresh[each - 1 : each]), shares[0][1])] + shares[1:]
            if not n and inside:
                shares = [(after(shares[0][0], gathered[0][0]), shares[0][1])] + shares[1:]
            if n and inside:
                shares = [(after(shares[0][0], fresh[each - 1], steps[each]), shares[0][1])] + shares[1:]
            place = (rep * number + g)[None]
            specs = [
                (v, pl.BlockSpec((part, width), lambda i, place, row=row: (row, 0))) for v, row in shares
            ]
            weights, grad = fresh_weights(place, count, specs, params)
            fresh.append(weights)
            grads.append(grad)
            if n + 1 == len(loads) or inside == 0:
                gathered.append(ways[g].gather(weights))
            if n and inside == 0:
                gathered.insert(1, ways[1].gather(fresh[1], steps[2]))
        inputs.append(laid)

    every = {0: jnp.concatenate(grads, axis=0)}
    k = near
    while k:
        for have in list(every):
            every[have ^ k] = swap(every[have], "rep", k)
        k //= 2

    mine = after(every[0], *[weights[1] for weights in gathered])
    own = update(rep[None], count, [mine], params, range(1), min(rows, 256), [])
    total = None
    if len(loads) > 1:
        total = project(inputs[0], jnp.concatenate([w for g in range(each) for w in gathered[g]], axis=0))
    held = range(number - each, number)
    begin = min(places[g][1] for g in held)
    assert all(places[g][1] == begin + i * half for i, g in enumerate(held))
    product = project(
        inputs[-1][begin : begin + each * half], jnp.concatenate([gathered[g][1] for g in held], axis=0)
    )
    total = product if total is None else total + product
    here = after(inputs[-1], every[near], total, own[0])
    sums, turn = [], here
    for side in (slice(0, features), slice(features, width)):
        here = after(here, turn)
        ends = []
        for columns in (slice(0, odd), slice(odd, 2 * odd)):
            end = total[columns, side]
            for g in held:
                row = places[g][0]
                end = end + project(here[row : row + half, columns], gathered[g][0][:, side])
            ends.append(end.astype(jnp.bfloat16))
            here = after(here, ends[0])
        away, stay = ends
        shares, turn = [stay, swap(away, "rep", 1)], stay
        size, k = odd // 2, 2
        while k < replicas:
            sent = sum(v[size : 2 * size].astype(jnp.float32) for v in shares).astype(jnp.bfloat16)
            shares.append(swap(sent, "rep", k))
            size, k = size // 2, 2 * k
        sums.append(shares)
    fresh = combine(sums, pair[None], pairs, block)

    others = [every[k] for k in range(1, replicas)]
    others[0] = after(others[0], sent)
    updated = update(rep[None], count, others, params, range(1, replicas), min(rows, 256), own)
    updated = [from_lane_rows(a, master.shape[0], features) for a in updated]
    return (*updated, fresh)


def solution(mesh):
    in_specs = (
        P(("rep", "shard", "tp"), None),
        P(("rep", "shard")),
        P(("rep", "shard"), None, "tp"),
        P("shard", None, "tp"),
        P("shard", None, "tp"),
        P("shard", None, "tp"),
    )
    out_specs = (
        P("shard", None, "tp"),
        P("shard", None, "tp"),
        P("shard", None, "tp"),
        P(("rep", "shard"), None, "tp"),
    )
    return jax.shard_map(local, mesh=mesh, in_specs=in_specs, out_specs=out_specs, check_vma=False)
```

```python
import functools

import jax
import jax.numpy as jnp
from jax import lax
from jax.experimental import pallas as pl
from jax.experimental.pallas import tpu as pltpu
from jax.sharding import PartitionSpec as P

beta_one = 0.9
beta_two = 0.95
step_count = 20
rate = 0.002
decay = 0.1
epsilon = 1e-08

LANES = 128
GROUPS = 4
LOADS = 2
VMEM_BYTES = 56 * 1024 * 1024

SMEM = pl.BlockSpec(memory_space=pltpu.SMEM)


def adamw(master, moment_one, moment_two, grad):
    first = beta_one * moment_one + (1.0 - beta_one) * grad
    second = beta_two * moment_two + (1.0 - beta_two) * grad * grad
    first_hat = first / (1.0 - beta_one**step_count)
    second_hat = second / (1.0 - beta_two**step_count)
    updated = master - rate * (first_hat / (jnp.sqrt(second_hat) + epsilon) + decay * master)
    return (updated, first, second)


def lane_rows(array):
    rows, two, features = array.shape
    split = array.reshape(rows, two, features // LANES, LANES)
    return split.transpose(0, 2, 1, 3).reshape(rows * two * features // LANES, LANES)


def from_lane_rows(array, rows, features):
    split = array.reshape(rows, features // LANES, 2, LANES)
    return split.transpose(0, 2, 1, 3).reshape(rows, 2, features)


def slots(features):
    return [half * features + tile * LANES for tile in range(features // LANES) for half in range(2)]


def call(kernel, out_shape, flops, moved, **kwargs):
    return pl.pallas_call(
        kernel,
        out_shape=out_shape,
        cost_estimate=pl.CostEstimate(flops=flops, bytes_accessed=moved, transcendentals=0),
        compiler_params=pltpu.CompilerParams(vmem_limit_bytes=VMEM_BYTES),
        **kwargs,
    )


def full(shape):
    return pl.BlockSpec(shape, lambda *_: (0,) * len(shape))


def f32(ref):
    return ref[...].astype(jnp.float32)


def pack(hidden, rep, loads, replicas, rows):
    tokens = hidden.shape[0]
    specs, shapes, orders = [], [], []
    for load in loads:
        for k in range(replicas):
            at = len(orders)
            for start, part, order in load:
                for _ in order:
                    at += 1

                    def index(i, place, at=at, k=k, start=start, part=part):
                        return (0, (place[at] * replicas + (place[0] ^ k)) * (rows // part) + start // part)

                    specs.append(pl.BlockSpec((tokens, part), index))
            shapes.append((sum(part * len(order) for _, part, order in load), tokens))
        orders += [shard for _, _, order in load for shard in order]

    def kernel(place, *refs):
        sources, outs = iter(refs[: len(specs)]), iter(refs[len(specs) :])
        for load in loads:
            for k in range(replicas):
                out, row = next(outs), 0
                for _, part, order in load:
                    for _ in order:
                        out[row : row + part, :] = next(sources)[...].T
                        row += part

    outs = call(
        kernel,
        [jax.ShapeDtypeStruct(shape, hidden.dtype) for shape in shapes],
        0,
        4 * sum(shape[0] * shape[1] for shape in shapes),
        grid_spec=pltpu.PrefetchScalarGridSpec(
            num_scalar_prefetch=1,
            grid=(1,),
            in_specs=specs,
            out_specs=[full(shape) for shape in shapes],
        ),
    )(jnp.stack([rep, *orders]), *[hidden] * len(specs))
    return [outs[i : i + replicas] for i in range(0, len(outs), replicas)]


def mask(cotan, place, pairs):
    block, _, features = cotan.shape
    width, tokens = 2 * features, block // pairs
    per = width // LANES

    def kernel(place, source, out, count, scratch):
        scratch[...] = source[...].astype(jnp.float32)
        count[...] = jnp.full(count.shape, place[0]).astype(jnp.float32)
        for o in range(pairs):
            start = (place[1] ^ o) * tokens
            row = lax.broadcasted_iota(jnp.int32, (tokens, LANES), 0) + start
            for slot, column in enumerate(slots(features)):
                rows = scratch[pl.ds(start * per + slot, tokens, stride=per), :]
                out[o * tokens : (o + 1) * tokens, column : column + LANES] = jnp.where(
                    row < place[0], rows, 0.0
                ).astype(out.dtype)

    return call(
        kernel,
        [jax.ShapeDtypeStruct((block, width), cotan.dtype), jax.ShapeDtypeStruct((8, LANES), jnp.float32)],
        0,
        4 * block * width,
        grid=(1,),
        in_specs=[SMEM, full((block * per, LANES))],
        out_specs=[full((block, width)), full((8, LANES))],
        scratch_shapes=[pltpu.VMEM((block * per, LANES), jnp.float32)],
    )(place, lane_rows(cotan))


def fresh_weights(place, count, shares, params):
    part, width = shares[0][1].block_shape
    per = width // LANES

    def kernel(place, count, *refs):
        sources = refs[: len(shares)]
        master, first, second, weights, grad, scratch = refs[len(shares) :]
        grad[...] = sum(f32(source) for source in sources).astype(grad.dtype)
        scale = 1.0 / count[0:1, 0:1]
        starts = slots(width // 2)
        for slot, start in enumerate(starts):
            scratch[pl.ds(slot, part, stride=per), :] = grad[:, start : start + LANES].astype(jnp.float32)
        updated, _, _ = adamw(master[...], first[...], second[...], scratch[...] * scale)
        scratch[...] = updated
        for slot, start in enumerate(starts):
            weights[:, start : start + LANES] = scratch[pl.ds(slot, part, stride=per), :].astype(weights.dtype)

    param_spec = pl.BlockSpec((part * per, LANES), lambda i, place: (place[0], 0))
    return call(
        kernel,
        [jax.ShapeDtypeStruct((part, width), jnp.bfloat16)] * 2,
        20 * part * width,
        20 * part * width,
        grid_spec=pltpu.PrefetchScalarGridSpec(
            num_scalar_prefetch=1,
            grid=(1,),
            in_specs=[full((8, LANES)), *[spec for _, spec in shares], param_spec, param_spec, param_spec],
            out_specs=[pl.BlockSpec((part, width), lambda i, place: (0, 0))] * 2,
            scratch_shapes=[pltpu.VMEM((part * per, LANES), jnp.float32)],
        ),
    )(place, count, *[a for a, _ in shares], *params)


def update(me, count, grads, params, ks, block, before):
    rows, width = grads[0].shape
    per = width // LANES
    steps = rows // block
    first_k = min(ks)

    def kernel(place, count, *refs):
        sources = refs[: len(grads)]
        master, first, second = refs[len(grads) : len(grads) + 3]
        new_master, new_first, new_second, scratch = refs[-4:]
        scale = 1.0 / count[0:1, 0:1]
        for j, grad in enumerate(sources):

            @pl.when(pl.program_id(0) == j)
            def _(grad=grad):
                for slot, start in enumerate(slots(width // 2)):
                    scratch[pl.ds(slot, block, stride=per), :] = grad[:, start : start + LANES].astype(jnp.float32)

        updated, one, two = adamw(master[...], first[...], second[...], scratch[...] * scale)
        new_master[...] = updated
        new_first[...] = one
        new_second[...] = two

    def grad_spec(j):
        return pl.BlockSpec(
            (block, width), lambda k, i, me: (jnp.where(k == j, i, jnp.where(k < j, 0, steps - 1)), 0)
        )

    param_spec = pl.BlockSpec((block * per, LANES), lambda k, i, me: ((me[0] ^ (k + first_k)) * steps + i, 0))
    size = len(ks) * rows * width
    return call(
        kernel,
        [jax.ShapeDtypeStruct(params[0].shape, jnp.float32)] * 3,
        20 * size,
        26 * size,
        grid_spec=pltpu.PrefetchScalarGridSpec(
            num_scalar_prefetch=1,
            grid=(len(ks), steps),
            in_specs=[full((8, LANES))]
            + [grad_spec(j) for j in range(len(grads))]
            + [param_spec] * 3
            + [pl.BlockSpec(memory_space=pl.ANY)] * len(before),
            out_specs=[param_spec] * 3,
            scratch_shapes=[pltpu.VMEM((block * per, LANES), jnp.float32)],
        ),
        input_output_aliases={2 + len(grads) + 3 + i: i for i in range(len(before))},
    )(me, count, *grads, *params, *before)


def combine(shares, pair, pairs, rows):
    features = shares[0][0].shape[1]
    tokens, per = rows // pairs, 2 * features // LANES
    each = len(shares[0])

    def kernel(pair, *refs):
        out, scratch = refs[-2], refs[-1]
        for o in range(pairs):
            start = (pair[0] ^ o) * tokens
            for slot, column in enumerate(slots(features)):
                half, at = divmod(column, features)
                total = sum(
                    source[o * tokens : (o + 1) * tokens, at : at + LANES].astype(jnp.float32)
                    for source in refs[half * each : (half + 1) * each]
                )
                scratch[pl.ds(start * per + slot, tokens, stride=per), :] = total
        out[...] = scratch[...].astype(out.dtype)

    out = call(
        kernel,
        jax.ShapeDtypeStruct((rows * per, LANES), jnp.bfloat16),
        0,
        16 * rows * features,
        grid=(1,),
        in_specs=[SMEM] + [full((rows, features))] * (2 * each),
        out_specs=full((rows * per, LANES)),
        scratch_shapes=[pltpu.VMEM((rows * per, LANES), jnp.float32)],
    )(pair, *shares[0], *shares[1])
    return from_lane_rows(out, rows, features)


def after(value, *deps):
    return lax.optimization_barrier((value, *deps))[0] if deps else value


def swap(value, axis, k):
    if k == 0:
        return value
    return lax.ppermute(value, axis, [(i, i ^ k) for i in range(lax.axis_size(axis))])


def add(a, b):
    return (a.astype(jnp.float32) + b.astype(jnp.float32)).astype(jnp.bfloat16)


class Line:
    ends_to_inner = [(0, 1), (3, 2)]
    across = [(1, 2), (2, 1)]
    inner_to_ends = [(1, 0), (2, 3)]

    away_first = True

    def __init__(self, shard):
        self.end = (shard == 0) | (shard == 3)
        low = shard < 2
        self.order = [jnp.where(low, 3, 0), jnp.where(low, 2, 1), shard ^ 1, shard]

    def send(self, away, soon):
        return add(away, after(lax.ppermute(away, "shard", self.ends_to_inner), *soon))

    def settle(self, far, last, soon):
        part = last.shape[0] // 2
        got = lax.ppermute(far, "shard", self.across)
        near = add(last[:part], after(got, *soon)[:part])
        return [(last, 1), (got, 1), (swap(near, "shard", 1), 0)], near

    def gather(self, own, *waits):
        side = after(jnp.concatenate([swap(own, "shard", 1), own], axis=0), *waits)
        got = lax.ppermute(side, "shard", self.across)
        far = lax.ppermute(got, "shard", self.inner_to_ends)
        return [jnp.where(self.end, far, got), side]


class Halves:
    away_first = False

    def __init__(self, shard, shards):
        order, k = [0], shards // 2
        while k:
            order, k = [i + k for i in order] + order, k // 2
        self.shards = shards
        self.order = [shard ^ q for q in order[shards // 2 :] + order[: shards // 2]]

    def send(self, away, soon):
        return after(swap(away, "shard", 1), *soon)

    def settle(self, far, last, soon):
        shares, half, k, sent = [last, far], last.shape[0], 2, far
        while k < self.shards:
            sent = sum(v[v.shape[0] - half : v.shape[0] - half // 2].astype(jnp.float32) for v in shares)
            sent, half, k = sent.astype(jnp.bfloat16), half // 2, 2 * k
            shares.append(swap(sent, "shard", k // 2))
        return [(v, v.shape[0] // half - 1) for v in shares], sent

    def gather(self, own, *waits):
        blocks, k = own, self.shards // 2
        while k > 1:
            blocks, k = jnp.concatenate([swap(blocks, "shard", k), blocks], axis=0), k // 2
        return [swap(blocks, "shard", 1), blocks]


def local(hidden_in, lengths, kv_grad_out, master, moment_one, moment_two):
    replicas, shards, pairs = (lax.axis_size(name) for name in ("rep", "shard", "tp"))
    rep, shard, pair = (lax.axis_index(name).astype(jnp.int32) for name in ("rep", "shard", "tp"))
    tokens, depth = hidden_in.shape
    block, _, features = kv_grad_out.shape
    width = 2 * features
    rows = depth // (shards * replicas)
    near = replicas // 2
    parities = [k for k in range(replicas) if k % 2] + [k for k in range(replicas) if not k % 2]
    odd = replicas // 2 * block

    number = max(1, min(GROUPS, rows // LANES))
    part = rows // number
    ways = [Line(shard) if shards == 4 and g < number - 1 else Halves(shard, shards) for g in range(number)]
    groups = [(g * part, part, way.order) for g, way in enumerate(ways)]
    each = max(1, number // LOADS)
    loads = [groups[g : g + each] for g in range(0, number, each)]
    by_rows = (((0,), (0,)), ((), ()))

    count, k = jnp.full((8, LANES), lengths[0]).astype(jnp.float32), near
    count = count + swap(count, "rep", k)
    early, k = count, k // 2
    while k:
        count, k = count + swap(count, "rep", k), k // 2
    k = 1
    while k < shards:
        count, k = count + swap(count, "shard", k), 2 * k
    pieces = pack(hidden_in, rep, loads[:1], replicas, rows)
    cotan, _ = mask(kv_grad_out, jnp.stack([lengths[0], pair]), pairs)
    if len(loads) > 1:
        pieces += pack(hidden_in, after(rep, count), loads[1:], replicas, rows)
    arrived, sides, line = [], [], []

    def travel(n, *waits):
        arrived.append(
            [pieces[n][0]]
            + [swap(after(h, *waits) if k >= near else h, "rep", k) for k, h in enumerate(pieces[n]) if k]
        )
        sides.append([])

    def pair_up(n, ks, *waits):
        for k in ks:
            sent = after(arrived[n][k], *line[-2:-1], *waits)
            sides[n].append([arrived[n][k]] + [swap(sent, "tp", o) for o in range(1, pairs)])
            line.append(sides[n][-1][-1])

    def lay(n):
        return jnp.concatenate([p for k in parities for p in sides[n][k]], axis=1)

    low, high = range(near), range(near, replicas)
    travel(0, early)
    pair_up(0, low)
    pair_up(0, high, cotan)
    ready = [*arrived[0][near:], *line[:near], *(pieces[1] if len(loads) > 1 else [])]
    cotans = {0: cotan, near: swap(after(cotan, *ready), "rep", near)}
    for n in range(1, len(loads)):
        travel(n, *([cotans[near]] if n == 1 else arrived[n - 1][near:]))
        if n == 1:
            pair_up(1, low)
    k = near // 2
    while k:
        for have in list(cotans):
            cotans[have ^ k] = swap(cotans[have], "rep", k)
        k //= 2
    cotans = jnp.concatenate([cotans[k] for k in parities], axis=0)

    params = [lane_rows(a) for a in (master, moment_one, moment_two)]
    steps, summed, grads, fresh, gathered, places, inputs, last = [], [], [], [], [], [], [], None

    def project(rows, weights):
        return lax.dot_general(rows, weights, by_rows, preferred_element_type=jnp.float32)

    half = shards // 2 * part
    for n, load in enumerate(loads):
        laid = lay(n)
        if n:
            laid = after(laid, fresh[(n - 1) * each], *steps)
        for inside in range(len(load)):
            g, way = n * each + inside, ways[n * each + inside]
            if last is not None:
                laid = after(laid, last)
            if n + 1 < len(loads) and inside == 1:
                laid = after(laid, line[(n + 1) * replicas])
            row = inside * 2 * half
            far_row, near_row = (row, row + half) if way.away_first else (row + half, row)
            places.append((far_row, near_row))
            away = jnp.dot(laid[far_row : far_row + half], cotans, preferred_element_type=jnp.float32)
            away = away.astype(jnp.bfloat16)
            laid = after(laid, away)
            last = jnp.dot(laid[near_row : near_row + half], cotans, preferred_element_type=jnp.float32)
            last = last.astype(jnp.bfloat16)
            soon, then = [], []
            if not n and inside:
                away = after(away, far)
            if n + 1 < len(loads) and inside:
                soon = arrived[n + 1][near:]
            if n and inside:
                soon = [summed[each - 1][-1][0]]
            far = way.send(away, soon)
            if n + 1 < len(loads):
                pair_up(n + 1, range(near + inside, near + inside + 1 if inside < each - 1 else replicas), far)
                then = line[-1:]
            shares, passed = way.settle(far, last, then)
            steps.append(passed)
            summed.append(shares)
        for inside in range(len(load)):
            g = n * each + inside
            shares = summed[g]
            if n and inside == 0:
                shares = [(after(shares[0][0], steps[-1], *fresh[each - 1 : each]), shares[0][1])] + shares[1:]
            if not n and inside:
                shares = [(after(shares[0][0], gathered[0][0]), shares[0][1])] + shares[1:]
            if n and inside:
                shares = [(after(shares[0][0], fresh[each - 1], steps[each]), shares[0][1])] + shares[1:]
            place = (rep * number + g)[None]
            specs = [
                (v, pl.BlockSpec((part, width), lambda i, place, row=row: (row, 0))) for v, row in shares
            ]
            weights, grad = fresh_weights(place, count, specs, params)
            fresh.append(weights)
            grads.append(grad)
            if n + 1 == len(loads) or inside == 0:
                gathered.append(ways[g].gather(weights))
            if n and inside == 0:
                gathered.insert(1, ways[1].gather(fresh[1], steps[2]))
        inputs.append(laid)

    every = {0: jnp.concatenate(grads, axis=0)}
    k = near
    while k:
        for have in list(every):
            every[have ^ k] = swap(every[have], "rep", k)
        k //= 2

    total = None
    if len(loads) > 1:
        total = project(inputs[0], jnp.concatenate([w for g in range(each) for w in gathered[g]], axis=0))
    held = range(number - each, number)
    begin = min(places[g][1] for g in held)
    assert all(places[g][1] == begin + i * half for i, g in enumerate(held))
    product = project(
        inputs[-1][begin : begin + each * half], jnp.concatenate([gathered[g][1] for g in held], axis=0)
    )
    total = product if total is None else total + product
    here = after(inputs[-1], every[near], total)
    sums, turn = [], here
    for side in (slice(0, features), slice(features, width)):
        here = after(here, turn)
        ends = []
        for columns in (slice(0, odd), slice(odd, 2 * odd)):
            end = total[columns, side]
            for g in held:
                row = places[g][0]
                end = end + project(here[row : row + half, columns], gathered[g][0][:, side])
            ends.append(end.astype(jnp.bfloat16))
            here = after(here, ends[0])
        away, stay = ends
        shares, turn = [stay, swap(away, "rep", 1)], stay
        size, k = odd // 2, 2
        while k < replicas:
            sent = sum(v[size : 2 * size].astype(jnp.float32) for v in shares).astype(jnp.bfloat16)
            shares.append(swap(sent, "rep", k))
            size, k = size // 2, 2 * k
        sums.append(shares)
    fresh = combine(sums, pair[None], pairs, block)

    everyone = [after(every[0], sent)] + [every[k] for k in range(1, replicas)]
    updated = update(rep[None], count, everyone, params, range(replicas), min(rows, 256), [])
    updated = [from_lane_rows(a, master.shape[0], features) for a in updated]
    return (*updated, fresh)


def solution(mesh):
    in_specs = (
        P(("rep", "shard", "tp"), None),
        P(("rep", "shard")),
        P(("rep", "shard"), None, "tp"),
        P("shard", None, "tp"),
        P("shard", None, "tp"),
        P("shard", None, "tp"),
    )
    out_specs = (
        P("shard", None, "tp"),
        P("shard", None, "tp"),
        P("shard", None, "tp"),
        P(("rep", "shard"), None, "tp"),
    )
    return jax.shard_map(local, mesh=mesh, in_specs=in_specs, out_specs=out_specs, check_vma=False)
```

```python
import functools

import jax
import jax.numpy as jnp
from jax import lax
from jax.experimental import pallas as pl
from jax.experimental.pallas import tpu as pltpu
from jax.sharding import PartitionSpec as P

beta_one = 0.9
beta_two = 0.95
step_count = 20
rate = 0.002
decay = 0.1
epsilon = 1e-08

LANES = 128
GROUPS = 4
LOADS = 2
VMEM_BYTES = 56 * 1024 * 1024

SMEM = pl.BlockSpec(memory_space=pltpu.SMEM)


def adamw(master, moment_one, moment_two, grad):
    first = beta_one * moment_one + (1.0 - beta_one) * grad
    second = beta_two * moment_two + (1.0 - beta_two) * grad * grad
    first_hat = first / (1.0 - beta_one**step_count)
    second_hat = second / (1.0 - beta_two**step_count)
    updated = master - rate * (first_hat / (jnp.sqrt(second_hat) + epsilon) + decay * master)
    return (updated, first, second)


def lane_rows(array):
    rows, two, features = array.shape
    split = array.reshape(rows, two, features // LANES, LANES)
    return split.transpose(0, 2, 1, 3).reshape(rows * two * features // LANES, LANES)


def from_lane_rows(array, rows, features):
    split = array.reshape(rows, features // LANES, 2, LANES)
    return split.transpose(0, 2, 1, 3).reshape(rows, 2, features)


def slots(features):
    return [half * features + tile * LANES for tile in range(features // LANES) for half in range(2)]


def call(kernel, out_shape, flops, moved, **kwargs):
    return pl.pallas_call(
        kernel,
        out_shape=out_shape,
        cost_estimate=pl.CostEstimate(flops=flops, bytes_accessed=moved, transcendentals=0),
        compiler_params=pltpu.CompilerParams(vmem_limit_bytes=VMEM_BYTES),
        **kwargs,
    )


def full(shape):
    return pl.BlockSpec(shape, lambda *_: (0,) * len(shape))


def f32(ref):
    return ref[...].astype(jnp.float32)


def pack(hidden, rep, loads, replicas, rows):
    tokens = hidden.shape[0]
    specs, shapes, orders = [], [], []
    for load in loads:
        for k in range(replicas):
            at = len(orders)
            for start, part, order in load:
                for _ in order:
                    at += 1

                    def index(i, place, at=at, k=k, start=start, part=part):
                        return (0, (place[at] * replicas + (place[0] ^ k)) * (rows // part) + start // part)

                    specs.append(pl.BlockSpec((tokens, part), index))
            shapes.append((sum(part * len(order) for _, part, order in load), tokens))
        orders += [shard for _, _, order in load for shard in order]

    def kernel(place, *refs):
        sources, outs = iter(refs[: len(specs)]), iter(refs[len(specs) :])
        for load in loads:
            for k in range(replicas):
                out, row = next(outs), 0
                for _, part, order in load:
                    for _ in order:
                        out[row : row + part, :] = next(sources)[...].T
                        row += part

    outs = call(
        kernel,
        [jax.ShapeDtypeStruct(shape, hidden.dtype) for shape in shapes],
        0,
        4 * sum(shape[0] * shape[1] for shape in shapes),
        grid_spec=pltpu.PrefetchScalarGridSpec(
            num_scalar_prefetch=1,
            grid=(1,),
            in_specs=specs,
            out_specs=[full(shape) for shape in shapes],
        ),
    )(jnp.stack([rep, *orders]), *[hidden] * len(specs))
    return [outs[i : i + replicas] for i in range(0, len(outs), replicas)]


def mask(cotan, place, pairs):
    block, _, features = cotan.shape
    width, tokens = 2 * features, block // pairs
    per = width // LANES

    def kernel(place, source, out, count, scratch):
        scratch[...] = source[...].astype(jnp.float32)
        count[...] = jnp.full(count.shape, place[0]).astype(jnp.float32)
        for o in range(pairs):
            start = (place[1] ^ o) * tokens
            row = lax.broadcasted_iota(jnp.int32, (tokens, LANES), 0) + start
            for slot, column in enumerate(slots(features)):
                rows = scratch[pl.ds(start * per + slot, tokens, stride=per), :]
                out[o * tokens : (o + 1) * tokens, column : column + LANES] = jnp.where(
                    row < place[0], rows, 0.0
                ).astype(out.dtype)

    return call(
        kernel,
        [jax.ShapeDtypeStruct((block, width), cotan.dtype), jax.ShapeDtypeStruct((8, LANES), jnp.float32)],
        0,
        4 * block * width,
        grid=(1,),
        in_specs=[SMEM, full((block * per, LANES))],
        out_specs=[full((block, width)), full((8, LANES))],
        scratch_shapes=[pltpu.VMEM((block * per, LANES), jnp.float32)],
    )(place, lane_rows(cotan))


def fresh_weights(place, count, shares, params):
    part, width = shares[0][1].block_shape
    per = width // LANES

    def kernel(place, count, *refs):
        sources = refs[: len(shares)]
        master, first, second, weights, grad, scratch = refs[len(shares) :]
        grad[...] = sum(f32(source) for source in sources).astype(grad.dtype)
        scale = 1.0 / count[0:1, 0:1]
        starts = slots(width // 2)
        for slot, start in enumerate(starts):
            scratch[pl.ds(slot, part, stride=per), :] = grad[:, start : start + LANES].astype(jnp.float32)
        updated, _, _ = adamw(master[...], first[...], second[...], scratch[...] * scale)
        scratch[...] = updated
        for slot, start in enumerate(starts):
            weights[:, start : start + LANES] = scratch[pl.ds(slot, part, stride=per), :].astype(weights.dtype)

    param_spec = pl.BlockSpec((part * per, LANES), lambda i, place: (place[0], 0))
    return call(
        kernel,
        [jax.ShapeDtypeStruct((part, width), jnp.bfloat16)] * 2,
        20 * part * width,
        20 * part * width,
        grid_spec=pltpu.PrefetchScalarGridSpec(
            num_scalar_prefetch=1,
            grid=(1,),
            in_specs=[full((8, LANES)), *[spec for _, spec in shares], param_spec, param_spec, param_spec],
            out_specs=[pl.BlockSpec((part, width), lambda i, place: (0, 0))] * 2,
            scratch_shapes=[pltpu.VMEM((part * per, LANES), jnp.float32)],
        ),
    )(place, count, *[a for a, _ in shares], *params)


def update(me, count, grads, params, ks, block, before):
    rows, width = grads[0].shape
    per = width // LANES
    steps = rows // block
    first_k = min(ks)

    def kernel(place, count, *refs):
        sources = refs[: len(grads)]
        master, first, second = refs[len(grads) : len(grads) + 3]
        new_master, new_first, new_second, scratch = refs[-4:]
        scale = 1.0 / count[0:1, 0:1]
        for j, grad in enumerate(sources):

            @pl.when(pl.program_id(0) == j)
            def _(grad=grad):
                for slot, start in enumerate(slots(width // 2)):
                    scratch[pl.ds(slot, block, stride=per), :] = grad[:, start : start + LANES].astype(jnp.float32)

        updated, one, two = adamw(master[...], first[...], second[...], scratch[...] * scale)
        new_master[...] = updated
        new_first[...] = one
        new_second[...] = two

    def grad_spec(j):
        return pl.BlockSpec(
            (block, width), lambda k, i, me: (jnp.where(k == j, i, jnp.where(k < j, 0, steps - 1)), 0)
        )

    param_spec = pl.BlockSpec((block * per, LANES), lambda k, i, me: ((me[0] ^ (k + first_k)) * steps + i, 0))
    size = len(ks) * rows * width
    return call(
        kernel,
        [jax.ShapeDtypeStruct(params[0].shape, jnp.float32)] * 3,
        20 * size,
        26 * size,
        grid_spec=pltpu.PrefetchScalarGridSpec(
            num_scalar_prefetch=1,
            grid=(len(ks), steps),
            in_specs=[full((8, LANES))]
            + [grad_spec(j) for j in range(len(grads))]
            + [param_spec] * 3
            + [pl.BlockSpec(memory_space=pl.ANY)] * len(before),
            out_specs=[param_spec] * 3,
            scratch_shapes=[pltpu.VMEM((block * per, LANES), jnp.float32)],
        ),
        input_output_aliases={2 + len(grads) + 3 + i: i for i in range(len(before))},
    )(me, count, *grads, *params, *before)


def combine(shares, pair, pairs, rows):
    features = shares[0][0].shape[1]
    tokens, per = rows // pairs, 2 * features // LANES
    each = len(shares[0])

    def kernel(pair, *refs):
        out, scratch = refs[-2], refs[-1]
        for o in range(pairs):
            start = (pair[0] ^ o) * tokens
            for slot, column in enumerate(slots(features)):
                half, at = divmod(column, features)
                total = sum(
                    source[o * tokens : (o + 1) * tokens, at : at + LANES].astype(jnp.float32)
                    for source in refs[half * each : (half + 1) * each]
                )
                scratch[pl.ds(start * per + slot, tokens, stride=per), :] = total
        out[...] = scratch[...].astype(out.dtype)

    out = call(
        kernel,
        jax.ShapeDtypeStruct((rows * per, LANES), jnp.bfloat16),
        0,
        16 * rows * features,
        grid=(1,),
        in_specs=[SMEM] + [full((rows, features))] * (2 * each),
        out_specs=full((rows * per, LANES)),
        scratch_shapes=[pltpu.VMEM((rows * per, LANES), jnp.float32)],
    )(pair, *shares[0], *shares[1])
    return from_lane_rows(out, rows, features)


def after(value, *deps):
    return lax.optimization_barrier((value, *deps))[0] if deps else value


def swap(value, axis, k):
    if k == 0:
        return value
    return lax.ppermute(value, axis, [(i, i ^ k) for i in range(lax.axis_size(axis))])


def add(a, b):
    return (a.astype(jnp.float32) + b.astype(jnp.float32)).astype(jnp.bfloat16)


class Line:
    ends_to_inner = [(0, 1), (3, 2)]
    across = [(1, 2), (2, 1)]
    inner_to_ends = [(1, 0), (2, 3)]

    away_first = True

    def __init__(self, shard):
        self.end = (shard == 0) | (shard == 3)
        low = shard < 2
        self.order = [jnp.where(low, 3, 0), jnp.where(low, 2, 1), shard ^ 1, shard]

    def send(self, away, soon):
        return add(away, after(lax.ppermute(away, "shard", self.ends_to_inner), *soon))

    def settle(self, far, last, soon):
        part = last.shape[0] // 2
        got = lax.ppermute(far, "shard", self.across)
        near = add(last[:part], after(got, *soon)[:part])
        return [(last, 1), (got, 1), (swap(near, "shard", 1), 0)], near

    def gather(self, own, *waits):
        side = after(jnp.concatenate([swap(own, "shard", 1), own], axis=0), *waits)
        got = lax.ppermute(side, "shard", self.across)
        far = lax.ppermute(got, "shard", self.inner_to_ends)
        return [jnp.where(self.end, far, got), side]


class Halves:
    away_first = False

    def __init__(self, shard, shards):
        order, k = [0], shards // 2
        while k:
            order, k = [i + k for i in order] + order, k // 2
        self.shards = shards
        self.order = [shard ^ q for q in order[shards // 2 :] + order[: shards // 2]]

    def send(self, away, soon):
        return after(swap(away, "shard", 1), *soon)

    def settle(self, far, last, soon):
        shares, half, k, sent = [last, far], last.shape[0], 2, far
        while k < self.shards:
            sent = sum(v[v.shape[0] - half : v.shape[0] - half // 2].astype(jnp.float32) for v in shares)
            sent, half, k = sent.astype(jnp.bfloat16), half // 2, 2 * k
            shares.append(swap(sent, "shard", k // 2))
        return [(v, v.shape[0] // half - 1) for v in shares], sent

    def gather(self, own, *waits):
        blocks, k = own, self.shards // 2
        while k > 1:
            blocks, k = jnp.concatenate([swap(blocks, "shard", k), blocks], axis=0), k // 2
        blocks = after(blocks, *waits)
        return [swap(blocks, "shard", 1), blocks]


def local(hidden_in, lengths, kv_grad_out, master, moment_one, moment_two):
    replicas, shards, pairs = (lax.axis_size(name) for name in ("rep", "shard", "tp"))
    rep, shard, pair = (lax.axis_index(name).astype(jnp.int32) for name in ("rep", "shard", "tp"))
    tokens, depth = hidden_in.shape
    block, _, features = kv_grad_out.shape
    width = 2 * features
    rows = depth // (shards * replicas)
    near = replicas // 2
    parities = [k for k in range(replicas) if k % 2] + [k for k in range(replicas) if not k % 2]
    odd = replicas // 2 * block

    number = max(1, min(GROUPS, rows // LANES))
    part = rows // number
    ways = [Line(shard) if shards == 4 and g < number - 1 else Halves(shard, shards) for g in range(number)]
    groups = [(g * part, part, way.order) for g, way in enumerate(ways)]
    each = max(1, number // LOADS)
    loads = [groups[g : g + each] for g in range(0, number, each)]
    by_rows = (((0,), (0,)), ((), ()))

    count, k = jnp.full((8, LANES), lengths[0]).astype(jnp.float32), near
    count = count + swap(count, "rep", k)
    early, k = count, k // 2
    while k:
        count, k = count + swap(count, "rep", k), k // 2
    k = 1
    while k < shards:
        count, k = count + swap(count, "shard", k), 2 * k
    pieces = pack(hidden_in, rep, loads[:1], replicas, rows)
    cotan, _ = mask(kv_grad_out, jnp.stack([lengths[0], pair]), pairs)
    if len(loads) > 1:
        pieces += pack(hidden_in, after(rep, count), loads[1:], replicas, rows)
    arrived, sides, line = [], [], []

    def travel(n, *waits):
        arrived.append(
            [pieces[n][0]]
            + [swap(after(h, *waits) if k >= near else h, "rep", k) for k, h in enumerate(pieces[n]) if k]
        )
        sides.append([])

    def pair_up(n, ks, *waits):
        for k in ks:
            sent = after(arrived[n][k], *line[-2:-1], *waits)
            sides[n].append([arrived[n][k]] + [swap(sent, "tp", o) for o in range(1, pairs)])
            line.append(sides[n][-1][-1])

    def lay(n):
        return jnp.concatenate([p for k in parities for p in sides[n][k]], axis=1)

    low, high = range(near), range(near, replicas)
    travel(0, early)
    pair_up(0, low)
    pair_up(0, high, cotan)
    ready = [*arrived[0][near:], *line[:near], *(pieces[1] if len(loads) > 1 else [])]
    cotans = {0: cotan, near: swap(after(cotan, *ready), "rep", near)}
    for n in range(1, len(loads)):
        travel(n, *([cotans[near]] if n == 1 else arrived[n - 1][near:]))
        if n == 1:
            pair_up(1, low)
    k = near // 2
    while k:
        for have in list(cotans):
            cotans[have ^ k] = swap(cotans[have], "rep", k)
        k //= 2
    cotans = jnp.concatenate([cotans[k] for k in parities], axis=0)

    params = [lane_rows(a) for a in (master, moment_one, moment_two)]
    steps, summed, grads, fresh, gathered, places, inputs, last = [], [], [], [], [], [], [], None

    def project(rows, weights):
        return lax.dot_general(rows, weights, by_rows, preferred_element_type=jnp.float32)

    half = shards // 2 * part
    for n, load in enumerate(loads):
        laid = lay(n)
        if n:
            laid = after(laid, fresh[(n - 1) * each], *steps)
        for inside in range(len(load)):
            g, way = n * each + inside, ways[n * each + inside]
            if last is not None:
                laid = after(laid, last)
            if n + 1 < len(loads) and inside == 1:
                laid = after(laid, line[(n + 1) * replicas])
            row = inside * 2 * half
            far_row, near_row = (row, row + half) if way.away_first else (row + half, row)
            places.append((far_row, near_row))
            away = jnp.dot(laid[far_row : far_row + half], cotans, preferred_element_type=jnp.float32)
            away = away.astype(jnp.bfloat16)
            laid = after(laid, away)
            last = jnp.dot(laid[near_row : near_row + half], cotans, preferred_element_type=jnp.float32)
            last = last.astype(jnp.bfloat16)
            soon, then = [], []
            if not n and inside:
                away = after(away, far)
            if n + 1 < len(loads) and inside:
                soon = arrived[n + 1][near:]
            if n and inside:
                soon = [summed[each - 1][-1][0]]
            far = way.send(away, soon)
            if n + 1 < len(loads):
                pair_up(n + 1, range(near + inside, near + inside + 1 if inside < each - 1 else replicas), far)
                then = line[-1:]
            shares, passed = way.settle(far, last, then)
            steps.append(passed)
            summed.append(shares)
        for inside in range(len(load)):
            g = n * each + inside
            shares = summed[g]
            if n and inside == 0:
                shares = [(after(shares[0][0], steps[-1], *fresh[each - 1 : each]), shares[0][1])] + shares[1:]
            if not n and inside:
                shares = [(after(shares[0][0], gathered[0][0]), shares[0][1])] + shares[1:]
            if n and inside:
                shares = [(after(shares[0][0], fresh[each - 1], steps[each]), shares[0][1])] + shares[1:]
            place = (rep * number + g)[None]
            specs = [
                (v, pl.BlockSpec((part, width), lambda i, place, row=row: (row, 0))) for v, row in shares
            ]
            weights, grad = fresh_weights(place, count, specs, params)
            fresh.append(weights)
            grads.append(grad)
            if n + 1 == len(loads) or inside == 0:
                gathered.append(ways[g].gather(weights, *(gathered[1][:1] if n and inside else [])))
            if n and inside == 0:
                gathered.insert(1, ways[1].gather(fresh[1], steps[2]))
        inputs.append(laid)

    every = {0: jnp.concatenate(grads, axis=0)}
    k = near
    while k:
        for have in list(every):
            every[have ^ k] = swap(every[have], "rep", k)
        k //= 2

    total = None
    if len(loads) > 1:
        total = project(inputs[0], jnp.concatenate([w for g in range(each) for w in gathered[g]], axis=0))
    held = range(number - each, number)
    begin = min(places[g][1] for g in held)
    assert all(places[g][1] == begin + i * half for i, g in enumerate(held))
    product = project(
        inputs[-1][begin : begin + each * half], jnp.concatenate([gathered[g][1] for g in held], axis=0)
    )
    total = product if total is None else total + product
    here = after(inputs[-1], every[near], total)
    sums, turn = [], here
    for side in (slice(0, features), slice(features, width)):
        here = after(here, turn)
        ends = []
        for columns in (slice(0, odd), slice(odd, 2 * odd)):
            end = total[columns, side]
            for g in held:
                row = places[g][0]
                end = end + project(here[row : row + half, columns], gathered[g][0][:, side])
            ends.append(end.astype(jnp.bfloat16))
            here = after(here, ends[0])
        away, stay = ends
        shares, turn = [stay, swap(away, "rep", 1)], stay
        size, k = odd // 2, 2
        while k < replicas:
            sent = sum(v[size : 2 * size].astype(jnp.float32) for v in shares).astype(jnp.bfloat16)
            shares.append(swap(sent, "rep", k))
            size, k = size // 2, 2 * k
        sums.append(shares)
    fresh = combine(sums, pair[None], pairs, block)

    everyone = [after(every[0], sent)] + [every[k] for k in range(1, replicas)]
    updated = update(rep[None], count, everyone, params, range(replicas), min(rows, 256), [])
    updated = [from_lane_rows(a, master.shape[0], features) for a in updated]
    return (*updated, fresh)


def solution(mesh):
    in_specs = (
        P(("rep", "shard", "tp"), None),
        P(("rep", "shard")),
        P(("rep", "shard"), None, "tp"),
        P("shard", None, "tp"),
        P("shard", None, "tp"),
        P("shard", None, "tp"),
    )
    out_specs = (
        P("shard", None, "tp"),
        P("shard", None, "tp"),
        P("shard", None, "tp"),
        P(("rep", "shard"), None, "tp"),
    )
    return jax.shard_map(local, mesh=mesh, in_specs=in_specs, out_specs=out_specs, check_vma=False)
```
